32 devices in a mesh: dp: 8 (over z, x), head: 4 (over y, core).
Axes of the slice: x: 2, y: 2, z: 4, core: 2. Of those that a mesh axis runs over, the one named last changes fastest.
Arguments:
- layer_input: bfloat16 [81920, 1024], P(('dp', 'head')), may hold values from -6 to 6
- cotangent: bfloat16 [81920, 1024], P(('dp', 'head')), may hold values from -6 to 6
- crop_blocks: int32 [8, 8], P('dp'), may hold values from 1 to 40, 80 in all within a row
- crop_padding: int32 [8, 8], P('dp'), may hold values from 0 to 127
- first_gain: float32 [1024], replicated, may hold values from 0.5 to 1.5
- first_shift: float32 [1024], replicated, may hold values from -1 to 1
- attend_weight: bfloat16 [1024, 3072], P(None, 'head'), may hold values from -0.1875 to 0.1875
- attend_bias: float32 [3072], P('head'), may hold values from -0.6 to 0.6
- output_weight: bfloat16 [1024, 1024], P('head'), may hold values from -1.5 to 1.5
- output_bias: float32 [1024], replicated, may hold values from -1 to 1
- second_gain: float32 [1024], replicated, may hold values from 0.5 to 1.5
- second_shift: float32 [1024], replicated, may hold values from -1 to 1
- expand_weight: bfloat16 [1024, 4096], P(None, 'head'), may hold values from -0.1875 to 0.1875
- expand_bias: float32 [4096], P('head'), may hold values from -1 to 1
- reduce_weight: bfloat16 [4096, 1024], P('head'), may hold values from -0.09375 to 0.09375
- reduce_bias: float32 [1024], replicated, may hold values from -1 to 1
Outputs:
- layer_output: bfloat16 [81920, 1024], P(('dp', 'head'))
- input_grad: float32 [81920, 1024], P(('dp', 'head'))
- first_gain_grad: float32 [1024], replicated
- first_shift_grad: float32 [1024], replicated
- attend_weight_grad: float32 [1024, 3072], P(None, 'head')
- attend_bias_grad: float32 [3072], P('head')
- output_weight_grad: float32 [1024, 1024], P('head')
- output_bias_grad: float32 [1024], replicated
- second_gain_grad: float32 [1024], replicated
- second_shift_grad: float32 [1024], replicated
- expand_weight_grad: float32 [1024, 4096], P(None, 'head')
- expand_bias_grad: float32 [4096], P('head')
- reduce_weight_grad: float32 [4096, 1024], P('head')
- reduce_bias_grad: float32 [1024], replicated
The draws below stay inside these ranges and needn't reach their ends.
Inputs may be any that keep to these rules, and one draw needn't show every extreme that they name: `crop_blocks`: each group's crop blocks sum to 80; the longest crop of every group has exactly 40 blocks.
All inputs are finite; a program needn't handle non-finite values.
Results may differ from the reference program's by a relative error of at most 0.02.
Values may be sent and summed in bfloat16 or wider, within the bound.
No kernel may reach another device: no remote copies, remote signals or barrier semaphores. Data moves between devices by JAX's collectives and lax.ppermute only.
A program may use at most 512 MiB of HBM per device.

```python
import math
import jax
import jax.numpy as jnp
import numpy as np
from jax import lax

D = 1024
H = 16
DH = 64
FF = 4096
STRETCH = 128
CROPS = 8
ROWS = 10240
GROUPS = 8
TOKENS = 81920
STRETCHES = 80
MOST = 40


def plant(entries, stream_key, least, top_value):
    spot = [jax.random.randint(jax.random.fold_in(stream_key, axis), (), 0, length) for axis, length in enumerate(entries.shape)]
    widest = entries.shape.index(max(entries.shape))
    next_to = spot[:widest] + [(spot[widest] + 1) % entries.shape[widest]] + spot[widest + 1:]
    return entries.at[tuple(spot)].set(least).at[tuple(next_to)].set(top_value)


def levels(key, extent, cuts, smallest, high):
    loudness, own = 1.0, jax.random.fold_in(key, 6)
    for axis_at, parts in cuts:
        steps = jnp.exp(jax.random.uniform(jax.random.fold_in(own, axis_at), (parts,), jnp.float32, smallest / len(cuts), high / len(cuts)))
        loudness = loudness * jnp.repeat(steps, extent[axis_at] // parts).reshape([-1 if axis == axis_at else 1 for axis in range(len(extent))])
    return loudness


def profile(count, total, limit, lean):
    weights = [(1 << 20) // math.isqrt(standing ** lean) + 1 for standing in range(2, count + 1)]
    spare, counts = total - limit - (count - 1), [1] * (count - 1)
    while spare > 0:
        movable = [i for i in range(count - 1) if counts[i] < limit]
        whole, remaining = sum([weights[i] for i in movable]), spare
        for i in movable:
            addition = min(limit - counts[i], max(1, remaining * weights[i] // whole), spare)
            counts[i] = counts[i] + addition
            spare = spare - addition
    return np.array([limit] + counts)


def uneven(stream_key, number_of, total, most, slope):
    if number_of == 2:
        one = jax.random.randint(stream_key, (), max(1, total - most), min(most, total - 1) + 1)
        return jnp.stack([one, total - one])
    tallies = jnp.asarray(profile(number_of, total, most, slope), jnp.int32)
    pairs = (number_of - 1) // 2
    donor, receiver = tallies[1:1 + 2 * pairs:2], tallies[2:2 + 2 * pairs:2]
    room = jnp.minimum(donor - 1, most - receiver)
    moved = jax.random.randint(jax.random.fold_in(stream_key, 1), (pairs,), 0, 1 << 20) % (room + 1)
    tallies = tallies.at[1:1 + 2 * pairs:2].set(donor - moved).at[2:2 + 2 * pairs:2].set(receiver + moved)
    return tallies[jax.random.permutation(jax.random.fold_in(stream_key, 2), number_of)]


def scatter_about(key, dims, scale, most, shards=(), kind=jnp.bfloat16):
    entries = jax.random.normal(key, dims, jnp.float32) * scale
    if len(shards) > 0:
        entries = levels(key, dims, shards, -0.22, 0.18) * entries
    return jnp.clip(entries, min=-most, max=most).astype(kind)


def setup_inputs(seed: int = 0) -> dict:
    key_list = jax.random.split(jax.random.key(seed), 17)
    layer_input = scatter_about(key_list[0], (TOKENS, D), 1.0, 6.0, ((0, 32),))
    cotangent = scatter_about(key_list[1], (TOKENS, D), 1.0, 6.0, ((0, 32),))
    crop_blocks = jax.vmap(lambda own: uneven(own, CROPS, STRETCHES, MOST, 2))(jax.random.split(key_list[2], GROUPS)).reshape((GROUPS, CROPS)).astype(jnp.int32)
    crop_padding = plant(jax.random.randint(key_list[3], (GROUPS, CROPS), 0, STRETCH), jax.random.fold_in(key_list[3], 1), 0, STRETCH - 1).astype(jnp.int32)
    first_gain = jnp.clip(1.0 + 0.1 * jax.random.normal(key_list[4], (D,), jnp.float32), 0.5, 1.5)
    first_shift = scatter_about(key_list[5], (D,), 0.2, 1.0, (), jnp.float32)
    attend_weight = scatter_about(key_list[6], (D, 3 * D), D ** -0.5, 0.1875, ((1, 4),))
    attend_bias = scatter_about(key_list[7], (3 * D,), 0.1, 0.6, ((0, 4),), jnp.float32)
    output_weight = scatter_about(key_list[8], (D, D), 16 ** -0.5, 1.5, ((0, 4),))
    output_bias = scatter_about(key_list[9], (D,), 0.2, 1.0, (), jnp.float32)
    second_gain = jnp.clip(1.0 + 0.1 * jax.random.normal(key_list[10], (D,), jnp.float32), 0.5, 1.5)
    second_shift = scatter_about(key_list[11], (D,), 0.2, 1.0, (), jnp.float32)
    expand_weight = scatter_about(key_list[12], (D, FF), D ** -0.5, 0.1875, ((1, 4),))
    expand_bias = scatter_about(key_list[13], (FF,), 0.2, 1.0, ((0, 4),), jnp.float32)
    reduce_weight = scatter_about(key_list[14], (FF, D), FF ** -0.5, 0.09375, ((0, 4),))
    reduce_bias = scatter_about(key_list[15], (D,), 0.2, 1.0, (), jnp.float32)
    return {"layer_input": layer_input, "cotangent": cotangent, "crop_blocks": crop_blocks, "crop_padding": crop_padding, "first_gain": first_gain, "first_shift": first_shift, "attend_weight": attend_weight, "attend_bias": attend_bias, "output_weight": output_weight, "output_bias": output_bias, "second_gain": second_gain, "second_shift": second_shift, "expand_weight": expand_weight, "expand_bias": expand_bias, "reduce_weight": reduce_weight, "reduce_bias": reduce_bias}


@jax.custom_vjp
def low(v):
    return lax.optimization_barrier(v.astype(jnp.bfloat16)).astype(jnp.float32)

@jax.custom_vjp
def low_back(v):
    return v

def low_keep(v):
    return (low(v), None)

def low_pass(kept, grad):
    return (grad,)

def back_keep(v):
    return (v, None)

def back_low(kept, grad):
    return (low(grad),)
low.defvjp(low_keep, low_pass)
low_back.defvjp(back_keep, back_low)
epsilon = 1e-05
highest = lax.Precision.HIGHEST

def crop_layout(block_sizes, pad_sizes, block_total, stretch_rows):
    closing = jnp.cumsum(block_sizes).astype(jnp.int32)
    opening = (closing - block_sizes).astype(jnp.int32)
    position = jnp.arange(block_total, dtype=jnp.int32)
    member = jnp.logical_and(position[:, None] >= opening[None, :], position[:, None] < closing[None, :]).astype(jnp.int32)
    first_block = lax.optimization_barrier(jnp.sum(member * opening[None, :], axis=1))
    padding = lax.optimization_barrier(jnp.sum(member * pad_sizes[None, :], axis=1))
    within = (position[:, None] - first_block[:, None]) * stretch_rows + jnp.arange(stretch_rows, dtype=jnp.int32)[None, :]
    validity = (within >= padding[:, None]).astype(jnp.float32).reshape(block_total * stretch_rows)
    crop_number = lax.optimization_barrier(jnp.sum(member * jnp.arange(member.shape[1], dtype=jnp.int32)[None, :], axis=1))
    same_crop = (crop_number[:, None] == crop_number[None, :]).astype(jnp.float32)
    earlier = same_crop * (position[None, :] < position[:, None]).astype(jnp.float32)
    return (validity, earlier)

def layer_norm(values, gain, shift):
    average = lax.optimization_barrier(jnp.mean(values, axis=-1, keepdims=True))
    centred = values - average
    spread = lax.optimization_barrier(jnp.mean(centred * centred, axis=-1, keepdims=True))
    return centred * lax.rsqrt(spread + epsilon) * gain + shift

def feature(values):
    return jax.nn.elu(values) + 1.0

def forward(inputs, weights, validity, earlier):
    first_gain, first_shift, attend_weight, attend_bias, output_weight, output_bias, second_gain, second_shift, expand_weight, expand_bias, reduce_weight, reduce_bias = weights
    row_total = inputs.shape[0]
    block_total = row_total // STRETCH
    normed = low(layer_norm(inputs, first_gain, first_shift))
    project = low_back(jnp.dot(normed, attend_weight, precision=highest) + attend_bias)
    shaped = project.reshape(block_total, STRETCH, H, 3, DH)
    keep = validity.reshape(block_total, STRETCH, 1, 1)
    query_map = low(feature(shaped[:, :, :, 0]))
    key_map = low(keep * feature(shaped[:, :, :, 1]))
    value_rows = low(shaped[:, :, :, 2])
    lower = jnp.tril(jnp.ones((STRETCH, STRETCH), jnp.float32))
    scores = low_back(jnp.einsum('cihd,cjhd->chij', query_map, key_map, precision=highest) * lower)
    products = low_back(jnp.einsum('cjhd,cjhe->chde', key_map, value_rows, precision=highest))
    states = jnp.einsum('ab,bhde->ahde', earlier, products, precision=highest)
    key_totals = jnp.einsum('ab,bjhd->ahd', earlier, key_map, precision=highest)
    numerator = low_back(jnp.einsum('chij,cjhe->cihe', low(scores), value_rows, precision=highest) + jnp.einsum('cihd,chde->cihe', query_map, low(states), precision=highest))
    denominator = lax.optimization_barrier(jnp.sum(scores, axis=3)).transpose(0, 2, 1) + jnp.einsum('cihd,chd->cih', query_map, key_totals, precision=highest)
    attended = keep * numerator / jnp.maximum(denominator, 1.0)[..., None]
    attended = low(low_back(attended)).reshape(row_total, D)
    branch = low_back(jnp.dot(attended, output_weight, precision=highest) + output_bias)
    middle = inputs + branch
    normed_two = low(layer_norm(middle, second_gain, second_shift))
    hidden = low_back(jnp.dot(normed_two, expand_weight, precision=highest) + expand_bias)
    activated = low(jax.nn.gelu(hidden, approximate=False))
    return middle + jnp.dot(activated, reduce_weight, precision=highest) + reduce_bias

def reference(layer_input, cotangent, crop_blocks, crop_padding, first_gain, first_shift, attend_weight, attend_bias, output_weight, output_bias, second_gain, second_shift, expand_weight, expand_bias, reduce_weight, reduce_bias):
    weights = tuple((value.astype(jnp.float32) for value in (first_gain, first_shift, attend_weight, attend_bias, output_weight, output_bias, second_gain, second_shift, expand_weight, expand_bias, reduce_weight, reduce_bias)))
    inputs = layer_input.astype(jnp.float32).reshape(GROUPS, ROWS, D)
    cotangents = cotangent.astype(jnp.float32).reshape(GROUPS, ROWS, D)

    def group(totals, item):
        rows_in, rows_cot, sizes_row, pads_row = item
        validity, earlier = crop_layout(sizes_row, pads_row, STRETCHES, STRETCH)

        def apply(values, *params):
            return forward(values, params, validity, earlier)
        result, pull = jax.vjp(apply, rows_in, *weights)
        gradients = pull(rows_cot)
        totals = tuple((left + right for left, right in zip(totals, gradients[1:])))
        return (totals, (result.astype(jnp.bfloat16), gradients[0]))
    initial = tuple((jnp.zeros_like(value) for value in weights))
    totals, (outputs, input_grads) = lax.scan(group, initial, (inputs, cotangents, crop_blocks, crop_padding))
    return (outputs.reshape(TOKENS, D), input_grads.reshape(TOKENS, D), totals[0], totals[1], totals[2], totals[3], totals[4], totals[5], totals[6], totals[7], totals[8], totals[9], totals[10], totals[11])
```

```python
import functools

import jax
import jax.numpy as jnp
from jax import lax
from jax.experimental import pallas as pl
from jax.experimental.pallas import tpu as pltpu
from jax.sharding import PartitionSpec as P

DH = 64
STRETCH = 128
D = 1024
QUADS = 4
QW = D // QUADS
PW = 3 * QW
EPS = 1e-05
VMEM = 60 * 1024 * 1024

f32 = jnp.float32
bf16 = jnp.bfloat16


def nn(a, b):
    return lax.dot_general(a, b, (((1,), (0,)), ((), ())), preferred_element_type=f32)


def nt(a, b):
    return lax.dot_general(a, b, (((1,), (1,)), ((), ())), preferred_element_type=f32)


def tn(a, b):
    return lax.dot_general(a, b, (((0,), (0,)), ((), ())), preferred_element_type=f32)


def params():
    return pltpu.CompilerParams(vmem_limit_bytes=VMEM)


def cost(flops, bytes_accessed):
    return pl.CostEstimate(flops=flops, bytes_accessed=bytes_accessed, transcendentals=0)


def head_rows():
    lane = lax.broadcasted_iota(jnp.int32, (1, QW), 1) // DH
    return [(lane == h).astype(f32) for h in range(4)]


def spread_heads(block, picks):
    return jnp.concatenate([block * pick for pick in picks], axis=0)


def spread_state(state, picks):
    return jnp.concatenate([state * pick for pick in picks], axis=0)


def gather_state(square, picks):
    total = square[0:DH] * picks[0]
    for h in range(1, 4):
        total = total + square[h * DH : (h + 1) * DH] * picks[h]
    return total


def centre(values):
    average = jnp.mean(values, axis=-1, keepdims=True)
    centred = values - average
    spread = jnp.mean(centred * centred, axis=-1, keepdims=True)
    inverse = lax.rsqrt(spread + EPS)
    return centred * inverse, inverse


def norm_back(xhat, inverse, grad, gain):
    w = grad * gain
    return inverse * (
        w
        - jnp.mean(w, axis=-1, keepdims=True)
        - xhat * jnp.mean(w * xhat, axis=-1, keepdims=True)
    )


def fold_rows(values):
    rows, columns = values.shape
    return jnp.sum(values.reshape(rows // 8, 8, columns), axis=0)


def normal_parts(v):
    size = jnp.abs(v) * 0.7071067811865476
    t = 1.0 / (1.0 + 0.3275911 * size)
    bell = jnp.exp(-0.5 * v * v)
    poly = t * (
        0.254829592
        + t * (-0.284496736 + t * (1.421413741 + t * (-1.453152027 + t * 1.061405429)))
    )
    tail = 0.5 * poly * bell
    return jnp.where(v < 0, tail, 1.0 - tail), bell


def qkv_kernel(blocks, thr, last, x, gain, shift, *refs):
    wa, ba = refs[0:4], refs[4]
    q_out, k_out, v_out, n_out, t_out = refs[5:10]
    step = pl.program_id(0)
    rows = blocks * STRETCH

    @pl.when(step == 0)
    def _():
        t_out[...] = jnp.zeros_like(t_out)

    xhat, _ = centre(x[...].astype(f32))
    normed = (xhat * gain[...] + shift[...]).astype(bf16)
    n_out[...] = normed
    place = lax.broadcasted_iota(jnp.int32, (STRETCH, 128), 0)
    valid = jnp.concatenate(
        [(place >= thr[step * blocks + b]).astype(f32) for b in range(blocks)], axis=0
    )
    low = lax.broadcasted_iota(jnp.int32, (rows, 128), 1) < DH

    def feature(values):
        return jnp.where(values > 0, values + 1.0, jnp.exp(jnp.minimum(values, 0.0)))

    for g in range(QUADS):
        project = nn(normed, wa[g][...]) + ba[:, g * PW : (g + 1) * PW]
        for pair in range(2):
            c0, c1, c2 = (
                project[:, pair * 384 + j * 128 : pair * 384 + (j + 1) * 128] for j in range(3)
            )
            at = slice(g * QW + pair * 128, g * QW + (pair + 1) * 128)
            q_out[:, at] = feature(jnp.where(low, c0, c1)).astype(bf16)
            key = pltpu.roll(jnp.where(low, c2, c0), DH, 1)
            k_out[:, at] = (valid * feature(key)).astype(bf16)
            v_out[:, at] = jnp.where(low, c1, c2).astype(bf16)
    picks = head_rows()
    for b in range(blocks):

        @pl.when(last[step * blocks + b] == 1)
        def _(b=b):
            here = slice(b * STRETCH, (b + 1) * STRETCH)
            for g in range(QUADS):
                at = slice(g * QW, (g + 1) * QW)
                key = k_out[here, at]
                t_out[0:DH, at] += gather_state(tn(key, v_out[here, at]), picks)
                t_out[DH : DH + 8, at] += fold_rows(key.astype(f32))


def attend_kernel(blocks, cont, q, k, v, x, s_in, ones, bo, gain, shift, *refs):
    wo = refs[0:4]
    att_out, rec_out, st_out, kt_out, mid_out, n_out = refs[4:10]
    state, total = refs[10:12]
    step = pl.program_id(0)

    @pl.when(step == 0)
    def _():
        state[...] = s_in[0:DH]
        total[...] = jnp.broadcast_to(
            jnp.sum(s_in[DH : DH + 8], axis=0, keepdims=True), total.shape
        )

    picks = head_rows()
    low_picks = [p.astype(bf16) for p in picks]
    row = lax.broadcasted_iota(jnp.int32, (STRETCH, 512), 0)
    lane = lax.broadcasted_iota(jnp.int32, (STRETCH, 512), 1) % STRETCH
    lower = lane <= row
    for b in range(blocks):
        keep = cont[step * blocks + b].astype(f32)
        here = slice(b * STRETCH, (b + 1) * STRETCH)
        state[...] = state[...] * keep
        total[...] = total[...] * keep
        low_state = state[...].astype(bf16)
        st_out[b * DH : (b + 1) * DH, :] = low_state
        kt_out[b * 8 : (b + 1) * 8, :] = total[...]
        for g in range(QUADS):
            at = slice(g * QW, (g + 1) * QW)
            qb, kb, vb = q[here, at], k[here, at], v[here, at]
            scores = nt(qb, spread_heads(kb, low_picks))
            scores = jnp.where(lower, scores, 0.0).astype(bf16)
            numer = nn(scores, spread_heads(vb, low_picks)) + nn(
                qb, spread_state(low_state[:, at], low_picks)
            )
            weighted = (qb.astype(f32) * total[0:1, at]).astype(bf16)
            denom = nn(scores, ones[0:512]) + nn(weighted, ones[512:768])
            rec = 1.0 / jnp.maximum(denom, 1.0)
            rec_out[here, at] = rec
            att_out[here, at] = (numer * rec).astype(bf16)
            state[:, at] += gather_state(tn(kb, vb), picks)
            total[:, at] += jnp.sum(kb.astype(f32), axis=0, keepdims=True)
    return picks


def attend_tile(blocks, cont, thr, *refs):
    q, k, v, x, s_in, ones, bo, gain, shift = refs[0:9]
    wo = refs[9:13]
    att_out, rec_out, st_out, kt_out, mid_out, n_out = refs[13:19]
    attend_kernel(blocks, cont, q, k, v, x, s_in, ones, bo, gain, shift, *refs[9:])
    step = pl.program_id(0)
    place = lax.broadcasted_iota(jnp.int32, (STRETCH, D), 0)
    for b in range(blocks):
        here = slice(b * STRETCH, (b + 1) * STRETCH)

        @pl.when(thr[step * blocks + b] > 0)
        def _(b=b, here=here):
            valid = (place >= thr[step * blocks + b]).astype(f32)
            rec = rec_out[here, :] * valid
            rec_out[here, :] = rec
            att_out[here, :] = (att_out[here, :].astype(f32) * valid).astype(bf16)

    middle = x[...].astype(f32) + bo[...]
    for g in range(QUADS):
        middle = middle + nn(att_out[:, g * QW : (g + 1) * QW], wo[g][...])
    mid_out[...] = middle
    xhat, _ = centre(middle)
    n_out[...] = (xhat * gain[...] + shift[...]).astype(bf16)


def ffn_kernel(blocks, first, n2, cot, mid, att, rec, q, gain, be, br, ones, *refs):
    we, wr, wo = refs[0:4], refs[4:8], refs[8:12]
    act, gh = refs[12:16], refs[16:20]
    out, gm_out, gb_out, gn_out, t_out, l_out, sums, be_sum = refs[20:28]
    step = pl.program_id(0)

    @pl.when(step == 0)
    def _():
        l_out[...] = jnp.zeros_like(l_out)
        sums[...] = jnp.zeros_like(sums)
        be_sum[...] = jnp.zeros_like(be_sum)

    normed = n2[...]
    cotangent = cot[...]
    reduced = None
    grad = None
    for g in range(QUADS):
        at = slice(g * D, (g + 1) * D)
        hidden = nn(normed, we[g][...]) + be[:, at]
        grad_act = nt(cotangent, wr[g][...])
        phi, bell = normal_parts(hidden)
        active = (hidden * phi).astype(bf16)
        back = (grad_act * (phi + hidden * (0.3989422804014327 * bell))).astype(bf16)
        act[g][...] = active
        gh[g][...] = back
        be_sum[:, at] += fold_rows(back.astype(f32))
        part = nn(active, wr[g][...])
        reduced = part if reduced is None else reduced + part
        part = nt(back, we[g][...])
        grad = part if grad is None else grad + part
    middle = mid[...]
    out[...] = (middle + reduced + br[...]).astype(bf16)
    xhat, inverse = centre(middle)
    cot_wide = cotangent.astype(f32)
    grad_middle = cot_wide + norm_back(xhat, inverse, grad, gain[...])
    gm_out[...] = grad_middle
    branch = grad_middle.astype(bf16)
    gb_out[...] = branch
    sums[0:8, :] += fold_rows(branch.astype(f32))
    sums[8:16, :] += fold_rows(grad * xhat)
    sums[16:24, :] += fold_rows(grad)
    sums[24:32, :] += fold_rows(cot_wide)
    for g in range(QUADS):
        at = slice(g * QW, (g + 1) * QW)
        grad_att = nt(branch, wo[g][...]).astype(bf16).astype(f32)
        share = rec[:, at]
        numer = grad_att * share
        gn_out[:, at] = numer.astype(bf16)
        t_out[:, at] = jnp.where(
            share < 1.0, -(numer * att[:, at].astype(f32)), 0.0
        ).astype(bf16)
    picks = head_rows()
    for b in range(blocks):

        @pl.when(first[step * blocks + b] == 1)
        def _(b=b):
            here = slice(b * STRETCH, (b + 1) * STRETCH)
            for g in range(QUADS):
                at = slice(g * QW, (g + 1) * QW)
                query = q[here, at]
                l_out[0:DH, at] += gather_state(tn(query, gn_out[here, at]), picks)
                grad_denom = nn(t_out[here, at], ones[512:768])
                l_out[DH : DH + 8, at] += fold_rows(grad_denom * query.astype(f32))


def back_kernel(blocks, tiles, cont, q, k, v, gn, t, st, kt, g_in, ones, *refs):
    gp_out, ba_sum = refs[0:4], refs[4]
    state, total = refs[5:7]
    step = pl.program_id(0)
    tile = tiles - 1 - step

    @pl.when(step == 0)
    def _():
        state[...] = g_in[0:DH]
        total[...] = jnp.broadcast_to(
            jnp.sum(g_in[DH : DH + 8], axis=0, keepdims=True), total.shape
        )
        ba_sum[...] = jnp.zeros_like(ba_sum)

    picks = head_rows()
    low_picks = [p.astype(bf16) for p in picks]
    row = lax.broadcasted_iota(jnp.int32, (STRETCH, 512), 0)
    lane = lax.broadcasted_iota(jnp.int32, (STRETCH, 512), 1) % STRETCH
    lower = lane <= row
    upper = lane >= row
    low_lane = lax.broadcasted_iota(jnp.int32, (STRETCH, 128), 1) < DH
    all_ones = jnp.ones((STRETCH, QW), bf16)
    for b in reversed(range(blocks)):
        keep = cont[tile * blocks + b + 1].astype(f32)
        here = slice(b * STRETCH, (b + 1) * STRETCH)
        state[...] = state[...] * keep
        total[...] = total[...] * keep
        low_state = state[...].astype(bf16)
        for g in range(QUADS):
            at = slice(g * QW, (g + 1) * QW)
            qb, kb, vb, gb, tb = q[here, at], k[here, at], v[here, at], gn[here, at], t[here, at]
            q_wide = qb.astype(f32)
            spread_q = spread_heads(qb, low_picks)
            spread_g = spread_heads(gb, low_picks)
            forward = spread_state(st[b * DH : (b + 1) * DH, at], low_picks)
            behind = spread_state(low_state[:, at], low_picks)
            scores = nt(gb, spread_heads(vb, low_picks)) + nt(tb, ones[0:512])
            scores = jnp.where(lower, scores, 0.0).astype(bf16)
            turned = nt(vb, spread_g) + nt(all_ones, spread_heads(tb, low_picks))
            turned = jnp.where(upper, turned, 0.0).astype(bf16)
            mixed = jnp.where(upper, nt(kb, spread_q), 0.0).astype(bf16)
            grad_denom = nn(tb, ones[512:768])
            grad_q = (
                nn(scores, spread_heads(kb, low_picks))
                + nt(gb, forward)
                + grad_denom * kt[b * 8 : b * 8 + 1, at]
            )
            grad_k = nn(turned, spread_q) + nt(vb, behind) + total[0:1, at]
            grad_v = nn(mixed, spread_g) + nn(kb, behind)
            grad_q = grad_q * jnp.minimum(q_wide, 1.0)
            grad_k = grad_k * jnp.minimum(kb.astype(f32), 1.0)
            for pair in range(2):
                two = slice(pair * 128, (pair + 1) * 128)
                swapped = pltpu.roll(grad_k[:, two], DH, 1)
                for j, piece in enumerate(
                    (
                        jnp.where(low_lane, grad_q[:, two], swapped),
                        jnp.where(low_lane, grad_v[:, two], grad_q[:, two]),
                        jnp.where(low_lane, swapped, grad_v[:, two]),
                    )
                ):
                    piece = piece.astype(bf16)
                    start = pair * 384 + j * 128
                    gp_out[g][here, start : start + 128] = piece
                    ba_sum[:, g * PW + start : g * PW + start + 128] += fold_rows(
                        piece.astype(f32)
                    )
            state[:, at] += gather_state(tn(qb, gb), picks)
            total[:, at] += jnp.sum(grad_denom * q_wide, axis=0, keepdims=True)


def input_kernel(x, gm, gain, *refs):
    gp, wa = refs[0:4], refs[4:8]
    out, sums = refs[8:10]

    @pl.when(pl.program_id(0) == 0)
    def _():
        sums[...] = jnp.zeros_like(sums)

    grad = nt(gp[0][...], wa[0][...])
    for g in range(1, QUADS):
        grad = grad + nt(gp[g][...], wa[g][...])
    xhat, inverse = centre(x[...].astype(f32))
    out[...] = gm[...] + norm_back(xhat, inverse, grad, gain[...])
    sums[0:8, :] += fold_rows(grad * xhat)
    sums[8:16, :] += fold_rows(grad)


def rows_spec(rows, columns):
    return pl.BlockSpec((rows, columns), lambda i, *_: (i, 0))


def back_spec(rows, columns, tiles):
    return pl.BlockSpec((rows, columns), lambda i, *_: (tiles - 1 - i, 0))


def whole_spec(shape):
    return pl.BlockSpec(shape, lambda i, *_: (0,) * len(shape), pipeline_mode=pl.Buffered(1))


def sum_spec(shape):
    return pl.BlockSpec(shape, lambda i, *_: (0,) * len(shape))


def grid_spec(scalars, tiles, in_specs, out_specs, scratch=()):
    return pltpu.PrefetchScalarGridSpec(
        num_scalar_prefetch=scalars,
        grid=(tiles,),
        in_specs=in_specs,
        out_specs=out_specs,
        scratch_shapes=list(scratch),
    )


def swap(value, axis, bit):
    size = lax.axis_size(axis)
    return lax.ppermute(value, axis, [(i, i ^ bit) for i in range(size)])


def bits_of(size):
    bit, bits = 1, []
    while bit < size:
        bits.append(bit)
        bit *= 2
    return bits


def gather_shards(own):
    size = lax.axis_size("head")
    held = {0: own}
    for bit in reversed(bits_of(size)):
        for k in list(held):
            held[k ^ bit] = swap(held[k], "head", bit)
    return [held[k] for k in range(size)]


def regroup(parts, count, axis):
    if len(parts) == count:
        return parts
    whole = jnp.concatenate(parts, axis=axis)
    width = whole.shape[axis] // count
    return [
        lax.slice_in_dim(whole, k * width, (k + 1) * width, axis=axis) for k in range(count)
    ]


def swap_state(mine, weights):
    size = lax.axis_size("head")
    sent = mine.astype(bf16)
    total = None
    for j in range(1, size):
        got = swap(sent, "head", j)
        slots = jnp.split(got, size, axis=1)
        got = jnp.concatenate([slots[k ^ j] for k in range(size)], axis=1).astype(f32)
        got = got * weights[j]
        total = got if total is None else total + got
    return total


def scatter_head(parts):
    held = dict(enumerate(parts))
    for bit in bits_of(len(parts)):
        for k in [k for k in held if k & bit]:
            got = swap(held.pop(k).astype(bf16), "head", bit)
            held[k ^ bit] = held[k ^ bit].astype(f32) + got.astype(f32)
    return held[0]


def sum_groups(value):
    size = lax.axis_size("dp")
    me = lax.axis_index("dp")
    bits = bits_of(size)
    value = value.astype(bf16)
    for bit in bits:
        half = value.shape[0] // 2
        mine = jnp.where((me & bit) != 0, 1, 0)
        sent = lax.dynamic_slice_in_dim(value, (1 - mine) * half, half, 0)
        kept = lax.dynamic_slice_in_dim(value, mine * half, half, 0)
        got = swap(sent, "dp", bit)
        value = (kept.astype(f32) + got.astype(f32)).astype(bf16)
    for bit in reversed(bits):
        got = swap(value, "dp", bit)
        upper = (me & bit) != 0
        value = jnp.concatenate(
            [jnp.where(upper, got, value), jnp.where(upper, value, got)], axis=0
        )
    return value.astype(f32)


def sum_small(shared, split):
    size = len(split)
    held = dict(enumerate(split))
    flat = shared.reshape(-1)
    for bit in bits_of(size):
        gone = [k for k in held if k & bit]
        sent = jnp.concatenate([flat] + [held[k] for k in gone])
        got = swap(sent, "head", bit)
        flat = flat + got[: flat.shape[0]]
        at = flat.shape[0]
        for k in gone:
            width = held[k].shape[0]
            held[k ^ bit] = held[k ^ bit] + got[at : at + width]
            del held[k]
            at += width
    both = jnp.concatenate([flat, held[0]])
    for bit in bits_of(lax.axis_size("dp")):
        both = both + swap(both, "dp", bit)
    return both[: flat.shape[0]].reshape(shared.shape), both[flat.shape[0] :]


def on_device(
    layer_input,
    cotangent,
    crop_blocks,
    crop_padding,
    first_gain,
    first_shift,
    attend_weight,
    attend_bias,
    output_weight,
    output_bias,
    second_gain,
    second_shift,
    expand_weight,
    expand_bias,
    reduce_weight,
    reduce_bias,
):
    R = layer_input.shape[0]
    n = lax.axis_size("head")
    me = lax.axis_index("head")
    nb = R // STRETCH
    FF = expand_weight.shape[1] * n

    wa_all = gather_shards(attend_weight)
    ba_all = gather_shards(attend_bias)
    wo_all = gather_shards(output_weight)
    we_all = gather_shards(expand_weight)
    wr_all = gather_shards(reduce_weight)
    be_all = gather_shards(expand_bias)
    wa = regroup(wa_all, QUADS, 1)
    wo = regroup(wo_all, QUADS, 0)
    we = regroup(we_all, QUADS, 1)
    wr = regroup(wr_all, QUADS, 0)
    ba = jnp.concatenate(ba_all)[None, :]
    be = jnp.concatenate(be_all)[None, :]

    sizes, pads = crop_blocks[0], crop_padding[0]
    crops = sizes.shape[0]
    closing = jnp.sum(jnp.tril(jnp.ones((crops, crops), jnp.int32)) * sizes[None, :], axis=1)

    def crop_of(position):
        return jnp.sum((position[..., None] >= closing).astype(jnp.int32), axis=-1)

    spots = me * nb + jnp.arange(nb, dtype=jnp.int32)
    crop = crop_of(spots)
    belongs = crop[:, None] == jnp.arange(crops, dtype=jnp.int32)[None, :]
    opening = jnp.sum(jnp.where(belongs, (closing - sizes)[None, :], 0), axis=1)
    padding = jnp.sum(jnp.where(belongs, pads[None, :], 0), axis=1)
    thr = jnp.maximum(padding - (spots - opening) * STRETCH, 0).astype(jnp.int32)
    first = (crop == crop[0]).astype(jnp.int32)
    last = (crop == crop[nb - 1]).astype(jnp.int32)
    one = jnp.ones((1,), jnp.int32)
    cont = jnp.concatenate([one, (crop[1:] == crop[:-1]).astype(jnp.int32), one])
    others = me ^ jnp.arange(n, dtype=jnp.int32)
    opens = crop_of(others * nb)
    closes = crop_of(others * nb + nb - 1)
    before = jnp.logical_and(others < me, closes == crop[0]).astype(f32)
    after = jnp.logical_and(others > me, opens == crop[nb - 1]).astype(f32)

    line = lax.broadcasted_iota(jnp.int32, (768, QW), 0)
    lane_head = lax.broadcasted_iota(jnp.int32, (768, QW), 1) // DH
    ones = (jnp.where(line < 512, line // STRETCH, (line - 512) // DH) == lane_head).astype(bf16)

    blocks = 2 if nb % 2 == 0 else 1
    rows = blocks * STRETCH
    tiles = R // rows
    vec = whole_spec((1, D))
    gain1, shift1 = first_gain[None, :], first_shift[None, :]
    gain2, shift2 = second_gain[None, :], second_shift[None, :]
    like = jax.ShapeDtypeStruct
    low = like((R, D), bf16)
    wide = like((R, D), f32)
    state_shape = (DH + 8, D)

    q, k, v, normed, trailing = pl.pallas_call(
        functools.partial(qkv_kernel, blocks),
        grid_spec=grid_spec(
            2,
            tiles,
            [rows_spec(rows, D), vec, vec]
            + [whole_spec((D, PW))] * 4
            + [whole_spec((1, 3 * D))],
            [rows_spec(rows, D)] * 4 + [sum_spec(state_shape)],
        ),
        out_shape=[low] * 4 + [like(state_shape, f32)],
        compiler_params=params(),
        cost_estimate=cost(2 * R * D * 3 * D, 10 * R * D + 6 * D * D),
        name="qkv",
    )(thr, last, layer_input, gain1, shift1, *wa, ba)

    s_in = swap_state(trailing, before)

    att, rec, st, kt, middle, n2 = pl.pallas_call(
        functools.partial(attend_tile, blocks),
        grid_spec=grid_spec(
            2,
            tiles,
            [rows_spec(rows, D)] * 4
            + [whole_spec(state_shape), whole_spec((768, QW)), vec, vec, vec]
            + [whole_spec((QW, D))] * 4,
            [
                rows_spec(rows, D),
                rows_spec(rows, D),
                rows_spec(blocks * DH, D),
                rows_spec(blocks * 8, D),
                rows_spec(rows, D),
                rows_spec(rows, D),
            ],
            [pltpu.VMEM((DH, D), f32), pltpu.VMEM((8, D), f32)],
        ),
        out_shape=[low, wide, like((nb * DH, D), bf16), like((nb * 8, D), f32), wide, low],
        compiler_params=params(),
        cost_estimate=cost(6 * R * D * D, 20 * R * D),
        name="attend",
    )(cont, thr, q, k, v, layer_input, s_in, ones, output_bias[None, :], gain2, shift2, *wo)

    results = pl.pallas_call(
        functools.partial(ffn_kernel, blocks),
        grid_spec=grid_spec(
            1,
            tiles,
            [rows_spec(rows, D)] * 6
            + [vec, whole_spec((1, FF)), vec, whole_spec((768, QW))]
            + [whole_spec((D, FF // 4))] * 4
            + [whole_spec((FF // 4, D))] * 4
            + [whole_spec((QW, D))] * 4,
            [rows_spec(rows, FF // 4)] * 8
            + [rows_spec(rows, D)] * 5
            + [sum_spec(state_shape), sum_spec((32, D)), sum_spec((8, FF))],
        ),
        out_shape=[like((R, FF // 4), bf16)] * 8
        + [low, wide, low, low, low]
        + [like(state_shape, f32), like((32, D), f32), like((8, FF), f32)],
        compiler_params=params(),
        cost_estimate=cost(8 * R * D * FF + 2 * R * D * D, 40 * R * D),
        name="ffn",
    )(
        first, n2, cotangent, middle, att, rec, q, gain2, be, reduce_bias[None, :], ones,
        *we, *wr, *wo,
    )
    act, gh = results[0:4], results[4:8]
    layer_output, grad_middle, branch, gn, t, leading, sums2, be_sum = results[8:]

    g_in = swap_state(leading, after)

    reduce_grads = regroup([tn(a, cotangent) for a in act], n, 0)
    expand_grads = regroup([tn(n2, g) for g in gh], n, 1)
    reduce_weight_grad = sum_groups(scatter_head(reduce_grads))
    expand_weight_grad = sum_groups(scatter_head(expand_grads))

    gp_and_sum = pl.pallas_call(
        functools.partial(back_kernel, blocks, tiles),
        grid_spec=grid_spec(
            1,
            tiles,
            [back_spec(rows, D, tiles)] * 5
            + [back_spec(blocks * DH, D, tiles), back_spec(blocks * 8, D, tiles)]
            + [whole_spec(state_shape), whole_spec((768, QW))],
            [back_spec(rows, PW, tiles)] * 4 + [sum_spec((8, 3 * D))],
            [pltpu.VMEM((DH, D), f32), pltpu.VMEM((8, D), f32)],
        ),
        out_shape=[like((R, PW), bf16)] * 4 + [like((8, 3 * D), f32)],
        compiler_params=params(),
        cost_estimate=cost(8 * R * D * D, 18 * R * D),
        name="attend_back",
    )(cont, q, k, v, gn, t, st, kt, g_in, ones)
    gp, ba_sum = gp_and_sum[0:4], gp_and_sum[4]

    out_grads = regroup([tn(att, branch)], n, 0)
    output_weight_grad = sum_groups(scatter_head(out_grads))
    attend_grads = regroup([tn(normed, g) for g in gp], n, 1)
    attend_weight_grad = sum_groups(scatter_head(attend_grads))

    input_grad, sums1 = pl.pallas_call(
        input_kernel,
        grid_spec=grid_spec(
            0,
            tiles,
            [rows_spec(rows, D)] * 2
            + [vec]
            + [rows_spec(rows, PW)] * 4
            + [whole_spec((D, PW))] * 4,
            [rows_spec(rows, D), sum_spec((16, D))],
        ),
        out_shape=[wide, like((16, D), f32)],
        compiler_params=params(),
        cost_estimate=cost(2 * R * D * 3 * D, 16 * R * D),
        name="input_grad",
    )(layer_input, grad_middle, gain1, *gp, *wa)

    shared2, expand_bias_grad = sum_small(
        jnp.sum(sums2.reshape(4, 8, D), axis=1), regroup([jnp.sum(be_sum, axis=0)], n, 0)
    )
    shared1, attend_bias_grad = sum_small(
        jnp.sum(sums1.reshape(2, 8, D), axis=1), regroup([jnp.sum(ba_sum, axis=0)], n, 0)
    )
    return (
        layer_output,
        input_grad,
        shared1[0],
        shared1[1],
        attend_weight_grad,
        attend_bias_grad,
        output_weight_grad,
        shared2[0],
        shared2[1],
        shared2[2],
        expand_weight_grad,
        expand_bias_grad,
        reduce_weight_grad,
        shared2[3],
    )


def solution(mesh):
    in_specs = (
        P(("dp", "head"), None),
        P(("dp", "head"), None),
        P("dp", None),
        P("dp", None),
        P(),
        P(),
        P(None, "head"),
        P("head"),
        P("head", None),
        P(),
        P(),
        P(),
        P(None, "head"),
        P("head"),
        P("head", None),
        P(),
    )
    out_specs = (
        P(("dp", "head"), None),
        P(("dp", "head"), None),
        P(),
        P(),
        P(None, "head"),
        P("head"),
        P("head", None),
        P(),
        P(),
        P(),
        P(None, "head"),
        P("head"),
        P("head", None),
        P(),
    )
    return jax.shard_map(
        on_device, mesh=mesh, in_specs=in_specs, out_specs=out_specs, check_vma=False
    )
```

```python
import functools

import jax
import jax.numpy as jnp
from jax import lax
from jax.experimental import pallas as pl
from jax.experimental.pallas import tpu as pltpu
from jax.sharding import PartitionSpec as P

DH = 64
STRETCH = 128
D = 1024
QUADS = 4
QW = D // QUADS
PW = 3 * QW
EPS = 1e-05
VMEM = 60 * 1024 * 1024

f32 = jnp.float32
bf16 = jnp.bfloat16


def nn(a, b):
    return lax.dot_general(a, b, (((1,), (0,)), ((), ())), preferred_element_type=f32)


def nt(a, b):
    return lax.dot_general(a, b, (((1,), (1,)), ((), ())), preferred_element_type=f32)


def tn(a, b):
    return lax.dot_general(a, b, (((0,), (0,)), ((), ())), preferred_element_type=f32)


def head_rows():
    lane = lax.broadcasted_iota(jnp.int32, (1, QW), 1) // DH
    return [(lane == h).astype(f32) for h in range(4)]


def spread_heads(block, picks):
    return jnp.concatenate([block * pick for pick in picks], axis=0)


def spread_state(state, picks):
    return jnp.concatenate([state * pick for pick in picks], axis=0)


def gather_state(square, picks):
    total = square[0:DH] * picks[0]
    for h in range(1, 4):
        total = total + square[h * DH : (h + 1) * DH] * picks[h]
    return total


def centre(values):
    average = jnp.mean(values, axis=-1, keepdims=True)
    centred = values - average
    spread = jnp.mean(centred * centred, axis=-1, keepdims=True)
    inverse = lax.rsqrt(spread + EPS)
    return centred * inverse, inverse


def norm_back(xhat, inverse, grad, gain):
    w = grad * gain
    return inverse * (
        w
        - jnp.mean(w, axis=-1, keepdims=True)
        - xhat * jnp.mean(w * xhat, axis=-1, keepdims=True)
    )


def fold_rows(values):
    rows, columns = values.shape
    return jnp.sum(values.reshape(rows // 8, 8, columns), axis=0)


def normal_parts(v):
    size = jnp.abs(v) * 0.7071067811865476
    t = 1.0 / (1.0 + 0.3275911 * size)
    bell = jnp.exp(-0.5 * v * v)
    poly = t * (
        0.254829592
        + t * (-0.284496736 + t * (1.421413741 + t * (-1.453152027 + t * 1.061405429)))
    )
    tail = 0.5 * poly * bell
    return jnp.where(v < 0, tail, 1.0 - tail), bell


def qkv_kernel(blocks, fresh, thr, last, *refs):
    if fresh:
        x, gain, shift, n_out = refs[0], refs[1], refs[2], refs[9]
        wa, ba = refs[3:5], refs[5]
        q_out, k_out, v_out = refs[6:9]
        t_out = refs[10]
    else:
        n_in = refs[0]
        wa, ba = refs[1:3], refs[3]
        q_out, k_out, v_out = refs[4:7]
        t_out = refs[7]
    step = pl.program_id(0)
    rows = blocks * STRETCH

    @pl.when(step == 0)
    def _():
        t_out[...] = jnp.zeros_like(t_out)

    if fresh:
        xhat, _ = centre(x[...].astype(f32))
        normed = (xhat * gain[...] + shift[...]).astype(bf16)
        n_out[...] = normed
    else:
        normed = n_in[...]
    place = lax.broadcasted_iota(jnp.int32, (STRETCH, 128), 0)
    valid = jnp.concatenate(
        [(place >= thr[step * blocks + b]).astype(f32) for b in range(blocks)], axis=0
    )
    low = lax.broadcasted_iota(jnp.int32, (rows, 128), 1) < DH

    def feature(values):
        return jnp.where(values > 0, values + 1.0, jnp.exp(jnp.minimum(values, 0.0)))

    for g in range(2):
        project = nn(normed, wa[g][...]) + ba[:, g * PW : (g + 1) * PW]
        for pair in range(2):
            c0, c1, c2 = (
                project[:, pair * 384 + j * 128 : pair * 384 + (j + 1) * 128] for j in range(3)
            )
            at = slice(g * QW + pair * 128, g * QW + (pair + 1) * 128)
            q_out[:, at] = feature(jnp.where(low, c0, c1)).astype(bf16)
            key = pltpu.roll(jnp.where(low, c2, c0), DH, 1)
            k_out[:, at] = (valid * feature(key)).astype(bf16)
            v_out[:, at] = jnp.where(low, c1, c2).astype(bf16)
    picks = head_rows()
    for b in range(blocks):

        @pl.when(last[step * blocks + b] == 1)
        def _(b=b):
            here = slice(b * STRETCH, (b + 1) * STRETCH)
            for g in range(2):
                at = slice(g * QW, (g + 1) * QW)
                key = k_out[here, at]
                t_out[0:DH, at] += gather_state(tn(key, v_out[here, at]), picks)
                t_out[DH : DH + 8, at] += fold_rows(key.astype(f32))


def attend_kernel(blocks, cont, thr, *refs):
    qkv = refs[0:3], refs[3:6]
    x, s_in, ones, bo, gain, shift = refs[6:12]
    wo = refs[12:16]
    att_out, rec_out, st_out, kt_out, mid_out, n_out = refs[16:22]
    state, total = refs[22:24]
    step = pl.program_id(0)

    @pl.when(step == 0)
    def _():
        state[...] = s_in[0:DH]
        total[...] = jnp.broadcast_to(
            jnp.sum(s_in[DH : DH + 8], axis=0, keepdims=True), total.shape
        )

    picks = head_rows()
    low_picks = [p.astype(bf16) for p in picks]
    row = lax.broadcasted_iota(jnp.int32, (STRETCH, 512), 0)
    lane = lax.broadcasted_iota(jnp.int32, (STRETCH, 512), 1) % STRETCH
    lower = lane <= row
    for b in range(blocks):
        keep = cont[step * blocks + b].astype(f32)
        here = slice(b * STRETCH, (b + 1) * STRETCH)
        state[...] = state[...] * keep
        total[...] = total[...] * keep
        low_state = state[...].astype(bf16)
        st_out[b * DH : (b + 1) * DH, :] = low_state
        kt_out[b * 8 : (b + 1) * 8, :] = total[...]
        for g in range(QUADS):
            at = slice(g * QW, (g + 1) * QW)
            own = slice((g % 2) * QW, (g % 2 + 1) * QW)
            qb, kb, vb = (part[here, own] for part in qkv[g // 2])
            scores = nt(qb, spread_heads(kb, low_picks))
            scores = jnp.where(lower, scores, 0.0).astype(bf16)
            numer = nn(scores, spread_heads(vb, low_picks)) + nn(
                qb, spread_state(low_state[:, at], low_picks)
            )
            weighted = (qb.astype(f32) * total[0:1, at]).astype(bf16)
            denom = nn(scores, ones[0:512]) + nn(weighted, ones[512:768])
            rec = 1.0 / jnp.maximum(denom, 1.0)
            rec_out[here, at] = rec
            att_out[here, at] = (numer * rec).astype(bf16)
            state[:, at] += gather_state(tn(kb, vb), picks)
            total[:, at] += jnp.sum(kb.astype(f32), axis=0, keepdims=True)
    place = lax.broadcasted_iota(jnp.int32, (STRETCH, D), 0)
    for b in range(blocks):
        here = slice(b * STRETCH, (b + 1) * STRETCH)

        @pl.when(thr[step * blocks + b] > 0)
        def _(b=b, here=here):
            valid = (place >= thr[step * blocks + b]).astype(f32)
            rec_out[here, :] = rec_out[here, :] * valid
            att_out[here, :] = (att_out[here, :].astype(f32) * valid).astype(bf16)

    middle = x[...].astype(f32) + bo[...]
    for g in range(QUADS):
        middle = middle + nn(att_out[:, g * QW : (g + 1) * QW], wo[g][...])
    mid_out[...] = middle
    xhat, _ = centre(middle)
    n_out[...] = (xhat * gain[...] + shift[...]).astype(bf16)


def ffn_kernel(blocks, slots, fresh, final, *refs):
    refs = list(refs)

    def take(count):
        taken = refs[:count]
        del refs[:count]
        return taken

    count = sum(len(widths) for widths in slots)
    if final:
        (first,) = take(1)
    n2, cot = take(2)
    be = take(len(slots))
    if not fresh:
        part_out, part_grad = take(2)
    we, wr = take(count), take(count)
    if final:
        mid, att, rec, q01, q23, gain, br, ones = take(8)
        wo = take(4)
    de_out, dr_out, be_sum = take(len(slots)), take(len(slots)), take(len(slots))
    if final:
        out, gm_out, gb_out, gn_out, t_out, l_out, sums = take(7)
    else:
        next_out, next_grad = take(2)
    de_sum, dr_sum = take(len(slots)), take(len(slots))
    step = pl.program_id(0)

    @pl.when(step == 0)
    def _():
        for total in de_sum + dr_sum + be_sum:
            total[...] = jnp.zeros_like(total)
        if final:
            l_out[...] = jnp.zeros_like(l_out)
            sums[...] = jnp.zeros_like(sums)

    normed = n2[...]
    cotangent = cot[...]
    reduced = None if fresh else part_out[...]
    grad = None if fresh else part_grad[...]
    i = 0
    for slot, widths in enumerate(slots):
        start = 0
        for width in widths:
            at = slice(start, start + width)
            hidden = nn(normed, we[i][...]) + be[slot][:, at]
            grad_act = nt(cotangent, wr[i][...])
            phi, bell = normal_parts(hidden)
            active = (hidden * phi).astype(bf16)
            back = (grad_act * (phi + hidden * (0.3989422804014327 * bell))).astype(bf16)
            be_sum[slot][:, at] += fold_rows(back.astype(f32))
            de_sum[slot][:, at] += tn(normed, back)
            dr_sum[slot][at, :] += tn(active, cotangent)
            more = nn(active, wr[i][...])
            reduced = more if reduced is None else reduced + more
            more = nt(back, we[i][...])
            grad = more if grad is None else grad + more
            start += width
            i += 1

    @pl.when(step == pl.num_programs(0) - 1)
    def _():
        for out_ref, total in zip(de_out + dr_out, de_sum + dr_sum):
            out_ref[...] = total[...].astype(bf16)

    if not final:
        next_out[...] = reduced
        next_grad[...] = grad
        return
    middle = mid[...]
    out[...] = (middle + reduced + br[...]).astype(bf16)
    xhat, inverse = centre(middle)
    cot_wide = cotangent.astype(f32)
    grad_middle = cot_wide + norm_back(xhat, inverse, grad, gain[...])
    gm_out[...] = grad_middle
    branch = grad_middle.astype(bf16)
    gb_out[...] = branch
    sums[0:8, :] += fold_rows(branch.astype(f32))
    sums[8:16, :] += fold_rows(grad * xhat)
    sums[16:24, :] += fold_rows(grad)
    sums[24:32, :] += fold_rows(cot_wide)
    for g in range(QUADS):
        at = slice(g * QW, (g + 1) * QW)
        grad_att = nt(branch, wo[g][...]).astype(bf16).astype(f32)
        share = rec[:, at]
        numer = grad_att * share
        gn_out[:, at] = numer.astype(bf16)
        t_out[:, at] = jnp.where(
            share < 1.0, -(numer * att[:, at].astype(f32)), 0.0
        ).astype(bf16)
    picks = head_rows()
    for b in range(blocks):

        @pl.when(first[step * blocks + b] == 1)
        def _(b=b):
            here = slice(b * STRETCH, (b + 1) * STRETCH)
            for g in range(QUADS):
                at = slice(g * QW, (g + 1) * QW)
                query = (q01, q23)[g // 2][here, (g % 2) * QW : (g % 2 + 1) * QW]
                l_out[0:DH, at] += gather_state(tn(query, gn_out[here, at]), picks)
                grad_denom = nn(t_out[here, at], ones[512:768])
                l_out[DH : DH + 8, at] += fold_rows(grad_denom * query.astype(f32))


def back_kernel(blocks, tiles, quads, cont, q, k, v, gn, t, st, kt, g_in, ones, normed, *refs):
    gp_out, da_out, ba_sum = refs[0:quads], refs[quads : 2 * quads], refs[2 * quads]
    state, total = refs[2 * quads + 1 : 2 * quads + 3]
    da_sum = refs[2 * quads + 3 :]
    step = pl.program_id(0)
    tile = tiles - 1 - step

    @pl.when(step == 0)
    def _():
        state[...] = g_in[0:DH]
        total[...] = jnp.broadcast_to(
            jnp.sum(g_in[DH : DH + 8], axis=0, keepdims=True), total.shape
        )
        ba_sum[...] = jnp.zeros_like(ba_sum)
        for da in da_sum:
            da[...] = jnp.zeros_like(da)

    picks = head_rows()
    low_picks = [p.astype(bf16) for p in picks]
    row = lax.broadcasted_iota(jnp.int32, (STRETCH, 512), 0)
    lane = lax.broadcasted_iota(jnp.int32, (STRETCH, 512), 1) % STRETCH
    lower = lane <= row
    upper = lane >= row
    low_lane = lax.broadcasted_iota(jnp.int32, (STRETCH, 128), 1) < DH
    all_ones = jnp.ones((STRETCH, QW), bf16)
    for b in reversed(range(blocks)):
        keep = cont[tile * blocks + b + 1].astype(f32)
        here = slice(b * STRETCH, (b + 1) * STRETCH)
        state[...] = state[...] * keep
        total[...] = total[...] * keep
        low_state = state[...].astype(bf16)
        for g in range(quads):
            at = slice(g * QW, (g + 1) * QW)
            qb, kb, vb, gb, tb = q[here, at], k[here, at], v[here, at], gn[here, at], t[here, at]
            q_wide = qb.astype(f32)
            spread_q = spread_heads(qb, low_picks)
            spread_g = spread_heads(gb, low_picks)
            forward = spread_state(st[b * DH : (b + 1) * DH, at], low_picks)
            behind = spread_state(low_state[:, at], low_picks)
            scores = nt(gb, spread_heads(vb, low_picks)) + nt(tb, ones[0:512])
            scores = jnp.where(lower, scores, 0.0).astype(bf16)
            turned = nt(vb, spread_g) + nt(all_ones, spread_heads(tb, low_picks))
            turned = jnp.where(upper, turned, 0.0).astype(bf16)
            mixed = jnp.where(upper, nt(kb, spread_q), 0.0).astype(bf16)
            grad_denom = nn(tb, ones[512:768])
            grad_q = (
                nn(scores, spread_heads(kb, low_picks))
                + nt(gb, forward)
                + grad_denom * kt[b * 8 : b * 8 + 1, at]
            )
            grad_k = nn(turned, spread_q) + nt(vb, behind) + total[0:1, at]
            grad_v = nn(mixed, spread_g) + nn(kb, behind)
            grad_q = grad_q * jnp.minimum(q_wide, 1.0)
            grad_k = grad_k * jnp.minimum(kb.astype(f32), 1.0)
            for pair in range(2):
                two = slice(pair * 128, (pair + 1) * 128)
                swapped = pltpu.roll(grad_k[:, two], DH, 1)
                for j, piece in enumerate(
                    (
                        jnp.where(low_lane, grad_q[:, two], swapped),
                        jnp.where(low_lane, grad_v[:, two], grad_q[:, two]),
                        jnp.where(low_lane, swapped, grad_v[:, two]),
                    )
                ):
                    piece = piece.astype(bf16)
                    start = pair * 384 + j * 128
                    gp_out[g][here, start : start + 128] = piece
                    ba_sum[:, g * PW + start : g * PW + start + 128] += fold_rows(
                        piece.astype(f32)
                    )
            state[:, at] += gather_state(tn(qb, gb), picks)
            total[:, at] += jnp.sum(grad_denom * q_wide, axis=0, keepdims=True)
    for g in range(quads):
        da_sum[g][...] += tn(normed[...], gp_out[g][...])

    @pl.when(step == tiles - 1)
    def _():
        for out, da in zip(da_out, da_sum):
            out[...] = da[...].astype(bf16)


def input_kernel(x, gm, gain, *refs):
    gp, wa = refs[0:4], refs[4:8]
    out, sums = refs[-2:]

    @pl.when(pl.program_id(0) == 0)
    def _():
        sums[...] = jnp.zeros_like(sums)

    grad = nt(gp[0][...], wa[0][...])
    for g in range(1, QUADS):
        grad = grad + nt(gp[g][...], wa[g][...])
    xhat, inverse = centre(x[...].astype(f32))
    out[...] = gm[...] + norm_back(xhat, inverse, grad, gain[...])
    sums[0:8, :] += fold_rows(grad * xhat)
    sums[8:16, :] += fold_rows(grad)


def rows_spec(rows, columns, at=0, start=0):
    return pl.BlockSpec((rows, columns), lambda i, *_: (i + start, at))


def back_spec(rows, columns, tiles, at=0):
    return pl.BlockSpec((rows, columns), lambda i, *_: (tiles - 1 - i, at))


def whole_spec(shape, at=0):
    last = len(shape) - 1
    return pl.BlockSpec(
        shape, lambda i, *_: (0,) * last + (at,), pipeline_mode=pl.Buffered(1)
    )


def sum_spec(shape):
    return pl.BlockSpec(shape, lambda i, *_: (0,) * len(shape))


def call(kernel, name, scalars, tiles, ins, outs, scratch, flops, moved, aliases=None):
    return pl.pallas_call(
        kernel,
        grid_spec=pltpu.PrefetchScalarGridSpec(
            num_scalar_prefetch=len(scalars),
            grid=(tiles,),
            in_specs=[spec for _, spec in ins],
            out_specs=[spec for _, spec in outs],
            scratch_shapes=list(scratch),
        ),
        out_shape=[shape for shape, _ in outs],
        compiler_params=pltpu.CompilerParams(vmem_limit_bytes=VMEM),
        cost_estimate=pl.CostEstimate(flops=flops, bytes_accessed=moved, transcendentals=0),
        input_output_aliases=aliases or {},
        name=name,
    )(*scalars, *[array for array, _ in ins])


def tie(*values):
    return lax.optimization_barrier(list(values))


def swap(value, axis, bit):
    size = lax.axis_size(axis)
    return lax.ppermute(value, axis, [(i, i ^ bit) for i in range(size)])


def bits_of(size):
    bit, bits = 1, []
    while bit < size:
        bits.append(bit)
        bit *= 2
    return bits


def gather_shards(own):
    size = lax.axis_size("head")
    held = {0: own}
    for bit in reversed(bits_of(size)):
        for k in list(held):
            held[k ^ bit] = swap(held[k], "head", bit)
    return [held[k] for k in range(size)]


def half_of(value, which, axis):
    size = value.shape[axis] // 2
    return lax.dynamic_slice_in_dim(value, which * size, size, axis)


def regroup(parts, count, axis):
    if len(parts) == count:
        return list(parts)
    whole = jnp.concatenate(parts, axis=axis)
    width = whole.shape[axis] // count
    return [
        lax.slice_in_dim(whole, k * width, (k + 1) * width, axis=axis) for k in range(count)
    ]


def swap_state(mine, weights):
    size = lax.axis_size("head")
    sent = mine.astype(bf16)
    total = None
    for j in range(1, size):
        got = swap(sent, "head", j)
        slots = jnp.split(got, size, axis=1)
        got = jnp.concatenate([slots[k ^ j] for k in range(size)], axis=1).astype(f32)
        got = got * weights[j]
        total = got if total is None else total + got
    return total


def scatter_head(parts):
    held = dict(enumerate(parts))
    for bit in bits_of(len(parts)):
        for k in [k for k in held if k & bit]:
            got = swap(held.pop(k).astype(bf16), "head", bit)
            held[k ^ bit] = held[k ^ bit].astype(f32) + got.astype(f32)
    return held[0]


class Stages:
    def __init__(self, generator):
        self.generator, self.got = generator, None

    def advance(self):
        sent, self.got = self.generator.send(self.got)
        return sent

    def finish(self):
        while self.advance():
            pass
        return self.got[0]


def sum_stages(terms):
    size = lax.axis_size("dp")
    me = lax.axis_index("dp")
    x, z, depth = me % 2, me // 2, size // 2

    def half(which):
        total = None
        for term in terms:
            part = half_of(term, which, 0).astype(f32)
            total = part if total is None else total + part
        return total.astype(bf16)

    sent, kept = tie(half(1 - x), half(x))
    (got,) = yield [sent, kept], [swap(sent, "dp", 1)]
    mine = (kept.astype(f32) + got.astype(f32)).astype(bf16)
    rows = mine.shape[0] // depth
    own = lax.dynamic_slice_in_dim(mine, z * rows, rows, 0)
    sent = [
        lax.dynamic_slice_in_dim(mine, (z ^ j) * rows, rows, 0) for j in range(1, depth)
    ]
    own, *sent = tie(own, *sent)
    got = yield [own] + sent, [swap(part, "dp", 2 * j) for j, part in enumerate(sent, 1)]
    total = own.astype(f32)
    for part in got:
        total = total + part.astype(f32)
    (own,) = tie(total.astype(bf16))
    got = yield [own], [swap(own, "dp", 2 * j) for j in range(1, depth)]
    (mine,) = tie(jnp.concatenate([own] + list(got), axis=0))
    (other,) = yield [mine], [swap(mine, "dp", 1)]

    def natural(value):
        for bit in bits_of(depth):
            shaped = value.reshape(depth // (2 * bit), 2, bit * rows, value.shape[1])
            turned = jnp.flip(shaped, axis=1)
            value = jnp.where((z & bit) != 0, turned, shaped).reshape(value.shape)
        return value

    mine, other = natural(mine), natural(other)
    pair = [jnp.where(x == 0, mine, other), jnp.where(x == 0, other, mine)]
    yield [], [jnp.concatenate(pair, axis=0).astype(f32)]


class Window:
    def __init__(self, *after):
        self.after, self.sent, self.got, self.chains = after, [], [], []

    def swap(self, value, axis, bit):
        value = tie(value, *self.after)[0]
        self.sent.append(value)
        self.got.append(swap(value, axis, bit))
        return Later(self, len(self.got) - 1)

    def step(self, chain):
        self.sent += chain.advance()
        self.chains.append((chain, len(self.got)))
        self.got += chain.got

    def open(self, *values):
        return tie(*values, *self.sent)[: len(values)]

    def close(self, *values):
        tied = tie(*values, *self.got)
        self.got = tied[len(values) :]
        for chain, start in self.chains:
            chain.got = self.got[start : start + len(chain.got)]
        return tied[: len(values)]


class Later:
    def __init__(self, window, place):
        self.window, self.place = window, place

    def get(self):
        return self.window.got[self.place]


def small_stages(shared, split):
    size = len(split)
    held = dict(enumerate(split))
    flat = shared.reshape(-1)
    for bit in bits_of(size):
        gone = [k for k in held if k & bit]
        (sent,) = tie(jnp.concatenate([flat] + [held[k] for k in gone]))
        (got,) = yield [sent], [swap(sent, "head", bit)]
        at = flat.shape[0]
        flat = flat + got[:at]
        for k in gone:
            width = held[k].shape[0]
            held[k ^ bit] = held[k ^ bit] + got[at : at + width]
            del held[k]
            at += width
    both = jnp.concatenate([flat, held[0]])
    for bit in bits_of(lax.axis_size("dp")):
        (both,) = tie(both)
        (got,) = yield [both], [swap(both, "dp", bit)]
        both = both + got
    yield [], [(both[: flat.shape[0]].reshape(shared.shape), both[flat.shape[0] :])]


def on_device(
    layer_input,
    cotangent,
    crop_blocks,
    crop_padding,
    first_gain,
    first_shift,
    attend_weight,
    attend_bias,
    output_weight,
    output_bias,
    second_gain,
    second_shift,
    expand_weight,
    expand_bias,
    reduce_weight,
    reduce_bias,
):
    R = layer_input.shape[0]
    n = lax.axis_size("head")
    me = lax.axis_index("head")
    x = lax.axis_index("dp") % 2
    nb = R // STRETCH
    FF = expand_weight.shape[1] * n
    FQ = FF // QUADS
    fast = n == QUADS

    if fast:
        near = swap(attend_weight, "head", 1)
        ba_near = jnp.concatenate([attend_bias, swap(attend_bias, "head", 1)])
        be_near = jnp.concatenate([expand_bias, swap(expand_bias, "head", 1)])
        wa = [attend_weight, near, None, None]
        w = Window()
        wa_far = w.swap(attend_weight, "head", 2)
        bias_far = w.swap(jnp.concatenate([ba_near, be_near]), "head", 2)
        wo_near = w.swap(output_weight, "head", 1)
        we_near = w.swap(expand_weight, "head", 1)
        wr_near = w.swap(reduce_weight, "head", 1)
    else:
        wa = regroup(gather_shards(attend_weight), QUADS, 1)
        ba_near, ba_far = jnp.split(jnp.concatenate(gather_shards(attend_bias)), 2)

    sizes, pads = crop_blocks[0], crop_padding[0]
    crops = sizes.shape[0]
    closing = jnp.sum(jnp.tril(jnp.ones((crops, crops), jnp.int32)) * sizes[None, :], axis=1)

    def crop_of(position):
        return jnp.sum((position[..., None] >= closing).astype(jnp.int32), axis=-1)

    spots = me * nb + jnp.arange(nb, dtype=jnp.int32)
    crop = crop_of(spots)
    belongs = crop[:, None] == jnp.arange(crops, dtype=jnp.int32)[None, :]
    opening = jnp.sum(jnp.where(belongs, (closing - sizes)[None, :], 0), axis=1)
    padding = jnp.sum(jnp.where(belongs, pads[None, :], 0), axis=1)
    thr = jnp.maximum(padding - (spots - opening) * STRETCH, 0).astype(jnp.int32)
    first = (crop == crop[0]).astype(jnp.int32)
    last = (crop == crop[nb - 1]).astype(jnp.int32)
    one = jnp.ones((1,), jnp.int32)
    cont = jnp.concatenate([one, (crop[1:] == crop[:-1]).astype(jnp.int32), one])
    others = me ^ jnp.arange(n, dtype=jnp.int32)
    opens = crop_of(others * nb)
    closes = crop_of(others * nb + nb - 1)
    before = jnp.logical_and(others < me, closes == crop[0]).astype(f32)
    after = jnp.logical_and(others > me, opens == crop[nb - 1]).astype(f32)

    line = lax.broadcasted_iota(jnp.int32, (768, QW), 0)
    lane_head = lax.broadcasted_iota(jnp.int32, (768, QW), 1) // DH
    ones = (jnp.where(line < 512, line // STRETCH, (line - 512) // DH) == lane_head).astype(bf16)

    blocks = 2 if nb % 2 == 0 else 1
    rows = blocks * STRETCH
    tiles = R // rows
    gain1, shift1 = first_gain[None, :], first_shift[None, :]
    gain2, shift2 = second_gain[None, :], second_shift[None, :]
    like = jax.ShapeDtypeStruct
    HALF = D // 2
    full, side = rows_spec(rows, D), rows_spec(rows, HALF)
    low, wide = (like((R, D), bf16), full), (like((R, D), f32), full)
    narrow = (like((R, HALF), bf16), side)
    vec = whole_spec((1, D))
    state_rows = DH + 8

    def vector(value):
        return (value, vec)

    def project(source, pick, bias, fresh):
        ins = [(source, full)]
        if fresh:
            ins += [vector(gain1), vector(shift1)]
        ins += [(wa[k], whole_spec((D, PW))) for k in pick]
        ins += [(bias, whole_spec((1, 2 * PW)))]
        outs = [narrow] * 3 + ([low] if fresh else [])
        outs += [(like((state_rows, HALF), f32), sum_spec((state_rows, HALF)))]
        return call(
            functools.partial(qkv_kernel, blocks, fresh),
            "qkv",
            (thr, last),
            tiles,
            ins,
            outs,
            [],
            3 * R * D * D,
            8 * R * D + 3 * D * D,
        )

    bias = ba_near[None, :]
    source = layer_input
    if fast:
        source, bias = w.open(source, bias)
    q01, k01, v01, normed, trail01 = project(source, (0, 1), bias, True)
    if fast:
        q01, k01, v01, normed, trail01 = w.close(q01, k01, v01, normed, trail01)
        wa[2] = wa_far.get()
        wa[3] = swap(wa[2], "head", 1)
        ba_far, be_far = bias_far.get()[: ba_near.shape[0]], bias_far.get()[ba_near.shape[0] :]
        be_slots = jnp.split(jnp.concatenate([be_near, be_far]), QUADS)
        wo = [output_weight, wo_near.get(), None, None]
        w = Window(trail01)
        wo_far = w.swap(output_weight, "head", 2)
        normed, wa[3] = w.open(normed, wa[3])
    else:
        wo = regroup(gather_shards(output_weight), QUADS, 0)
        we = regroup(gather_shards(expand_weight), QUADS, 1)
        wr = regroup(gather_shards(reduce_weight), QUADS, 0)
        be_slots = jnp.split(jnp.concatenate(gather_shards(expand_bias)), QUADS)
    q23, k23, v23, trail23 = project(normed, (2, 3), ba_far[None, :], False)
    if fast:
        q23, k23, v23, trail23 = w.close(q23, k23, v23, trail23)
        wo[2] = wo_far.get()
        wo[3] = swap(wo[2], "head", 1)
    s_in = swap_state(jnp.concatenate([trail01, trail23], axis=1), before)
    if fast:
        w = Window(s_in)
        wr_far = w.swap(reduce_weight, "head", 2)
        (s_in,) = w.open(s_in)

    att, rec, st, kt, middle, n2 = call(
        functools.partial(attend_kernel, blocks),
        "attend",
        (cont, thr),
        tiles,
        [(a, side) for a in (q01, k01, v01, q23, k23, v23)]
        + [
            (layer_input, full),
            (s_in, whole_spec((state_rows, D))),
            (ones, whole_spec((768, QW))),
            vector(output_bias[None, :]),
            vector(gain2),
            vector(shift2),
        ]
        + [(w, whole_spec((QW, D))) for w in wo],
        [
            low,
            wide,
            (like((nb * DH, D), bf16), rows_spec(blocks * DH, D)),
            (like((nb * 8, D), f32), rows_spec(blocks * 8, D)),
            wide,
            low,
        ],
        [pltpu.VMEM((DH, D), f32), pltpu.VMEM((8, D), f32)],
        12 * R * D * D,
        20 * R * D,
    )

    if fast:
        att, rec, st, kt, middle, n2 = w.close(att, rec, st, kt, middle, n2)
        we = [expand_weight, we_near.get(), None, None]
        wr = [reduce_weight, wr_near.get(), wr_far.get(), None]

    def ffn(picks, part, extra):
        slots = [[FQ]] * len(picks)
        ins = [(n2, full), (cotangent, full)]
        ins += [(be_slots[k][None, :], whole_spec((1, FQ))) for k in picks]
        if part is not None:
            ins += [(part[0], full), (part[1], full)]
        ins += [(we[k], whole_spec(we[k].shape)) for k in picks]
        ins += [(wr[k], whole_spec(wr[k].shape)) for k in picks]
        outs = [(like((D, FQ), bf16), whole_spec((D, FQ)))] * len(picks)
        outs += [(like((FQ, D), bf16), whole_spec((FQ, D)))] * len(picks)
        outs += [(like((8, FQ), f32), sum_spec((8, FQ)))] * len(picks)
        if extra is None:
            outs += [wide, wide]
        else:
            ins += extra
            outs += [low, wide, low, low, low]
            outs += [
                (like((state_rows, D), f32), sum_spec((state_rows, D))),
                (like((32, D), f32), sum_spec((32, D))),
            ]
        results = call(
            functools.partial(ffn_kernel, blocks, slots, part is None, extra is not None),
            "ffn",
            (first,) if extra is not None else (),
            tiles,
            ins,
            outs,
            [pltpu.VMEM((D, FQ), f32)] * len(picks) + [pltpu.VMEM((FQ, D), f32)] * len(picks),
            12 * R * D * FQ * len(picks),
            20 * R * D,
        )
        for i, k in enumerate(picks):
            de[k], dr[k], eb[k] = (results[i + j * len(picks)] for j in range(3))
        return list(results[3 * len(picks) :])

    de, dr, eb = [None] * 4, [None] * 4, [None] * 4
    extra = [
        (middle, full),
        (att, full),
        (rec, full),
        (q01, side),
        (q23, side),
        vector(gain2),
        vector(reduce_bias[None, :]),
        (ones, whole_spec((768, QW))),
    ] + [(w, whole_spec((QW, D))) for w in wo]
    if fast:
        w = Window(n2)
        we_far = w.swap(expand_weight, "head", 2)
        wr_last = w.swap(wr[2], "head", 1)
        (n2,) = w.open(n2)
        part = ffn((1,), None, None)
        n2, *part = w.close(n2, *part)
        we[2], wr[3] = we_far.get(), wr_last.get()
        we[3] = swap(we[2], "head", 1)
        w = Window(part[0])
        near = w.swap(de[1], "head", 1), w.swap(dr[1], "head", 1)
        (part[0],) = w.open(part[0])
        part = ffn((3,), part, None)
        part = w.close(*part)
        near = [late.get() for late in near]
        w = Window(part[0])
        got = w.swap(de[3], "head", 1), w.swap(dr[3], "head", 1)
        (part[0],) = w.open(part[0])
        part = ffn((2,), part, None)
        part[0], part[1], de[2], dr[2] = w.close(*part, de[2], dr[2])
        far = [
            (a.astype(f32) + b.get().astype(f32)).astype(bf16)
            for a, b in zip((de[2], dr[2]), got)
        ]
        w = Window(part[0])
        r_cut = jnp.split(far[1], 2)
        e_far = w.swap(far[0], "head", 2)
        r_far = w.swap(r_cut[0], "head", 2)
        (part[0],) = w.open(part[0])
        results = ffn((0,), part, extra)
        de[0], dr[0], *results = w.close(de[0], dr[0], *results)
    else:
        part = ffn((3,), None, None)
        part = ffn((2,), part, None)
        results = ffn((1, 0), part, extra)
    layer_output, grad_middle, branch, gn, t, leading, sums2 = results

    def back(pick, q, k, v, state):
        count = len(pick)
        at, inner, width = pick[0] // count, (pick[0] % 2) // count, count * QW
        return call(
            functools.partial(back_kernel, blocks, tiles, count),
            "attend_back",
            (cont,),
            tiles,
            [(a, back_spec(rows, width, tiles, inner)) for a in (q, k, v)]
            + [(a, back_spec(rows, width, tiles, at)) for a in (gn, t)]
            + [
                (st, back_spec(blocks * DH, width, tiles, at)),
                (kt, back_spec(blocks * 8, width, tiles, at)),
                (state, whole_spec((state_rows, width), at)),
                (ones, whole_spec((768, QW))),
                (normed, back_spec(rows, D, tiles)),
            ],
            [(like((R, PW), bf16), back_spec(rows, PW, tiles))] * count
            + [(like((D, PW), bf16), whole_spec((D, PW)))] * count
            + [(like((8, count * PW), f32), sum_spec((8, count * PW)))],
            [pltpu.VMEM((DH, width), f32), pltpu.VMEM((8, width), f32)]
            + [pltpu.VMEM((D, PW), f32)] * count,
            6 * count * R * D * D,
            5 * count * R * D,
        )

    def inputs(start, count, out, x_in):
        at = rows_spec(rows, D, 0, start)
        ins = [(x_in, at), (grad_middle, at), vector(gain1)]
        ins += [(g, rows_spec(rows, PW, 0, start)) for g in gp]
        ins += [(w, whole_spec((D, PW))) for w in wa]
        if out is not None:
            ins += [(out, pl.BlockSpec(memory_space=pl.ANY))]
        return call(
            input_kernel,
            "input_grad",
            (),
            count,
            ins,
            [(wide[0], at), (like((16, D), f32), sum_spec((16, D)))],
            [],
            6 * rows * count * D * D,
            16 * rows * count * D,
            None if out is None else {len(ins) - 1: 0},
        )

    gp = [None] * 4
    shared2 = jnp.sum(sums2.reshape(4, 8, D), axis=1)
    eb = regroup([jnp.sum(e, axis=0) for e in eb], n, 0)
    ss = Stages(small_stages(shared2, eb))
    if fast:
        es = Stages(sum_stages([de[0], near[0], e_far.get()]))
        w = Window(branch)
        w.step(es)
        g_in = swap_state(leading, after)
        (branch,) = tie(branch, *w.sent)[:1]
        do = tn(att, branch).astype(bf16)
        do, g_in = tie(do, g_in)
        w.after = (g_in,)
        do = jnp.split(do, QUADS)
        r_far_last = w.swap(r_cut[1], "head", 2)

        def back_beside(w, k, g_in):
            w.step(ss)
            (g_in,) = w.open(g_in)
            parts = (q01, k01, v01) if k < 2 else (q23, k23, v23)
            gp[k], da, ba_part = back((k,), *parts, g_in)
            gp[k], da, ba_part, g_in = w.close(gp[k], da, ba_part, g_in)
            return da, ba_part, g_in

        o_got = w.swap(do[3], "head", 1), w.swap(do[1], "head", 1)
        da3, ba3, g_in = back_beside(w, 3, g_in)

        o_far = (do[2].astype(f32) + o_got[0].get().astype(f32)).astype(bf16)
        r_far = jnp.concatenate([r_far.get(), r_far_last.get()], axis=0)
        rs = Stages(sum_stages([dr[0], near[1], r_far]))
        w = Window(g_in)
        w.step(es)
        w.step(rs)
        a_got = w.swap(da3, "head", 1)
        o_far = w.swap(o_far, "head", 2)
        da2, ba2, g_in = back_beside(w, 2, g_in)

        a_far = (da2.astype(f32) + a_got.get().astype(f32)).astype(bf16)
        os = Stages(sum_stages([do[0], o_got[1].get(), o_far.get()]))
        a_cut = jnp.split(a_far, 2)
        w = Window(g_in)
        a_far = w.swap(a_cut[0], "head", 2)
        w.step(rs)
        w.step(os)
        da1, ba1, g_in = back_beside(w, 1, g_in)

        w = Window(g_in)
        a_far_last = w.swap(a_cut[1], "head", 2)
        a_near = w.swap(da1, "head", 1)
        w.step(es)
        w.step(os)
        da0, ba0, g_in = back_beside(w, 0, g_in)

        a_far = jnp.concatenate([a_far.get(), a_far_last.get()], axis=0)
        at = Stages(sum_stages([da0, a_near.get(), a_far]))
        w = Window(g_in)
        w.step(at)
        w.step(rs)
        w.step(ss)
        half = tiles // 2
        (layer_in,) = w.open(layer_input)
        input_grad, sums1 = inputs(0, half, None, layer_in)
        input_grad, sums1 = w.close(input_grad, sums1)
        w = Window(input_grad)
        w.step(at)
        w.step(es)
        w.step(os)
        (input_grad,) = w.open(input_grad)
        input_grad, more = inputs(half, tiles - half, input_grad, layer_in)
        input_grad, more = w.close(input_grad, more)
        sums1 = sums1 + more
        expand_weight_grad = es.finish()
        reduce_weight_grad = rs.finish()
        attend_weight_grad = at.finish()
        output_weight_grad = os.finish()
        ba_sum = jnp.concatenate([ba0, ba1, ba2, ba3], axis=1)
    else:
        g_in = swap_state(leading, after)
        gp[2], gp[3], *da23, ba23 = back((2, 3), q23, k23, v23, g_in)
        gp[0], gp[1], *da01, ba01 = back((0, 1), q01, k01, v01, g_in)
        do = [tn(att, branch).astype(bf16)]

        def reduce(grads, axis):
            return Stages(sum_stages([scatter_head(regroup(grads, n, axis))])).finish()

        expand_weight_grad = reduce(de, 1)
        reduce_weight_grad = reduce(dr, 0)
        attend_weight_grad = reduce(da01 + da23, 1)
        output_weight_grad = reduce(do, 0)
        input_grad, sums1 = inputs(0, tiles, None, layer_input)
        ba_sum = jnp.concatenate([ba01, ba23], axis=1)

    shared2, expand_bias_grad = ss.finish()
    shared1, attend_bias_grad = Stages(
        small_stages(
            jnp.sum(sums1.reshape(2, 8, D), axis=1),
            regroup([jnp.sum(ba_sum, axis=0)], n, 0),
        )
    ).finish()
    return (
        layer_output,
        input_grad,
        shared1[0],
        shared1[1],
        attend_weight_grad,
        attend_bias_grad,
        output_weight_grad,
        shared2[0],
        shared2[1],
        shared2[2],
        expand_weight_grad,
        expand_bias_grad,
        reduce_weight_grad,
        shared2[3],
    )


def solution(mesh):
    in_specs = (
        P(("dp", "head"), None),
        P(("dp", "head"), None),
        P("dp", None),
        P("dp", None),
        P(),
        P(),
        P(None, "head"),
        P("head"),
        P("head", None),
        P(),
        P(),
        P(),
        P(None, "head"),
        P("head"),
        P("head", None),
        P(),
    )
    out_specs = (
        P(("dp", "head"), None),
        P(("dp", "head"), None),
        P(),
        P(),
        P(None, "head"),
        P("head"),
        P("head", None),
        P(),
        P(),
        P(),
        P(None, "head"),
        P("head"),
        P("head", None),
        P(),
    )
    return jax.shard_map(
        on_device, mesh=mesh, in_specs=in_specs, out_specs=out_specs, check_vma=False
    )
```

```python
import functools

import jax
import jax.numpy as jnp
from jax import lax
from jax.experimental import pallas as pl
from jax.experimental.pallas import tpu as pltpu
from jax.sharding import PartitionSpec as P

DH = 64
STRETCH = 128
D = 1024
QUADS = 4
QW = D // QUADS
PW = 3 * QW
EPS = 1e-05
VMEM = 60 * 1024 * 1024

f32 = jnp.float32
bf16 = jnp.bfloat16


def nn(a, b):
    return lax.dot_general(a, b, (((1,), (0,)), ((), ())), preferred_element_type=f32)


def nt(a, b):
    return lax.dot_general(a, b, (((1,), (1,)), ((), ())), preferred_element_type=f32)


def tn(a, b):
    return lax.dot_general(a, b, (((0,), (0,)), ((), ())), preferred_element_type=f32)


PAIR = 2 * DH


def side_rows(kind):
    lane = lax.broadcasted_iota(jnp.int32, (1, PAIR), 1) // DH
    return [(lane == h).astype(kind) for h in range(2)]


def spread(block, picks):
    return jnp.concatenate([block * picks[0], block * picks[1]], axis=0)


def pair_product(left, right, picks):
    square = tn(left, right)
    return square[0:DH] * picks[0] + square[DH:PAIR] * picks[1]


def cut(start, width=PAIR):
    return slice(start * width, (start + 1) * width)


def centre(values):
    average = jnp.mean(values, axis=-1, keepdims=True)
    centred = values - average
    spread = jnp.mean(centred * centred, axis=-1, keepdims=True)
    inverse = lax.rsqrt(spread + EPS)
    return centred * inverse, inverse


def norm_back(xhat, inverse, grad, gain):
    w = grad * gain
    return inverse * (
        w
        - jnp.mean(w, axis=-1, keepdims=True)
        - xhat * jnp.mean(w * xhat, axis=-1, keepdims=True)
    )


def fold_rows(values):
    rows, columns = values.shape
    return jnp.sum(values.reshape(rows // 8, 8, columns), axis=0)


def normal_parts(v):
    size = jnp.abs(v) * 0.7071067811865476
    t = 1.0 / (1.0 + 0.3275911 * size)
    bell = jnp.exp(-0.5 * v * v)
    poly = t * (
        0.254829592
        + t * (-0.284496736 + t * (1.421413741 + t * (-1.453152027 + t * 1.061405429)))
    )
    tail = 0.5 * poly * bell
    return jnp.where(v < 0, tail, 1.0 - tail), bell


def qkv_kernel(blocks, fresh, thr, cont, *refs):
    if fresh:
        x, gain, shift, n_out = refs[0], refs[1], refs[2], refs[9]
        wa, ba = refs[3:5], refs[5]
        q_out, k_out, v_out = refs[6:9]
        t_out, st_out, kt_out, state, sums = refs[10:15]
    else:
        n_in = refs[0]
        wa, ba = refs[1:3], refs[3]
        q_out, k_out, v_out = refs[4:7]
        t_out, st_out, kt_out, state, sums = refs[7:12]
    step = pl.program_id(0)
    rows = blocks * STRETCH

    @pl.when(step == 0)
    def _():
        state[...] = jnp.zeros_like(state)
        sums[...] = jnp.zeros_like(sums)

    if fresh:
        xhat, _ = centre(x[...].astype(f32))
        normed = (xhat * gain[...] + shift[...]).astype(bf16)
        n_out[...] = normed
    else:
        normed = n_in[...]
    place = lax.broadcasted_iota(jnp.int32, (STRETCH, 128), 0)
    valid = jnp.concatenate(
        [(place >= thr[step * blocks + b]).astype(f32) for b in range(blocks)], axis=0
    )
    low = lax.broadcasted_iota(jnp.int32, (rows, 128), 1) < DH

    def feature(values):
        return jnp.where(values > 0, values + 1.0, jnp.exp(jnp.minimum(values, 0.0)))

    for g in range(2):
        project = nn(normed, wa[g][...]) + ba[:, g * PW : (g + 1) * PW]
        for pair in range(2):
            c0, c1, c2 = (
                project[:, pair * 384 + j * 128 : pair * 384 + (j + 1) * 128] for j in range(3)
            )
            at = slice(g * QW + pair * 128, g * QW + (pair + 1) * 128)
            q_out[:, at] = feature(jnp.where(low, c0, c1)).astype(bf16)
            key = pltpu.roll(jnp.where(low, c2, c0), DH, 1)
            k_out[:, at] = (valid * feature(key)).astype(bf16)
            v_out[:, at] = jnp.where(low, c1, c2).astype(bf16)
    picks = side_rows(f32)
    for b in range(blocks):
        keep = cont[step * blocks + b].astype(f32)
        here = cut(b, STRETCH)
        state[...] = state[...] * keep
        sums[...] = sums[...] * keep
        st_out[cut(b, DH), :] = state[...]
        kt_out[cut(b, 8), :] = sums[...]
        for p in range(4):
            key = k_out[here, cut(p)]
            state[:, cut(p)] += pair_product(key, v_out[here, cut(p)], picks)
            sums[:, cut(p)] += fold_rows(key.astype(f32))

    @pl.when(step == pl.num_programs(0) - 1)
    def _():
        t_out[0:DH, :] = state[...]
        t_out[DH : DH + 8, :] = sums[...]


def attend_kernel(blocks, first, thr, *refs):
    qkv = refs[0:5], refs[5:10]
    x, s_in, bo, gain, shift = refs[10:15]
    wo = refs[15:19]
    att_out, rec_out, st_out, kt_out, mid_out, n_out = refs[19:25]
    step = pl.program_id(0)
    picks = side_rows(bf16)
    row = lax.broadcasted_iota(jnp.int32, (STRETCH, 2 * STRETCH), 0)
    lane = lax.broadcasted_iota(jnp.int32, (STRETCH, 2 * STRETCH), 1) % STRETCH
    lower = lane <= row
    ones_scores = spread(jnp.ones((STRETCH, PAIR), bf16), picks)
    ones_state = spread(jnp.ones((DH, PAIR), bf16), picks)
    zeros = jnp.zeros((PAIR, PAIR), bf16)
    ones = jnp.concatenate([ones_scores, zeros, ones_state], axis=0)
    came = jnp.sum(s_in[DH : DH + 8], axis=0, keepdims=True)
    for b in range(blocks):
        joins = first[step * blocks + b].astype(f32)
        here = cut(b, STRETCH)
        for p in range(8):
            at, own = cut(p), cut(p % 4)
            q, k, v, st, kt = qkv[p // 4]
            qb, kb, vb = q[here, own], k[here, own], v[here, own]
            state = (st[cut(b, DH), own] + joins * s_in[0:DH, at]).astype(bf16)
            total = jnp.sum(kt[cut(b, 8), own], axis=0, keepdims=True) + joins * came[:, at]
            st_out[cut(b, DH), at] = state
            kt_out[cut(b, 8), at] = jnp.broadcast_to(total, (8, PAIR))
            scores = nt(qb, spread(kb, picks))
            scores = jnp.where(lower, scores, 0.0).astype(bf16)
            weighted = (qb.astype(f32) * total).astype(bf16)
            left = jnp.concatenate([scores, qb, weighted], axis=1)
            right = jnp.concatenate([spread(vb, picks), spread(state, picks), zeros], axis=0)
            both = nn(left, jnp.concatenate([right, ones], axis=1))
            rec = 1.0 / jnp.maximum(both[:, PAIR:], 1.0)
            rec_out[here, at] = rec
            att_out[here, at] = (both[:, :PAIR] * rec).astype(bf16)
    place = lax.broadcasted_iota(jnp.int32, (STRETCH, D), 0)
    for b in range(blocks):
        here = slice(b * STRETCH, (b + 1) * STRETCH)

        @pl.when(thr[step * blocks + b] > 0)
        def _(b=b, here=here):
            valid = (place >= thr[step * blocks + b]).astype(f32)
            rec_out[here, :] = rec_out[here, :] * valid
            att_out[here, :] = (att_out[here, :].astype(f32) * valid).astype(bf16)

    middle = x[...].astype(f32) + bo[...]
    for g in range(QUADS):
        middle = middle + nn(att_out[:, g * QW : (g + 1) * QW], wo[g][...])
    mid_out[...] = middle
    xhat, _ = centre(middle)
    n_out[...] = (xhat * gain[...] + shift[...]).astype(bf16)


def ffn_kernel(blocks, widths, fresh, final, *refs):
    refs = list(refs)

    def take(count):
        taken = refs[:count]
        del refs[:count]
        return taken

    count = len(widths)
    if final:
        (first,) = take(1)
    n2, cot = take(2)
    be = take(count)
    if not fresh:
        part_out, part_grad = take(2)
    we, wr = take(count), take(count)
    if final:
        mid, att, rec, q01, q23, gain, br = take(7)
        wo = take(4)
    grad_out, be_sum = take(count), take(count)
    if final:
        out, gm_out, gb_out, gn_out, t_out, l_out, pr_out, kr_out, sums = take(9)
    else:
        next_out, next_grad = take(2)
    grad_sum = take(count)
    step = pl.program_id(0)

    @pl.when(step == 0)
    def _():
        for total in grad_sum + be_sum:
            total[...] = jnp.zeros_like(total)
        if final:
            l_out[...] = jnp.zeros_like(l_out)
            sums[...] = jnp.zeros_like(sums)

    normed = n2[...]
    cotangent = cot[...]
    reduced = None if fresh else part_out[...]
    grad = None if fresh else part_grad[...]
    for i, width in enumerate(widths):
        hidden = nn(normed, we[i][...]) + be[i][...]
        grad_act = nt(cotangent, wr[i][...])
        phi, bell = normal_parts(hidden)
        active = (hidden * phi).astype(bf16)
        back = (grad_act * (phi + hidden * (0.3989422804014327 * bell))).astype(bf16)
        be_sum[i][...] += fold_rows(back.astype(f32))
        grad_sum[i][0:width, :] += tn(back, normed)
        grad_sum[i][width : 2 * width, :] += tn(active, cotangent)
        more = nn(active, wr[i][...])
        reduced = more if reduced is None else reduced + more
        more = nt(back, we[i][...])
        grad = more if grad is None else grad + more

    @pl.when(step == pl.num_programs(0) - 1)
    def _():
        for out_ref, total in zip(grad_out, grad_sum):
            out_ref[...] = total[...].astype(bf16)

    if not final:
        next_out[...] = reduced
        next_grad[...] = grad
        return
    middle = mid[...]
    out[...] = (middle + reduced + br[...]).astype(bf16)
    xhat, inverse = centre(middle)
    cot_wide = cotangent.astype(f32)
    grad_middle = cot_wide + norm_back(xhat, inverse, grad, gain[...])
    gm_out[...] = grad_middle
    branch = grad_middle.astype(bf16)
    gb_out[...] = branch
    sums[0:8, :] += fold_rows(branch.astype(f32))
    sums[8:16, :] += fold_rows(grad * xhat)
    sums[16:24, :] += fold_rows(grad)
    sums[24:32, :] += fold_rows(cot_wide)
    for g in range(QUADS):
        at = slice(g * QW, (g + 1) * QW)
        grad_att = nt(branch, wo[g][...]).astype(bf16).astype(f32)
        share = rec[:, at]
        numer = grad_att * share
        gn_out[:, at] = numer.astype(bf16)
        t_out[:, at] = jnp.where(
            share < 1.0, -(numer * att[:, at].astype(f32)), 0.0
        ).astype(bf16)
    picks = side_rows(f32)
    ones = spread(jnp.ones((DH, PAIR), bf16), side_rows(bf16))
    for b in range(blocks):
        here = cut(b, STRETCH)
        for p in range(8):
            at = cut(p)
            query = (q01, q23)[p // 4][here, cut(p % 4)]
            pr_out[cut(b, DH), at] = pair_product(query, gn_out[here, at], picks)
            grad_denom = nn(t_out[here, at], ones)
            kr_out[cut(b, 8), at] = fold_rows(grad_denom * query.astype(f32))

        @pl.when(first[step * blocks + b] == 1)
        def _(b=b):
            l_out[0:DH, :] += pr_out[cut(b, DH), :]
            l_out[DH : DH + 8, :] += kr_out[cut(b, 8), :]


def back_kernel(blocks, tiles, quads, cont, q, k, v, gn, t, st, kt, pr, kr, g_in, normed, att, branch, *refs):
    gp_out, da_out, ba_sum = refs[0:quads], refs[quads : 2 * quads], refs[2 * quads]
    state, total = refs[2 * quads + 1 : 2 * quads + 3]
    da_sum = refs[2 * quads + 3 :]
    step = pl.program_id(0)
    tile = tiles - 1 - step

    @pl.when(step == 0)
    def _():
        state[...] = g_in[0:DH]
        total[...] = jnp.broadcast_to(
            jnp.sum(g_in[DH : DH + 8], axis=0, keepdims=True), total.shape
        )
        ba_sum[...] = jnp.zeros_like(ba_sum)
        for da in da_sum:
            da[...] = jnp.zeros_like(da)

    picks = side_rows(bf16)
    row = lax.broadcasted_iota(jnp.int32, (STRETCH, 2 * STRETCH), 0)
    lane = lax.broadcasted_iota(jnp.int32, (STRETCH, 2 * STRETCH), 1) % STRETCH
    lower = lane <= row
    upper = lane >= row
    low_lane = lax.broadcasted_iota(jnp.int32, (STRETCH, PAIR), 1) < DH
    all_ones = jnp.ones((STRETCH, PAIR), bf16)
    ones_scores = spread(all_ones, picks)
    ones_state = spread(jnp.ones((DH, PAIR), bf16), picks)
    for b in reversed(range(blocks)):
        keep = cont[tile * blocks + b + 1].astype(f32)
        here = cut(b, STRETCH)
        for p in range(2 * quads):
            at = cut(p)
            qb, kb, vb, gb, tb = q[here, at], k[here, at], v[here, at], gn[here, at], t[here, at]
            state_here = state[:, at] * keep
            total_here = total[:, at] * keep
            behind = spread(state_here.astype(bf16), picks)
            state[:, at] = state_here + pr[cut(b, DH), at]
            total[:, at] = total_here + jnp.sum(kr[cut(b, 8), at], axis=0, keepdims=True)
            spread_q, spread_g = spread(qb, picks), spread(gb, picks)
            forward = spread(st[cut(b, DH), at], picks)
            scores = nt(
                jnp.concatenate([gb, tb], axis=1),
                jnp.concatenate([spread(vb, picks), ones_scores], axis=1),
            )
            scores = jnp.where(lower, scores, 0.0).astype(bf16)
            turned = nt(
                jnp.concatenate([vb, all_ones], axis=1),
                jnp.concatenate([spread_g, spread(tb, picks)], axis=1),
            )
            turned = jnp.where(upper, turned, 0.0).astype(bf16)
            mixed = jnp.where(upper, nt(kb, spread_q), 0.0).astype(bf16)
            grad_denom = nn(tb, ones_state)
            grad_q = (
                nn(scores, spread(kb, picks))
                + nt(gb, forward)
                + grad_denom * kt[b * 8 : b * 8 + 1, at]
            )
            grad_k = nn(turned, spread_q) + nt(vb, behind) + total_here[0:1]
            grad_v = nn(jnp.concatenate([mixed, kb], axis=1), jnp.concatenate([spread_g, behind]))
            grad_q = grad_q * jnp.minimum(qb.astype(f32), 1.0)
            grad_k = grad_k * jnp.minimum(kb.astype(f32), 1.0)
            swapped = pltpu.roll(grad_k, DH, 1)
            for j, piece in enumerate(
                (
                    jnp.where(low_lane, grad_q, swapped),
                    jnp.where(low_lane, grad_v, grad_q),
                    jnp.where(low_lane, swapped, grad_v),
                )
            ):
                piece = piece.astype(bf16)
                start = (p % 2) * 384 + j * 128
                gp_out[p // 2][here, start : start + 128] = piece
                start += (p // 2) * PW
                ba_sum[:, start : start + 128] += fold_rows(piece.astype(f32))
    for g in range(quads):
        da_sum[g][0:PW, :] += tn(gp_out[g][...], normed[...])
        da_sum[g][PW:, :] += tn(att[:, cut(g, QW)], branch[...])

    @pl.when(step == tiles - 1)
    def _():
        for out, da in zip(da_out, da_sum):
            out[...] = da[...].astype(bf16)


def input_kernel(x, gm, gain, *refs):
    gp, wa = refs[0:4], refs[4:8]
    out, sums = refs[-2:]

    @pl.when(pl.program_id(0) == 0)
    def _():
        sums[...] = jnp.zeros_like(sums)

    grad = nt(gp[0][...], wa[0][...])
    for g in range(1, QUADS):
        grad = grad + nt(gp[g][...], wa[g][...])
    xhat, inverse = centre(x[...].astype(f32))
    out[...] = gm[...] + norm_back(xhat, inverse, grad, gain[...])
    sums[0:8, :] += fold_rows(grad * xhat)
    sums[8:16, :] += fold_rows(grad)


def rows_spec(rows, columns, at=0, start=0):
    return pl.BlockSpec((rows, columns), lambda i, *_: (i + start, at))


def back_spec(rows, columns, tiles, at=0):
    return pl.BlockSpec((rows, columns), lambda i, *_: (tiles - 1 - i, at))


def whole_spec(shape, at=0):
    last = len(shape) - 1
    return pl.BlockSpec(
        shape, lambda i, *_: (0,) * last + (at,), pipeline_mode=pl.Buffered(1)
    )


def part_spec(shape, at):
    return pl.BlockSpec(shape, lambda i, *_: (at, 0), pipeline_mode=pl.Buffered(1))


def sum_spec(shape):
    return pl.BlockSpec(shape, lambda i, *_: (0,) * len(shape))


def call(kernel, name, scalars, tiles, ins, outs, scratch, flops, moved, aliases=None):
    return pl.pallas_call(
        kernel,
        grid_spec=pltpu.PrefetchScalarGridSpec(
            num_scalar_prefetch=len(scalars),
            grid=(tiles,),
            in_specs=[spec for _, spec in ins],
            out_specs=[spec for _, spec in outs],
            scratch_shapes=list(scratch),
        ),
        out_shape=[shape for shape, _ in outs],
        compiler_params=pltpu.CompilerParams(vmem_limit_bytes=VMEM),
        cost_estimate=pl.CostEstimate(flops=flops, bytes_accessed=moved, transcendentals=0),
        input_output_aliases=aliases or {},
        name=name,
    )(*scalars, *[array for array, _ in ins])


def tie(*values):
    return lax.optimization_barrier(list(values))


def swap(value, axis, bit):
    size = lax.axis_size(axis)
    return lax.ppermute(value, axis, [(i, i ^ bit) for i in range(size)])


def bits_of(size):
    bit, bits = 1, []
    while bit < size:
        bits.append(bit)
        bit *= 2
    return bits


def gather_shards(own):
    size = lax.axis_size("head")
    held = {0: own}
    for bit in reversed(bits_of(size)):
        for k in list(held):
            held[k ^ bit] = swap(held[k], "head", bit)
    return [held[k] for k in range(size)]


def half_of(value, which, axis):
    size = value.shape[axis] // 2
    return lax.dynamic_slice_in_dim(value, which * size, size, axis)


def regroup(parts, count, axis):
    if len(parts) == count:
        return list(parts)
    whole = jnp.concatenate(parts, axis=axis)
    width = whole.shape[axis] // count
    return [
        lax.slice_in_dim(whole, k * width, (k + 1) * width, axis=axis) for k in range(count)
    ]


def swap_state(mine, weights):
    size = lax.axis_size("head")
    sent = mine.astype(bf16)
    total = None
    for j in range(1, size):
        got = swap(sent, "head", j)
        slots = jnp.split(got, size, axis=1)
        got = jnp.concatenate([slots[k ^ j] for k in range(size)], axis=1).astype(f32)
        got = got * weights[j]
        total = got if total is None else total + got
    return total


def scatter_head(parts):
    held = dict(enumerate(parts))
    for bit in bits_of(len(parts)):
        for k in [k for k in held if k & bit]:
            got = swap(held.pop(k).astype(bf16), "head", bit)
            held[k ^ bit] = held[k ^ bit].astype(f32) + got.astype(f32)
    return held[0]


class Stages:
    def __init__(self, generator):
        self.generator, self.got = generator, None

    def advance(self):
        sent, self.got = self.generator.send(self.got)
        return sent

    def finish(self):
        while self.advance():
            pass
        return self.got


def sum_stages(terms, apart=False):
    size = lax.axis_size("dp")
    me = lax.axis_index("dp")
    x, z, depth = me % 2, me // 2, size // 2

    def half(which):
        total = None
        for term in terms:
            part = half_of(term, which, 0).astype(f32)
            total = part if total is None else total + part
        return total.astype(bf16)

    sent, kept = tie(half(1 - x), half(x))
    (got,) = yield [sent, kept], [swap(sent, "dp", 1)]
    mine = (kept.astype(f32) + got.astype(f32)).astype(bf16)
    rows = mine.shape[0] // depth
    own = lax.dynamic_slice_in_dim(mine, z * rows, rows, 0)
    sent = [
        lax.dynamic_slice_in_dim(mine, (z ^ j) * rows, rows, 0) for j in range(1, depth)
    ]
    own, *sent = tie(own, *sent)
    got = yield [own] + sent, [swap(part, "dp", 2 * j) for j, part in enumerate(sent, 1)]
    total = own.astype(f32)
    for part in got:
        total = total + part.astype(f32)
    (own,) = tie(total.astype(bf16))
    got = yield [own], [swap(own, "dp", 2 * j) for j in range(1, depth)]
    if apart:
        parts = [own] + list(got)
        got = yield parts, [swap(part, "dp", 1) for part in parts]
        mine, other = jnp.concatenate(parts, axis=0), jnp.concatenate(list(got), axis=0)
    else:
        (mine,) = tie(jnp.concatenate([own] + list(got), axis=0))
        (other,) = yield [mine], [swap(mine, "dp", 1)]

    yield [], [mine, other]


def whole_sum(stages):
    mine, other = stages.finish()
    me = lax.axis_index("dp")
    x, z, depth = me % 2, me // 2, lax.axis_size("dp") // 2
    rows = mine.shape[0] // depth

    def natural(value):
        for bit in bits_of(depth):
            shaped = value.reshape(depth // (2 * bit), 2, bit * rows, value.shape[1])
            turned = jnp.flip(shaped, axis=1)
            value = jnp.where((z & bit) != 0, turned, shaped).reshape(value.shape)
        return value

    mine, other = natural(mine), natural(other)
    pair = [jnp.where(x == 0, mine, other), jnp.where(x == 0, other, mine)]
    return jnp.concatenate(pair, axis=0).astype(f32)


def place_kernel(depth, half, where, *refs):
    sources, out = refs[0:4], refs[4]
    step = pl.program_id(0)
    for unit in range(2):
        for side in range(2):

            @pl.when(jnp.logical_and(step // depth == unit, where[0] == side))
            def _(unit=unit, side=side):
                part = sources[2 * unit + (side ^ half)][...].astype(f32)
                out[...] = part if half else part.T


class Window:
    def __init__(self, *after):
        self.after, self.sent, self.got, self.chains = after, [], [], []

    def swap(self, value, axis, bit):
        value = tie(value, *self.after)[0]
        self.sent.append(value)
        self.got.append(swap(value, axis, bit))
        return Later(self, len(self.got) - 1)

    def step(self, chain):
        self.sent += chain.advance()
        self.chains.append((chain, len(self.got)))
        self.got += chain.got

    def open(self, *values):
        return tie(*values, *self.sent)[: len(values)]

    def close(self, *values):
        tied = tie(*values, *self.got)
        self.got = tied[len(values) :]
        for chain, start in self.chains:
            chain.got = self.got[start : start + len(chain.got)]
        return tied[: len(values)]


class Later:
    def __init__(self, window, place):
        self.window, self.place = window, place

    def get(self):
        return self.window.got[self.place]


def small_stages(shared, split):
    size = len(split)
    held = dict(enumerate(split))
    flat = shared.reshape(-1)
    for bit in bits_of(size):
        gone = [k for k in held if k & bit]
        (sent,) = tie(jnp.concatenate([flat] + [held[k] for k in gone]))
        (got,) = yield [sent], [swap(sent, "head", bit)]
        at = flat.shape[0]
        flat = flat + got[:at]
        for k in gone:
            width = held[k].shape[0]
            held[k ^ bit] = held[k ^ bit] + got[at : at + width]
            del held[k]
            at += width
    both = jnp.concatenate([flat, held[0]])
    for bit in bits_of(lax.axis_size("dp")):
        (both,) = tie(both)
        (got,) = yield [both], [swap(both, "dp", bit)]
        both = both + got
    yield [], [both[: flat.shape[0]].reshape(shared.shape), both[flat.shape[0] :]]


def on_device(
    layer_input,
    cotangent,
    crop_blocks,
    crop_padding,
    first_gain,
    first_shift,
    attend_weight,
    attend_bias,
    output_weight,
    output_bias,
    second_gain,
    second_shift,
    expand_weight,
    expand_bias,
    reduce_weight,
    reduce_bias,
):
    R = layer_input.shape[0]
    n = lax.axis_size("head")
    me = lax.axis_index("head")
    x = lax.axis_index("dp") % 2
    nb = R // STRETCH
    FF = expand_weight.shape[1] * n
    FQ = FF // QUADS
    fast = n == QUADS

    if fast:
        near = swap(attend_weight, "head", 1)
        ba_near = jnp.concatenate([attend_bias, swap(attend_bias, "head", 1)])
        be_near = jnp.concatenate([expand_bias, swap(expand_bias, "head", 1)])
        wa = [attend_weight, near, None, None]
        w = Window()
        wa_far = w.swap(attend_weight, "head", 2)
        bias_far = w.swap(jnp.concatenate([ba_near, be_near]), "head", 2)
        wo_near = w.swap(output_weight, "head", 1)
        we_near = w.swap(expand_weight, "head", 1)
        wr_near = w.swap(reduce_weight, "head", 1)
    else:
        wa = regroup(gather_shards(attend_weight), QUADS, 1)
        ba_near, ba_far = jnp.split(jnp.concatenate(gather_shards(attend_bias)), 2)

    sizes, pads = crop_blocks[0], crop_padding[0]
    crops = sizes.shape[0]
    closing = jnp.sum(jnp.tril(jnp.ones((crops, crops), jnp.int32)) * sizes[None, :], axis=1)

    def crop_of(position):
        return jnp.sum((position[..., None] >= closing).astype(jnp.int32), axis=-1)

    spots = me * nb + jnp.arange(nb, dtype=jnp.int32)
    crop = crop_of(spots)
    belongs = crop[:, None] == jnp.arange(crops, dtype=jnp.int32)[None, :]
    opening = jnp.sum(jnp.where(belongs, (closing - sizes)[None, :], 0), axis=1)
    padding = jnp.sum(jnp.where(belongs, pads[None, :], 0), axis=1)
    thr = jnp.maximum(padding - (spots - opening) * STRETCH, 0).astype(jnp.int32)
    first = (crop == crop[0]).astype(jnp.int32)
    one = jnp.ones((1,), jnp.int32)
    cont = jnp.concatenate([one, (crop[1:] == crop[:-1]).astype(jnp.int32), one])
    others = me ^ jnp.arange(n, dtype=jnp.int32)
    opens = crop_of(others * nb)
    closes = crop_of(others * nb + nb - 1)
    before = jnp.logical_and(others < me, closes == crop[0]).astype(f32)
    after = jnp.logical_and(others > me, opens == crop[nb - 1]).astype(f32)

    blocks = 2 if nb % 2 == 0 else 1
    rows = blocks * STRETCH
    tiles = R // rows
    gain1, shift1 = first_gain[None, :], first_shift[None, :]
    gain2, shift2 = second_gain[None, :], second_shift[None, :]
    like = jax.ShapeDtypeStruct
    HALF = D // 2
    full, side = rows_spec(rows, D), rows_spec(rows, HALF)
    low, wide = (like((R, D), bf16), full), (like((R, D), f32), full)
    narrow = (like((R, HALF), bf16), side)
    vec = whole_spec((1, D))
    state_rows = DH + 8

    def vector(value):
        return (value, vec)

    def project(source, pick, bias, fresh):
        ins = [(source, full)]
        if fresh:
            ins += [vector(gain1), vector(shift1)]
        ins += [(wa[k], whole_spec((D, PW))) for k in pick]
        ins += [(bias, whole_spec((1, 2 * PW)))]
        outs = [narrow] * 3 + ([low] if fresh else [])
        outs += [
            (like((state_rows, HALF), f32), sum_spec((state_rows, HALF))),
            (like((nb * DH, HALF), f32), rows_spec(blocks * DH, HALF)),
            (like((nb * 8, HALF), f32), rows_spec(blocks * 8, HALF)),
        ]
        return call(
            functools.partial(qkv_kernel, blocks, fresh),
            "qkv",
            (thr, cont),
            tiles,
            ins,
            outs,
            [pltpu.VMEM((DH, HALF), f32), pltpu.VMEM((8, HALF), f32)],
            3 * R * D * D,
            8 * R * D + 3 * D * D,
        )

    bias = ba_near[None, :]
    source = layer_input
    if fast:
        source, bias = w.open(source, bias)
    q01, k01, v01, normed, trail01, st01, kt01 = project(source, (0, 1), bias, True)
    if fast:
        q01, k01, v01, normed, trail01 = w.close(q01, k01, v01, normed, trail01)
        wa[2] = wa_far.get()
        wa[3] = swap(wa[2], "head", 1)
        ba_far, be_far = bias_far.get()[: ba_near.shape[0]], bias_far.get()[ba_near.shape[0] :]
        be_slots = jnp.split(jnp.concatenate([be_near, be_far]), QUADS)
        wo = [output_weight, wo_near.get(), None, None]
        w = Window(trail01)
        wo_far = w.swap(output_weight, "head", 2)
        normed, wa[3] = w.open(normed, wa[3])
    else:
        wo = regroup(gather_shards(output_weight), QUADS, 0)
        we = regroup(gather_shards(expand_weight), QUADS, 1)
        wr = regroup(gather_shards(reduce_weight), QUADS, 0)
        be_slots = jnp.split(jnp.concatenate(gather_shards(expand_bias)), QUADS)
    q23, k23, v23, trail23, st23, kt23 = project(normed, (2, 3), ba_far[None, :], False)
    if fast:
        q23, k23, v23, trail23 = w.close(q23, k23, v23, trail23)
        wo[2] = wo_far.get()
        wo[3] = swap(wo[2], "head", 1)
    s_in = swap_state(jnp.concatenate([trail01, trail23], axis=1), before)
    if fast:
        w = Window(s_in)
        wr_far = w.swap(reduce_weight, "head", 2)
        (s_in,) = w.open(s_in)

    att, rec, st, kt, middle, n2 = call(
        functools.partial(attend_kernel, blocks),
        "attend",
        (first, thr),
        tiles,
        [
            (a, spec)
            for part in ((q01, k01, v01, st01, kt01), (q23, k23, v23, st23, kt23))
            for a, spec in zip(
                part,
                [side] * 3 + [rows_spec(blocks * DH, HALF), rows_spec(blocks * 8, HALF)],
            )
        ]
        + [
            (layer_input, full),
            (s_in, whole_spec((state_rows, D))),
            vector(output_bias[None, :]),
            vector(gain2),
            vector(shift2),
        ]
        + [(w, whole_spec((QW, D))) for w in wo],
        [
            low,
            wide,
            (like((nb * DH, D), bf16), rows_spec(blocks * DH, D)),
            (like((nb * 8, D), f32), rows_spec(blocks * 8, D)),
            wide,
            low,
        ],
        [],
        12 * R * D * D,
        20 * R * D,
    )

    if fast:
        att, rec, st, kt, middle, n2 = w.close(att, rec, st, kt, middle, n2)
        we = [expand_weight, we_near.get(), None, None]
        wr = [reduce_weight, wr_near.get(), wr_far.get(), None]

    def ffn(picks, part, extra):
        widths = [FQ if half is None else FQ // 2 for _, half in picks]
        spots = [(k, width, half or 0) for (k, half), width in zip(picks, widths)]
        ins = [(n2, full), (cotangent, full)]
        ins += [(be_slots[k][None, :], whole_spec((1, width), at)) for k, width, at in spots]
        if part is not None:
            ins += [(part[0], full), (part[1], full)]
        ins += [(we[k], whole_spec((D, width), at)) for k, width, at in spots]
        ins += [(wr[k], part_spec((width, D), at)) for k, width, at in spots]
        outs = [(like((2 * w, D), bf16), whole_spec((2 * w, D))) for w in widths]
        outs += [(like((8, w), f32), sum_spec((8, w))) for w in widths]
        if extra is None:
            outs += [wide, wide]
        else:
            ins += extra
            outs += [low, wide, low, low, low]
            outs += [
                (like((state_rows, D), f32), sum_spec((state_rows, D))),
                (like((nb * DH, D), f32), rows_spec(blocks * DH, D)),
                (like((nb * 8, D), f32), rows_spec(blocks * 8, D)),
                (like((32, D), f32), sum_spec((32, D))),
            ]
        results = call(
            functools.partial(ffn_kernel, blocks, widths, part is None, extra is not None),
            "ffn",
            (first,) if extra is not None else (),
            tiles,
            ins,
            outs,
            [pltpu.VMEM((2 * w, D), f32) for w in widths],
            12 * R * D * sum(widths),
            20 * R * D,
        )
        for i, (k, half) in enumerate(picks):
            eb[k].append(results[len(picks) + i])
        return list(results[: len(picks)]), list(results[2 * len(picks) :])

    eb = [[], [], [], []]
    extra = [
        (middle, full),
        (att, full),
        (rec, full),
        (q01, side),
        (q23, side),
        vector(gain2),
        vector(reduce_bias[None, :]),
    ] + [(w, whole_spec((QW, D))) for w in wo]
    def total(*terms):
        return sum(term.astype(f32) for term in terms).astype(bf16)

    if fast:
        w = Window(n2)
        we_far = w.swap(expand_weight, "head", 2)
        wr_last = w.swap(wr[2], "head", 1)
        (n2,) = w.open(n2)
        (near, own), part = ffn([(1, 0), (0, 0)], None, None)
        n2, near, own, *part = w.close(n2, near, own, *part)
        we[2], wr[3] = we_far.get(), wr_last.get()
        we[3] = swap(we[2], "head", 1)
        w = Window(part[0])
        near = w.swap(near, "head", 1)
        (part[0],) = w.open(part[0])
        (last_far, far), part = ffn([(3, 0), (2, 0)], part, None)
        last_far, far, *part = w.close(last_far, far, *part)
        far = total(far, swap(last_far, "head", 1))
        near_a = near.get()
        w = Window(part[0])
        far = w.swap(far, "head", 2)
        (part[0],) = w.open(part[0])
        (last_far, far_b), part = ffn([(3, 1), (2, 1)], part, None)
        last_far, far_b, *part = w.close(last_far, far_b, *part)
        sum_a = Stages(sum_stages([own, near_a, far.get()]))
        far = total(far_b, swap(last_far, "head", 1))
        w = Window(part[0])
        w.step(sum_a)
        far, part[0] = w.open(far, part[0])
        (near,), part = ffn([(1, 1)], part, None)
        near, *part = w.close(near, *part)
        w = Window(part[0])
        far = w.swap(far, "head", 2)
        near = w.swap(near, "head", 1)
        w.step(sum_a)
        (part[0],) = w.open(part[0])
        (own,), results = ffn([(0, 1)], part, extra)
        own, *results = w.close(own, *results)
        far, near = far.get(), near.get()
    else:
        grads, part = [None] * 4, None
        for k in (3, 2, 1):
            (grads[k],), part = ffn([(k, None)], part, None)
        (grads[0],), results = ffn([(0, None)], part, extra)
    layer_output, grad_middle, branch, gn, t, leading, pr, kr, sums2 = results

    def back(pick, q, k, v, state):
        count = len(pick)
        at, inner, width = pick[0] // count, (pick[0] % 2) // count, count * QW
        return call(
            functools.partial(back_kernel, blocks, tiles, count),
            "attend_back",
            (cont,),
            tiles,
            [(a, back_spec(rows, width, tiles, inner)) for a in (q, k, v)]
            + [(a, back_spec(rows, width, tiles, at)) for a in (gn, t)]
            + [
                (st, back_spec(blocks * DH, width, tiles, at)),
                (kt, back_spec(blocks * 8, width, tiles, at)),
                (pr, back_spec(blocks * DH, width, tiles, at)),
                (kr, back_spec(blocks * 8, width, tiles, at)),
                (state, whole_spec((state_rows, width), at)),
                (normed, back_spec(rows, D, tiles)),
                (att, back_spec(rows, width, tiles, at)),
                (branch, back_spec(rows, D, tiles)),
            ],
            [(like((R, PW), bf16), back_spec(rows, PW, tiles))] * count
            + [(like((PW + QW, D), bf16), whole_spec((PW + QW, D)))] * count
            + [(like((8, count * PW), f32), sum_spec((8, count * PW)))],
            [pltpu.VMEM((DH, width), f32), pltpu.VMEM((8, width), f32)]
            + [pltpu.VMEM((PW + QW, D), f32)] * count,
            6 * count * R * D * D,
            5 * count * R * D,
        )

    def inputs(start, count, out, x_in):
        at = rows_spec(rows, D, 0, start)
        ins = [(x_in, at), (grad_middle, at), vector(gain1)]
        ins += [(g, rows_spec(rows, PW, 0, start)) for g in gp]
        ins += [(w, whole_spec((D, PW))) for w in wa]
        if out is not None:
            ins += [(out, pl.BlockSpec(memory_space=pl.ANY))]
        return call(
            input_kernel,
            "input_grad",
            (),
            count,
            ins,
            [(wide[0], at), (like((16, D), f32), sum_spec((16, D)))],
            [],
            6 * rows * count * D * D,
            16 * rows * count * D,
            None if out is None else {len(ins) - 1: 0},
        )

    gp = [None] * 4
    if fast:
        g_in = swap_state(leading, after)
        sum_b = Stages(sum_stages([own, near, far]))
        w = Window(g_in)
        w.step(sum_b)
        w.step(sum_a)
        (g_in,) = w.open(g_in)
        gp[2], gp[3], da2, da3, ba23 = back((2, 3), q23, k23, v23, g_in)
        gp[2], gp[3], da2, da3, ba23, g_in = w.close(gp[2], gp[3], da2, da3, ba23, g_in)

        far = total(da2, swap(da3, "head", 1))
        w = Window(g_in)
        far = w.swap(far, "head", 2)
        w.step(sum_b)
        w.step(sum_a)
        (g_in,) = w.open(g_in)
        gp[0], gp[1], da0, da1, ba01 = back((0, 1), q01, k01, v01, g_in)
        gp[0], gp[1], da0, da1, ba01 = w.close(gp[0], gp[1], da0, da1, ba01)
        near = swap(da1, "head", 1)
        sum_c = Stages(sum_stages([da0, near, far.get()], True))
        w = Window(gp[0])
        w.step(sum_c)
        w.step(sum_b)
        half = tiles // 2
        (layer_in,) = w.open(layer_input)
        input_grad, sums1 = inputs(0, half, None, layer_in)
        input_grad, sums1 = w.close(input_grad, sums1)
        w = Window(input_grad)
        w.step(sum_c)
        w.step(sum_b)
        (input_grad,) = w.open(input_grad)
        input_grad, more = inputs(half, tiles - half, input_grad, layer_in)
        input_grad, more = w.close(input_grad, more)
        sums1 = sums1 + more
        where = lax.axis_index("dp")
        where = jnp.stack([where % 2, where // 2]).astype(jnp.int32)
        depth = lax.axis_size("dp") // 2
        piece = FQ // 2 // depth

        def source(unit):
            def index(i, where):
                at = jnp.where(i // depth == unit, i % depth, 0 if unit else depth - 1)
                return (at ^ where[1], 0)

            return pl.BlockSpec((piece, D), index)

        ins = [(v, source(0)) for v in sum_a.finish()] + [(v, source(1)) for v in sum_b.finish()]

        def placed(half, shape, block, index):
            w = Window(input_grad)
            w.step(sum_c)
            (at,) = w.open(where)
            out = call(
                functools.partial(place_kernel, depth, half),
                "place",
                (at,),
                2 * depth,
                ins,
                [(like(shape, f32), pl.BlockSpec(block, index))],
                [],
                0,
                6 * FQ * D,
            )
            return w.close(*out)[0]

        expand_weight_grad = placed(0, (D, FQ), (D, piece), lambda i, *_: (0, i))
        sums1 = tie(sums1, expand_weight_grad)[0]
        eb = [list(tie(*parts, sums1)[: len(parts)]) for parts in eb]
        reduce_weight_grad = placed(1, (FQ, D), (piece, D), lambda i, *_: (i, 0))
        sum_c = whole_sum(sum_c)
        attend_weight_grad, output_weight_grad = sum_c[:PW].T, sum_c[PW:]
    else:
        g_in = swap_state(leading, after)
        gp[2], gp[3], *da23, ba23 = back((2, 3), q23, k23, v23, g_in)
        gp[0], gp[1], *da01, ba01 = back((0, 1), q01, k01, v01, g_in)
        da = da01 + da23

        def reduce(parts):
            return whole_sum(Stages(sum_stages([scatter_head(regroup(parts, n, 0))])))

        expand_weight_grad = reduce([g[:FQ] for g in grads]).T
        reduce_weight_grad = reduce([g[FQ:] for g in grads])
        attend_weight_grad = reduce([g[:PW] for g in da]).T
        output_weight_grad = reduce([g[PW:] for g in da])
        input_grad, sums1 = inputs(0, tiles, None, layer_input)

    eb = [jnp.sum(jnp.concatenate(parts, axis=1), axis=0) for parts in eb]
    eb = regroup(eb, n, 0)
    ab = regroup([jnp.sum(jnp.concatenate([ba01, ba23], axis=1), axis=0)], n, 0)
    shared = jnp.concatenate(
        [
            jnp.sum(sums1.reshape(2, 8, D), axis=1),
            jnp.sum(sums2.reshape(4, 8, D), axis=1),
        ]
    )
    split = [jnp.concatenate(both) for both in zip(eb, ab)]
    shared, split = Stages(small_stages(shared, split)).finish()
    shared1, shared2 = shared[:2], shared[2:]
    expand_bias_grad, attend_bias_grad = split[: eb[0].shape[0]], split[eb[0].shape[0] :]
    return (
        layer_output,
        input_grad,
        shared1[0],
        shared1[1],
        attend_weight_grad,
        attend_bias_grad,
        output_weight_grad,
        shared2[0],
        shared2[1],
        shared2[2],
        expand_weight_grad,
        expand_bias_grad,
        reduce_weight_grad,
        shared2[3],
    )


def solution(mesh):
    in_specs = (
        P(("dp", "head"), None),
        P(("dp", "head"), None),
        P("dp", None),
        P("dp", None),
        P(),
        P(),
        P(None, "head"),
        P("head"),
        P("head", None),
        P(),
        P(),
        P(),
        P(None, "head"),
        P("head"),
        P("head", None),
        P(),
    )
    out_specs = (
        P(("dp", "head"), None),
        P(("dp", "head"), None),
        P(),
        P(),
        P(None, "head"),
        P("head"),
        P("head", None),
        P(),
        P(),
        P(),
        P(None, "head"),
        P("head"),
        P("head", None),
        P(),
    )
    return jax.shard_map(
        on_device, mesh=mesh, in_specs=in_specs, out_specs=out_specs, check_vma=False
    )
```

```python
import functools

import jax
import jax.numpy as jnp
from jax import lax
from jax.experimental import pallas as pl
from jax.experimental.pallas import tpu as pltpu
from jax.sharding import PartitionSpec as P

DH = 64
STRETCH = 128
D = 1024
QUADS = 4
QW = D // QUADS
PW = 3 * QW
EPS = 1e-05
VMEM = 60 * 1024 * 1024

f32 = jnp.float32
bf16 = jnp.bfloat16


def nn(a, b):
    return lax.dot_general(a, b, (((1,), (0,)), ((), ())), preferred_element_type=f32)


def nt(a, b):
    return lax.dot_general(a, b, (((1,), (1,)), ((), ())), preferred_element_type=f32)


def tn(a, b):
    return lax.dot_general(a, b, (((0,), (0,)), ((), ())), preferred_element_type=f32)


PAIR = 2 * DH


def side_rows(kind):
    lane = lax.broadcasted_iota(jnp.int32, (1, PAIR), 1) // DH
    return [(lane == h).astype(kind) for h in range(2)]


def spread(block, picks):
    return jnp.concatenate([block * picks[0], block * picks[1]], axis=0)


def pair_product(left, right, picks):
    square = tn(left, right)
    return square[0:DH] * picks[0] + square[DH:PAIR] * picks[1]


def cut(start, width=PAIR):
    return slice(start * width, (start + 1) * width)


def centre(values):
    average = jnp.mean(values, axis=-1, keepdims=True)
    centred = values - average
    spread = jnp.mean(centred * centred, axis=-1, keepdims=True)
    inverse = lax.rsqrt(spread + EPS)
    return centred * inverse, inverse


def norm_back(xhat, inverse, grad, gain):
    w = grad * gain
    return inverse * (
        w
        - jnp.mean(w, axis=-1, keepdims=True)
        - xhat * jnp.mean(w * xhat, axis=-1, keepdims=True)
    )


def fold_rows(values):
    rows, columns = values.shape
    return jnp.sum(values.reshape(rows // 8, 8, columns), axis=0)


def normal_parts(v):
    size = jnp.abs(v) * 0.7071067811865476
    t = 1.0 / (1.0 + 0.3275911 * size)
    bell = jnp.exp(-0.5 * v * v)
    poly = t * (
        0.254829592
        + t * (-0.284496736 + t * (1.421413741 + t * (-1.453152027 + t * 1.061405429)))
    )
    tail = 0.5 * poly * bell
    return jnp.where(v < 0, tail, 1.0 - tail), bell


def qkv_kernel(blocks, fresh, thr, cont, *refs):
    if fresh:
        x, gain, shift, n_out = refs[0], refs[1], refs[2], refs[9]
        wa, ba = refs[3:5], refs[5]
        q_out, k_out, v_out = refs[6:9]
        t_out, st_out, kt_out, state, sums = refs[10:15]
    else:
        n_in = refs[0]
        wa, ba = refs[1:3], refs[3]
        q_out, k_out, v_out = refs[4:7]
        t_out, st_out, kt_out, state, sums = refs[7:12]
    step = pl.program_id(0)
    rows = blocks * STRETCH

    @pl.when(step == 0)
    def _():
        state[...] = jnp.zeros_like(state)
        sums[...] = jnp.zeros_like(sums)

    if fresh:
        xhat, _ = centre(x[...].astype(f32))
        normed = (xhat * gain[...] + shift[...]).astype(bf16)
        n_out[...] = normed
    else:
        normed = n_in[...]
    place = lax.broadcasted_iota(jnp.int32, (STRETCH, 128), 0)
    valid = jnp.concatenate(
        [(place >= thr[step * blocks + b]).astype(f32) for b in range(blocks)], axis=0
    )
    low = lax.broadcasted_iota(jnp.int32, (rows, 128), 1) < DH

    def feature(values):
        return jnp.where(values > 0, values + 1.0, jnp.exp(jnp.minimum(values, 0.0)))

    for g in range(2):
        project = nn(normed, wa[g][...]) + ba[:, g * PW : (g + 1) * PW]
        for pair in range(2):
            c0, c1, c2 = (
                project[:, pair * 384 + j * 128 : pair * 384 + (j + 1) * 128] for j in range(3)
            )
            at = slice(g * QW + pair * 128, g * QW + (pair + 1) * 128)
            q_out[:, at] = feature(jnp.where(low, c0, c1)).astype(bf16)
            key = pltpu.roll(jnp.where(low, c2, c0), DH, 1)
            k_out[:, at] = (valid * feature(key)).astype(bf16)
            v_out[:, at] = jnp.where(low, c1, c2).astype(bf16)
    picks = side_rows(f32)
    for b in range(blocks):
        keep = cont[step * blocks + b].astype(f32)
        here = cut(b, STRETCH)
        state[...] = state[...] * keep
        sums[...] = sums[...] * keep
        st_out[cut(b, DH), :] = state[...]
        kt_out[cut(b, 8), :] = sums[...]
        for p in range(4):
            key = k_out[here, cut(p)]
            state[:, cut(p)] += pair_product(key, v_out[here, cut(p)], picks)
            sums[:, cut(p)] += fold_rows(key.astype(f32))

    @pl.when(step == pl.num_programs(0) - 1)
    def _():
        t_out[0:DH, :] = state[...]
        t_out[DH : DH + 8, :] = sums[...]


def attend_kernel(blocks, first, thr, *refs):
    qkv = refs[0:5], refs[5:10]
    x, s_in, bo, gain, shift = refs[10:15]
    wo = refs[15:19]
    att_out, rec_out, st_out, kt_out, mid_out, n_out = refs[19:25]
    step = pl.program_id(0)
    picks = side_rows(bf16)
    row = lax.broadcasted_iota(jnp.int32, (STRETCH, 2 * STRETCH), 0)
    lane = lax.broadcasted_iota(jnp.int32, (STRETCH, 2 * STRETCH), 1) % STRETCH
    lower = lane <= row
    ones_scores = spread(jnp.ones((STRETCH, PAIR), bf16), picks)
    ones_state = spread(jnp.ones((DH, PAIR), bf16), picks)
    zeros = jnp.zeros((PAIR, PAIR), bf16)
    ones = jnp.concatenate([ones_scores, zeros, ones_state], axis=0)
    came = jnp.sum(s_in[DH : DH + 8], axis=0, keepdims=True)
    for b in range(blocks):
        joins = first[step * blocks + b].astype(f32)
        here = cut(b, STRETCH)
        for p in range(8):
            at, own = cut(p), cut(p % 4)
            q, k, v, st, kt = qkv[p // 4]
            qb, kb, vb = q[here, own], k[here, own], v[here, own]
            state = (st[cut(b, DH), own] + joins * s_in[0:DH, at]).astype(bf16)
            total = jnp.sum(kt[cut(b, 8), own], axis=0, keepdims=True) + joins * came[:, at]
            st_out[cut(b, DH), at] = state
            kt_out[cut(b, 8), at] = jnp.broadcast_to(total, (8, PAIR))
            scores = nt(qb, spread(kb, picks))
            scores = jnp.where(lower, scores, 0.0).astype(bf16)
            weighted = (qb.astype(f32) * total).astype(bf16)
            left = jnp.concatenate([scores, qb, weighted], axis=1)
            right = jnp.concatenate([spread(vb, picks), spread(state, picks), zeros], axis=0)
            both = nn(left, jnp.concatenate([right, ones], axis=1))
            rec = 1.0 / jnp.maximum(both[:, PAIR:], 1.0)
            rec_out[here, at] = rec
            att_out[here, at] = (both[:, :PAIR] * rec).astype(bf16)
    place = lax.broadcasted_iota(jnp.int32, (STRETCH, D), 0)
    for b in range(blocks):
        here = slice(b * STRETCH, (b + 1) * STRETCH)

        @pl.when(thr[step * blocks + b] > 0)
        def _(b=b, here=here):
            valid = (place >= thr[step * blocks + b]).astype(f32)
            rec_out[here, :] = rec_out[here, :] * valid
            att_out[here, :] = (att_out[here, :].astype(f32) * valid).astype(bf16)

    middle = x[...].astype(f32) + bo[...]
    for g in range(QUADS):
        middle = middle + nn(att_out[:, g * QW : (g + 1) * QW], wo[g][...])
    mid_out[...] = middle
    xhat, _ = centre(middle)
    n_out[...] = (xhat * gain[...] + shift[...]).astype(bf16)


def ffn_kernel(blocks, widths, fresh, final, *refs):
    refs = list(refs)

    def take(count):
        taken = refs[:count]
        del refs[:count]
        return taken

    count = len(widths)
    if final:
        (first,) = take(1)
    n2, cot = take(2)
    be = take(count)
    if not fresh:
        part_out, part_grad = take(2)
    we, wr = take(count), take(count)
    if final:
        mid, att, rec, q01, q23, gain, br = take(7)
        wo = take(4)
    grad_out, be_sum = take(count), take(count)
    if final:
        out, gm_out, gb_out, gn_out, t_out, l_out, pr_out, kr_out, sums = take(9)
    else:
        next_out, next_grad = take(2)
    grad_sum = take(count)
    step = pl.program_id(0)

    @pl.when(step == 0)
    def _():
        for total in grad_sum + be_sum:
            total[...] = jnp.zeros_like(total)
        if final:
            l_out[...] = jnp.zeros_like(l_out)
            sums[...] = jnp.zeros_like(sums)

    normed = n2[...]
    cotangent = cot[...]
    reduced = None if fresh else part_out[...]
    grad = None if fresh else part_grad[...]
    for i, width in enumerate(widths):
        hidden = nn(normed, we[i][...]) + be[i][...]
        grad_act = nt(cotangent, wr[i][...])
        phi, bell = normal_parts(hidden)
        active = (hidden * phi).astype(bf16)
        back = (grad_act * (phi + hidden * (0.3989422804014327 * bell))).astype(bf16)
        be_sum[i][...] += fold_rows(back.astype(f32))
        grad_sum[i][0:width, :] += tn(back, normed)
        grad_sum[i][width : 2 * width, :] += tn(active, cotangent)
        more = nn(active, wr[i][...])
        reduced = more if reduced is None else reduced + more
        more = nt(back, we[i][...])
        grad = more if grad is None else grad + more

    @pl.when(step == pl.num_programs(0) - 1)
    def _():
        for out_ref, total in zip(grad_out, grad_sum):
            out_ref[...] = total[...].astype(bf16)

    if not final:
        next_out[...] = reduced
        next_grad[...] = grad
        return
    middle = mid[...]
    out[...] = (middle + reduced + br[...]).astype(bf16)
    xhat, inverse = centre(middle)
    cot_wide = cotangent.astype(f32)
    grad_middle = cot_wide + norm_back(xhat, inverse, grad, gain[...])
    gm_out[...] = grad_middle
    branch = grad_middle.astype(bf16)
    gb_out[...] = branch
    sums[0:8, :] += fold_rows(branch.astype(f32))
    sums[8:16, :] += fold_rows(grad * xhat)
    sums[16:24, :] += fold_rows(grad)
    sums[24:32, :] += fold_rows(cot_wide)
    for g in range(QUADS):
        at = slice(g * QW, (g + 1) * QW)
        grad_att = nt(branch, wo[g][...]).astype(bf16).astype(f32)
        share = rec[:, at]
        numer = grad_att * share
        gn_out[:, at] = numer.astype(bf16)
        t_out[:, at] = jnp.where(
            share < 1.0, -(numer * att[:, at].astype(f32)), 0.0
        ).astype(bf16)
    picks = side_rows(f32)
    ones = spread(jnp.ones((DH, PAIR), bf16), side_rows(bf16))
    for b in range(blocks):
        here = cut(b, STRETCH)
        for p in range(8):
            at = cut(p)
            query = (q01, q23)[p // 4][here, cut(p % 4)]
            pr_out[cut(b, DH), at] = pair_product(query, gn_out[here, at], picks)
            grad_denom = nn(t_out[here, at], ones)
            kr_out[cut(b, 8), at] = fold_rows(grad_denom * query.astype(f32))

        @pl.when(first[step * blocks + b] == 1)
        def _(b=b):
            l_out[0:DH, :] += pr_out[cut(b, DH), :]
            l_out[DH : DH + 8, :] += kr_out[cut(b, 8), :]


def back_kernel(blocks, tiles, quads, cont, q, k, v, gn, t, st, kt, pr, kr, g_in, normed, att, branch, *refs):
    gp_out, da_out, ba_sum = refs[0:quads], refs[quads : 2 * quads], refs[2 * quads]
    state, total = refs[2 * quads + 1 : 2 * quads + 3]
    da_sum = refs[2 * quads + 3 :]
    step = pl.program_id(0)
    tile = tiles - 1 - step

    @pl.when(step == 0)
    def _():
        state[...] = g_in[0:DH]
        total[...] = jnp.broadcast_to(
            jnp.sum(g_in[DH : DH + 8], axis=0, keepdims=True), total.shape
        )
        ba_sum[...] = jnp.zeros_like(ba_sum)
        for da in da_sum:
            da[...] = jnp.zeros_like(da)

    picks = side_rows(bf16)
    row = lax.broadcasted_iota(jnp.int32, (STRETCH, 2 * STRETCH), 0)
    lane = lax.broadcasted_iota(jnp.int32, (STRETCH, 2 * STRETCH), 1) % STRETCH
    lower = lane <= row
    upper = lane >= row
    low_lane = lax.broadcasted_iota(jnp.int32, (STRETCH, PAIR), 1) < DH
    all_ones = jnp.ones((STRETCH, PAIR), bf16)
    ones_scores = spread(all_ones, picks)
    ones_state = spread(jnp.ones((DH, PAIR), bf16), picks)
    for b in reversed(range(blocks)):
        keep = cont[tile * blocks + b + 1].astype(f32)
        here = cut(b, STRETCH)
        for p in range(2 * quads):
            at = cut(p)
            qb, kb, vb, gb, tb = q[here, at], k[here, at], v[here, at], gn[here, at], t[here, at]
            state_here = state[:, at] * keep
            total_here = total[:, at] * keep
            behind = spread(state_here.astype(bf16), picks)
            state[:, at] = state_here + pr[cut(b, DH), at]
            total[:, at] = total_here + jnp.sum(kr[cut(b, 8), at], axis=0, keepdims=True)
            spread_q, spread_g = spread(qb, picks), spread(gb, picks)
            forward = spread(st[cut(b, DH), at], picks)
            scores = nt(
                jnp.concatenate([gb, tb], axis=1),
                jnp.concatenate([spread(vb, picks), ones_scores], axis=1),
            )
            scores = jnp.where(lower, scores, 0.0).astype(bf16)
            turned = nt(
                jnp.concatenate([vb, all_ones], axis=1),
                jnp.concatenate([spread_g, spread(tb, picks)], axis=1),
            )
            turned = jnp.where(upper, turned, 0.0).astype(bf16)
            mixed = jnp.where(upper, nt(kb, spread_q), 0.0).astype(bf16)
            grad_denom = nn(tb, ones_state)
            grad_q = (
                nn(scores, spread(kb, picks))
                + nt(gb, forward)
                + grad_denom * kt[b * 8 : b * 8 + 1, at]
            )
            grad_k = nn(turned, spread_q) + nt(vb, behind) + total_here[0:1]
            grad_v = nn(jnp.concatenate([mixed, kb], axis=1), jnp.concatenate([spread_g, behind]))
            grad_q = grad_q * jnp.minimum(qb.astype(f32), 1.0)
            grad_k = grad_k * jnp.minimum(kb.astype(f32), 1.0)
            swapped = pltpu.roll(grad_k, DH, 1)
            for j, piece in enumerate(
                (
                    jnp.where(low_lane, grad_q, swapped),
                    jnp.where(low_lane, grad_v, grad_q),
                    jnp.where(low_lane, swapped, grad_v),
                )
            ):
                piece = piece.astype(bf16)
                start = (p % 2) * 384 + j * 128
                gp_out[p // 2][here, start : start + 128] = piece
                start += (p // 2) * PW
                ba_sum[:, start : start + 128] += fold_rows(piece.astype(f32))
    for g in range(quads):
        da_sum[g][0:PW, :] += tn(gp_out[g][...], normed[...])
        da_sum[g][PW:, :] += tn(att[:, cut(g, QW)], branch[...])

    @pl.when(step == tiles - 1)
    def _():
        for out, da in zip(da_out, da_sum):
            out[...] = da[...].astype(bf16)


def input_kernel(x, gm, gain, *refs):
    gp, wa = refs[0:4], refs[4:8]
    out, sums = refs[-2:]

    @pl.when(pl.program_id(0) == 0)
    def _():
        sums[...] = jnp.zeros_like(sums)

    grad = nt(gp[0][...], wa[0][...])
    for g in range(1, QUADS):
        grad = grad + nt(gp[g][...], wa[g][...])
    xhat, inverse = centre(x[...].astype(f32))
    out[...] = gm[...] + norm_back(xhat, inverse, grad, gain[...])
    sums[0:8, :] += fold_rows(grad * xhat)
    sums[8:16, :] += fold_rows(grad)


def rows_spec(rows, columns, at=0, start=0):
    return pl.BlockSpec((rows, columns), lambda i, *_: (i + start, at))


def back_spec(rows, columns, tiles, at=0):
    return pl.BlockSpec((rows, columns), lambda i, *_: (tiles - 1 - i, at))


def whole_spec(shape, at=0):
    last = len(shape) - 1
    return pl.BlockSpec(
        shape, lambda i, *_: (0,) * last + (at,), pipeline_mode=pl.Buffered(1)
    )


def part_spec(shape, at):
    return pl.BlockSpec(shape, lambda i, *_: (at, 0), pipeline_mode=pl.Buffered(1))


def sum_spec(shape):
    return pl.BlockSpec(shape, lambda i, *_: (0,) * len(shape))


def call(kernel, name, scalars, tiles, ins, outs, scratch, flops, moved, aliases=None):
    return pl.pallas_call(
        kernel,
        grid_spec=pltpu.PrefetchScalarGridSpec(
            num_scalar_prefetch=len(scalars),
            grid=(tiles,),
            in_specs=[spec for _, spec in ins],
            out_specs=[spec for _, spec in outs],
            scratch_shapes=list(scratch),
        ),
        out_shape=[shape for shape, _ in outs],
        compiler_params=pltpu.CompilerParams(vmem_limit_bytes=VMEM),
        cost_estimate=pl.CostEstimate(flops=flops, bytes_accessed=moved, transcendentals=0),
        input_output_aliases=aliases or {},
        name=name,
    )(*scalars, *[array for array, _ in ins])


def tie(*values):
    return lax.optimization_barrier(list(values))


def swap(value, axis, bit):
    size = lax.axis_size(axis)
    return lax.ppermute(value, axis, [(i, i ^ bit) for i in range(size)])


def bits_of(size):
    bit, bits = 1, []
    while bit < size:
        bits.append(bit)
        bit *= 2
    return bits


def gather_shards(own):
    size = lax.axis_size("head")
    held = {0: own}
    for bit in reversed(bits_of(size)):
        for k in list(held):
            held[k ^ bit] = swap(held[k], "head", bit)
    return [held[k] for k in range(size)]


def half_of(value, which, axis):
    size = value.shape[axis] // 2
    return lax.dynamic_slice_in_dim(value, which * size, size, axis)


def regroup(parts, count, axis):
    if len(parts) == count:
        return list(parts)
    whole = jnp.concatenate(parts, axis=axis)
    width = whole.shape[axis] // count
    return [
        lax.slice_in_dim(whole, k * width, (k + 1) * width, axis=axis) for k in range(count)
    ]


def swap_state(mine, weights):
    size = lax.axis_size("head")
    sent = mine.astype(bf16)
    total = None
    for j in range(1, size):
        got = swap(sent, "head", j)
        slots = jnp.split(got, size, axis=1)
        got = jnp.concatenate([slots[k ^ j] for k in range(size)], axis=1).astype(f32)
        got = got * weights[j]
        total = got if total is None else total + got
    return total


def scatter_head(parts):
    held = dict(enumerate(parts))
    for bit in bits_of(len(parts)):
        for k in [k for k in held if k & bit]:
            got = swap(held.pop(k).astype(bf16), "head", bit)
            held[k ^ bit] = held[k ^ bit].astype(f32) + got.astype(f32)
    return held[0]


class Stages:
    def __init__(self, generator):
        self.generator, self.got = generator, None

    def advance(self):
        sent, self.got = self.generator.send(self.got)
        return sent

    def finish(self):
        while self.advance():
            pass
        return self.got


def sum_stages(terms, apart=False):
    size = lax.axis_size("dp")
    me = lax.axis_index("dp")
    x, z, depth = me % 2, me // 2, size // 2

    def half(which):
        total = None
        for term in terms:
            part = half_of(term, which, 0).astype(f32)
            total = part if total is None else total + part
        return total.astype(bf16)

    sent, kept = tie(half(1 - x), half(x))
    (got,) = yield [sent, kept], [swap(sent, "dp", 1)]
    mine = (kept.astype(f32) + got.astype(f32)).astype(bf16)
    rows = mine.shape[0] // depth
    own = lax.dynamic_slice_in_dim(mine, z * rows, rows, 0)
    sent = [
        lax.dynamic_slice_in_dim(mine, (z ^ j) * rows, rows, 0) for j in range(1, depth)
    ]
    own, *sent = tie(own, *sent)
    got = yield [own] + sent, [swap(part, "dp", 2 * j) for j, part in enumerate(sent, 1)]
    total = own.astype(f32)
    for part in got:
        total = total + part.astype(f32)
    (own,) = tie(total.astype(bf16))
    got = yield [own], [swap(own, "dp", 2 * j) for j in range(1, depth)]
    if apart:
        parts = [own] + list(got)
        got = yield parts, [swap(part, "dp", 1) for part in parts]
        mine, other = jnp.concatenate(parts, axis=0), jnp.concatenate(list(got), axis=0)
    else:
        (mine,) = tie(jnp.concatenate([own] + list(got), axis=0))
        (other,) = yield [mine], [swap(mine, "dp", 1)]

    yield [], [mine, other]


def whole_sum(stages):
    mine, other = stages.finish()
    me = lax.axis_index("dp")
    x, z, depth = me % 2, me // 2, lax.axis_size("dp") // 2
    rows = mine.shape[0] // depth

    def natural(value):
        for bit in bits_of(depth):
            shaped = value.reshape(depth // (2 * bit), 2, bit * rows, value.shape[1])
            turned = jnp.flip(shaped, axis=1)
            value = jnp.where((z & bit) != 0, turned, shaped).reshape(value.shape)
        return value

    mine, other = natural(mine), natural(other)
    pair = [jnp.where(x == 0, mine, other), jnp.where(x == 0, other, mine)]
    return jnp.concatenate(pair, axis=0).astype(f32)


def place_kernel(depth, half, where, *refs):
    sources, out = refs[0:4], refs[4]
    step = pl.program_id(0)
    for unit in range(2):
        for side in range(2):

            @pl.when(jnp.logical_and(step // depth == unit, where[0] == side))
            def _(unit=unit, side=side):
                part = sources[2 * unit + (side ^ half)][...].astype(f32)
                out[...] = part if half else part.T


class Window:
    def __init__(self, *after):
        self.after, self.sent, self.got, self.chains = after, [], [], []

    def swap(self, value, axis, bit):
        value = tie(value, *self.after)[0]
        self.sent.append(value)
        self.got.append(swap(value, axis, bit))
        return Later(self, len(self.got) - 1)

    def step(self, chain):
        self.sent += chain.advance()
        self.chains.append((chain, len(self.got)))
        self.got += chain.got

    def open(self, *values):
        return tie(*values, *self.sent)[: len(values)]

    def close(self, *values):
        tied = tie(*values, *self.got)
        self.got = tied[len(values) :]
        for chain, start in self.chains:
            chain.got = self.got[start : start + len(chain.got)]
        return tied[: len(values)]


class Later:
    def __init__(self, window, place):
        self.window, self.place = window, place

    def get(self):
        return self.window.got[self.place]


def small_stages(shared, split):
    size = len(split)
    held = dict(enumerate(split))
    flat = shared.reshape(-1)
    for bit in bits_of(size):
        gone = [k for k in held if k & bit]
        (sent,) = tie(jnp.concatenate([flat] + [held[k] for k in gone]))
        (got,) = yield [sent], [swap(sent, "head", bit)]
        at = flat.shape[0]
        flat = flat + got[:at]
        for k in gone:
            width = held[k].shape[0]
            held[k ^ bit] = held[k ^ bit] + got[at : at + width]
            del held[k]
            at += width
    both = jnp.concatenate([flat, held[0]])
    for bit in bits_of(lax.axis_size("dp")):
        (both,) = tie(both)
        (got,) = yield [both], [swap(both, "dp", bit)]
        both = both + got
    yield [], [both[: flat.shape[0]].reshape(shared.shape), both[flat.shape[0] :]]


def on_device(
    layer_input,
    cotangent,
    crop_blocks,
    crop_padding,
    first_gain,
    first_shift,
    attend_weight,
    attend_bias,
    output_weight,
    output_bias,
    second_gain,
    second_shift,
    expand_weight,
    expand_bias,
    reduce_weight,
    reduce_bias,
):
    R = layer_input.shape[0]
    n = lax.axis_size("head")
    me = lax.axis_index("head")
    x = lax.axis_index("dp") % 2
    nb = R // STRETCH
    FF = expand_weight.shape[1] * n
    FQ = FF // QUADS
    fast = n == QUADS

    if fast:
        near = swap(attend_weight, "head", 1)
        ba_near = jnp.concatenate([attend_bias, swap(attend_bias, "head", 1)])
        be_near = jnp.concatenate([expand_bias, swap(expand_bias, "head", 1)])
        wa = [attend_weight, near, None, None]
        w = Window()
        wa_far = w.swap(attend_weight, "head", 2)
        bias_far = w.swap(jnp.concatenate([ba_near, be_near]), "head", 2)
        wo_near = w.swap(output_weight, "head", 1)
        we_near = w.swap(expand_weight, "head", 1)
        wr_near = w.swap(reduce_weight, "head", 1)
    else:
        wa = regroup(gather_shards(attend_weight), QUADS, 1)
        ba_near, ba_far = jnp.split(jnp.concatenate(gather_shards(attend_bias)), 2)

    sizes, pads = crop_blocks[0], crop_padding[0]
    crops = sizes.shape[0]
    closing = jnp.sum(jnp.tril(jnp.ones((crops, crops), jnp.int32)) * sizes[None, :], axis=1)

    def crop_of(position):
        return jnp.sum((position[..., None] >= closing).astype(jnp.int32), axis=-1)

    spots = me * nb + jnp.arange(nb, dtype=jnp.int32)
    crop = crop_of(spots)
    belongs = crop[:, None] == jnp.arange(crops, dtype=jnp.int32)[None, :]
    opening = jnp.sum(jnp.where(belongs, (closing - sizes)[None, :], 0), axis=1)
    padding = jnp.sum(jnp.where(belongs, pads[None, :], 0), axis=1)
    thr = jnp.maximum(padding - (spots - opening) * STRETCH, 0).astype(jnp.int32)
    first = (crop == crop[0]).astype(jnp.int32)
    one = jnp.ones((1,), jnp.int32)
    cont = jnp.concatenate([one, (crop[1:] == crop[:-1]).astype(jnp.int32), one])
    others = me ^ jnp.arange(n, dtype=jnp.int32)
    opens = crop_of(others * nb)
    closes = crop_of(others * nb + nb - 1)
    before = jnp.logical_and(others < me, closes == crop[0]).astype(f32)
    after = jnp.logical_and(others > me, opens == crop[nb - 1]).astype(f32)

    blocks = 2 if nb % 2 == 0 else 1
    rows = blocks * STRETCH
    tiles = R // rows
    many = 4 if nb % 4 == 0 else blocks
    gain1, shift1 = first_gain[None, :], first_shift[None, :]
    gain2, shift2 = second_gain[None, :], second_shift[None, :]
    like = jax.ShapeDtypeStruct
    HALF = D // 2
    full, side = rows_spec(rows, D), rows_spec(rows, HALF)
    low, wide = (like((R, D), bf16), full), (like((R, D), f32), full)
    narrow = (like((R, HALF), bf16), side)
    vec = whole_spec((1, D))
    state_rows = DH + 8

    def vector(value):
        return (value, vec)

    def project(source, pick, bias, fresh):
        tall, thin = rows_spec(many * STRETCH, D), rows_spec(many * STRETCH, HALF)
        ins = [(source, tall)]
        if fresh:
            ins += [vector(gain1), vector(shift1)]
        ins += [(wa[k], whole_spec((D, PW))) for k in pick]
        ins += [(bias, whole_spec((1, 2 * PW)))]
        outs = [(narrow[0], thin)] * 3 + ([(low[0], tall)] if fresh else [])
        outs += [
            (like((state_rows, HALF), f32), sum_spec((state_rows, HALF))),
            (like((nb * DH, HALF), f32), rows_spec(many * DH, HALF)),
            (like((nb * 8, HALF), f32), rows_spec(many * 8, HALF)),
        ]
        return call(
            functools.partial(qkv_kernel, many, fresh),
            "qkv",
            (thr, cont),
            nb // many,
            ins,
            outs,
            [pltpu.VMEM((DH, HALF), f32), pltpu.VMEM((8, HALF), f32)],
            3 * R * D * D,
            8 * R * D + 3 * D * D,
        )

    bias = ba_near[None, :]
    source = layer_input
    if fast:
        source, bias = w.open(source, bias)
    q01, k01, v01, normed, trail01, st01, kt01 = project(source, (0, 1), bias, True)
    if fast:
        q01, k01, v01, normed, trail01 = w.close(q01, k01, v01, normed, trail01)
        wa[2] = wa_far.get()
        wa[3] = swap(wa[2], "head", 1)
        ba_far, be_far = bias_far.get()[: ba_near.shape[0]], bias_far.get()[ba_near.shape[0] :]
        be_slots = jnp.split(jnp.concatenate([be_near, be_far]), QUADS)
        wo = [output_weight, wo_near.get(), None, None]
        w = Window(trail01)
        wo_far = w.swap(output_weight, "head", 2)
        normed, wa[3] = w.open(normed, wa[3])
    else:
        wo = regroup(gather_shards(output_weight), QUADS, 0)
        we = regroup(gather_shards(expand_weight), QUADS, 1)
        wr = regroup(gather_shards(reduce_weight), QUADS, 0)
        be_slots = jnp.split(jnp.concatenate(gather_shards(expand_bias)), QUADS)
    q23, k23, v23, trail23, st23, kt23 = project(normed, (2, 3), ba_far[None, :], False)
    if fast:
        q23, k23, v23, trail23 = w.close(q23, k23, v23, trail23)
        wo[2] = wo_far.get()
        wo[3] = swap(wo[2], "head", 1)
    s_in = swap_state(jnp.concatenate([trail01, trail23], axis=1), before)
    if fast:
        w = Window(s_in)
        we_cut, wr_cut = jnp.split(expand_weight, 2, axis=1), jnp.split(reduce_weight, 2)
        wr_far = w.swap(wr_cut[0], "head", 2)
        (s_in,) = w.open(s_in)

    tall, thin = rows_spec(many * STRETCH, D), rows_spec(many * STRETCH, HALF)
    att, rec, st, kt, middle, n2 = call(
        functools.partial(attend_kernel, many),
        "attend",
        (first, thr),
        nb // many,
        [
            (a, spec)
            for part in ((q01, k01, v01, st01, kt01), (q23, k23, v23, st23, kt23))
            for a, spec in zip(
                part,
                [thin] * 3 + [rows_spec(many * DH, HALF), rows_spec(many * 8, HALF)],
            )
        ]
        + [
            (layer_input, tall),
            (s_in, whole_spec((state_rows, D))),
            vector(output_bias[None, :]),
            vector(gain2),
            vector(shift2),
        ]
        + [(w, whole_spec((QW, D))) for w in wo],
        [
            (low[0], tall),
            (wide[0], tall),
            (like((nb * DH, D), bf16), rows_spec(many * DH, D)),
            (like((nb * 8, D), f32), rows_spec(many * 8, D)),
            (wide[0], tall),
            (low[0], tall),
        ],
        [],
        12 * R * D * D,
        20 * R * D,
    )

    if fast:
        att, rec, st, kt, middle, n2 = w.close(att, rec, st, kt, middle, n2)
        we = [expand_weight, we_near.get(), [None, None], [None, None]]
        wr = [reduce_weight, wr_near.get(), [wr_far.get(), None], [None, None]]

    def ffn(picks, part, extra):
        widths = [FQ if half is None else FQ // 2 for _, half in picks]
        spots = [(k, width, half or 0) for (k, half), width in zip(picks, widths)]
        ins = [(n2, full), (cotangent, full)]
        ins += [(be_slots[k][None, :], whole_spec((1, width), at)) for k, width, at in spots]
        if part is not None:
            ins += [(part[0], full), (part[1], full)]
        for group, spec, dims in ((we, whole_spec, (D, None)), (wr, part_spec, (None, D))):
            for k, width, at in spots:
                shape = tuple(d or width for d in dims)
                halves = isinstance(group[k], list)
                weight = group[k][at] if halves else group[k]
                ins.append((weight, spec(shape, 0 if halves else at)))
        outs = [(like((2 * w, D), bf16), whole_spec((2 * w, D))) for w in widths]
        outs += [(like((8, w), f32), sum_spec((8, w))) for w in widths]
        if extra is None:
            outs += [wide, wide]
        else:
            ins += extra
            outs += [low, wide, low, low, low]
            outs += [
                (like((state_rows, D), f32), sum_spec((state_rows, D))),
                (like((nb * DH, D), f32), rows_spec(blocks * DH, D)),
                (like((nb * 8, D), f32), rows_spec(blocks * 8, D)),
                (like((32, D), f32), sum_spec((32, D))),
            ]
        results = call(
            functools.partial(ffn_kernel, blocks, widths, part is None, extra is not None),
            "ffn",
            (first,) if extra is not None else (),
            tiles,
            ins,
            outs,
            [pltpu.VMEM((2 * w, D), f32) for w in widths],
            12 * R * D * sum(widths),
            20 * R * D,
        )
        for i, (k, half) in enumerate(picks):
            eb[k].append(results[len(picks) + i])
        return list(results[: len(picks)]), list(results[2 * len(picks) :])

    eb = [[], [], [], []]
    extra = [
        (middle, full),
        (att, full),
        (rec, full),
        (q01, side),
        (q23, side),
        vector(gain2),
        vector(reduce_bias[None, :]),
    ] + [(w, whole_spec((QW, D))) for w in wo]
    def total(*terms):
        return sum(term.astype(f32) for term in terms).astype(bf16)

    if fast:
        w = Window(n2)
        we_far = w.swap(we_cut[0], "head", 2)
        wr_far = w.swap(wr_cut[1], "head", 2)
        wr_last = w.swap(wr[2][0], "head", 1)
        (n2,) = w.open(n2)
        (near, own), part = ffn([(1, 0), (0, 0)], None, None)
        n2, near, own, *part = w.close(n2, near, own, *part)
        we[2][0], wr[2][1], wr[3][0] = we_far.get(), wr_far.get(), wr_last.get()
        we[3][0] = swap(we[2][0], "head", 1)
        w = Window(part[0])
        we_far = w.swap(we_cut[1], "head", 2)
        wr_last = w.swap(wr[2][1], "head", 1)
        near = w.swap(near, "head", 1)
        (part[0],) = w.open(part[0])
        (last_far, far), part = ffn([(3, 0), (2, 0)], part, None)
        last_far, far, *part = w.close(last_far, far, *part)
        we[2][1], wr[3][1] = we_far.get(), wr_last.get()
        we[3][1] = swap(we[2][1], "head", 1)
        far = total(far, swap(last_far, "head", 1))
        near_a = near.get()
        w = Window(part[0])
        far = w.swap(far, "head", 2)
        (part[0],) = w.open(part[0])
        (last_far, far_b), part = ffn([(3, 1), (2, 1)], part, None)
        last_far, far_b, *part = w.close(last_far, far_b, *part)
        sum_a = Stages(sum_stages([own, near_a, far.get()]))
        far = total(far_b, swap(last_far, "head", 1))
        w = Window(part[0])
        w.step(sum_a)
        far, part[0] = w.open(far, part[0])
        (near,), part = ffn([(1, 1)], part, None)
        near, *part = w.close(near, *part)
        w = Window(part[0])
        far = w.swap(far, "head", 2)
        near = w.swap(near, "head", 1)
        w.step(sum_a)
        (part[0],) = w.open(part[0])
        (own,), results = ffn([(0, 1)], part, extra)
        own, *results = w.close(own, *results)
        far, near = far.get(), near.get()
    else:
        grads, part = [None] * 4, None
        for k in (3, 2, 1):
            (grads[k],), part = ffn([(k, None)], part, None)
        (grads[0],), results = ffn([(0, None)], part, extra)
    layer_output, grad_middle, branch, gn, t, leading, pr, kr, sums2 = results

    def back(pick, q, k, v, state):
        count = len(pick)
        at, inner, width = pick[0] // count, (pick[0] % 2) // count, count * QW
        return call(
            functools.partial(back_kernel, blocks, tiles, count),
            "attend_back",
            (cont,),
            tiles,
            [(a, back_spec(rows, width, tiles, inner)) for a in (q, k, v)]
            + [(a, back_spec(rows, width, tiles, at)) for a in (gn, t)]
            + [
                (st, back_spec(blocks * DH, width, tiles, at)),
                (kt, back_spec(blocks * 8, width, tiles, at)),
                (pr, back_spec(blocks * DH, width, tiles, at)),
                (kr, back_spec(blocks * 8, width, tiles, at)),
                (state, whole_spec((state_rows, width), at)),
                (normed, back_spec(rows, D, tiles)),
                (att, back_spec(rows, width, tiles, at)),
                (branch, back_spec(rows, D, tiles)),
            ],
            [(like((R, PW), bf16), back_spec(rows, PW, tiles))] * count
            + [(like((PW + QW, D), bf16), whole_spec((PW + QW, D)))] * count
            + [(like((8, count * PW), f32), sum_spec((8, count * PW)))],
            [pltpu.VMEM((DH, width), f32), pltpu.VMEM((8, width), f32)]
            + [pltpu.VMEM((PW + QW, D), f32)] * count,
            6 * count * R * D * D,
            5 * count * R * D,
        )

    def inputs(start, count, out, x_in):
        at = rows_spec(rows, D, 0, start)
        ins = [(x_in, at), (grad_middle, at), vector(gain1)]
        ins += [(g, rows_spec(rows, PW, 0, start)) for g in gp]
        ins += [(w, whole_spec((D, PW))) for w in wa]
        if out is not None:
            ins += [(out, pl.BlockSpec(memory_space=pl.ANY))]
        return call(
            input_kernel,
            "input_grad",
            (),
            count,
            ins,
            [(wide[0], at), (like((16, D), f32), sum_spec((16, D)))],
            [],
            6 * rows * count * D * D,
            16 * rows * count * D,
            None if out is None else {len(ins) - 1: 0},
        )

    gp = [None] * 4
    if fast:
        g_in = swap_state(leading, after)
        sum_b = Stages(sum_stages([own, near, far]))
        w = Window(g_in)
        w.step(sum_b)
        w.step(sum_a)
        (g_in,) = w.open(g_in)
        gp[2], gp[3], da2, da3, ba23 = back((2, 3), q23, k23, v23, g_in)
        gp[2], gp[3], da2, da3, ba23, g_in = w.close(gp[2], gp[3], da2, da3, ba23, g_in)

        far = total(da2, swap(da3, "head", 1))
        w = Window(g_in)
        far = w.swap(far, "head", 2)
        w.step(sum_b)
        w.step(sum_a)
        (g_in,) = w.open(g_in)
        gp[0], gp[1], da0, da1, ba01 = back((0, 1), q01, k01, v01, g_in)
        gp[0], gp[1], da0, da1, ba01 = w.close(gp[0], gp[1], da0, da1, ba01)
        near = swap(da1, "head", 1)
        sum_c = Stages(sum_stages([da0, near, far.get()], True))
        w = Window(gp[0])
        w.step(sum_c)
        w.step(sum_b)
        half = tiles // 2
        (layer_in,) = w.open(layer_input)
        input_grad, sums1 = inputs(0, half, None, layer_in)
        input_grad, sums1 = w.close(input_grad, sums1)
        w = Window(input_grad)
        w.step(sum_c)
        w.step(sum_b)
        (input_grad,) = w.open(input_grad)
        input_grad, more = inputs(half, tiles - half, input_grad, layer_in)
        input_grad, more = w.close(input_grad, more)
        sums1 = sums1 + more
        where = lax.axis_index("dp")
        where = jnp.stack([where % 2, where // 2]).astype(jnp.int32)
        depth = lax.axis_size("dp") // 2
        piece = FQ // 2 // depth

        def source(unit):
            def index(i, where):
                at = jnp.where(i // depth == unit, i % depth, 0 if unit else depth - 1)
                return (at ^ where[1], 0)

            return pl.BlockSpec((piece, D), index)

        ins = [(v, source(0)) for v in sum_a.finish()] + [(v, source(1)) for v in sum_b.finish()]

        def placed(half, shape, block, index):
            w = Window(input_grad)
            w.step(sum_c)
            (at,) = w.open(where)
            out = call(
                functools.partial(place_kernel, depth, half),
                "place",
                (at,),
                2 * depth,
                ins,
                [(like(shape, f32), pl.BlockSpec(block, index))],
                [],
                0,
                6 * FQ * D,
            )
            return w.close(*out)[0]

        expand_weight_grad = placed(0, (D, FQ), (D, piece), lambda i, *_: (0, i))
        sums1 = tie(sums1, expand_weight_grad)[0]
        eb = [list(tie(*parts, sums1)[: len(parts)]) for parts in eb]
        reduce_weight_grad = placed(1, (FQ, D), (piece, D), lambda i, *_: (i, 0))
        sum_c = whole_sum(sum_c)
        attend_weight_grad, output_weight_grad = sum_c[:PW].T, sum_c[PW:]
    else:
        g_in = swap_state(leading, after)
        gp[2], gp[3], *da23, ba23 = back((2, 3), q23, k23, v23, g_in)
        gp[0], gp[1], *da01, ba01 = back((0, 1), q01, k01, v01, g_in)
        da = da01 + da23

        def reduce(parts):
            return whole_sum(Stages(sum_stages([scatter_head(regroup(parts, n, 0))])))

        expand_weight_grad = reduce([g[:FQ] for g in grads]).T
        reduce_weight_grad = reduce([g[FQ:] for g in grads])
        attend_weight_grad = reduce([g[:PW] for g in da]).T
        output_weight_grad = reduce([g[PW:] for g in da])
        input_grad, sums1 = inputs(0, tiles, None, layer_input)

    eb = [jnp.sum(jnp.concatenate(parts, axis=1), axis=0) for parts in eb]
    eb = regroup(eb, n, 0)
    ab = regroup([jnp.sum(jnp.concatenate([ba01, ba23], axis=1), axis=0)], n, 0)
    shared = jnp.concatenate(
        [
            jnp.sum(sums1.reshape(2, 8, D), axis=1),
            jnp.sum(sums2.reshape(4, 8, D), axis=1),
        ]
    )
    split = [jnp.concatenate(both) for both in zip(eb, ab)]
    shared, split = Stages(small_stages(shared, split)).finish()
    shared1, shared2 = shared[:2], shared[2:]
    expand_bias_grad, attend_bias_grad = split[: eb[0].shape[0]], split[eb[0].shape[0] :]
    return (
        layer_output,
        input_grad,
        shared1[0],
        shared1[1],
        attend_weight_grad,
        attend_bias_grad,
        output_weight_grad,
        shared2[0],
        shared2[1],
        shared2[2],
        expand_weight_grad,
        expand_bias_grad,
        reduce_weight_grad,
        shared2[3],
    )


def solution(mesh):
    in_specs = (
        P(("dp", "head"), None),
        P(("dp", "head"), None),
        P("dp", None),
        P("dp", None),
        P(),
        P(),
        P(None, "head"),
        P("head"),
        P("head", None),
        P(),
        P(),
        P(),
        P(None, "head"),
        P("head"),
        P("head", None),
        P(),
    )
    out_specs = (
        P(("dp", "head"), None),
        P(("dp", "head"), None),
        P(),
        P(),
        P(None, "head"),
        P("head"),
        P("head", None),
        P(),
        P(),
        P(),
        P(None, "head"),
        P("head"),
        P("head", None),
        P(),
    )
    return jax.shard_map(
        on_device, mesh=mesh, in_specs=in_specs, out_specs=out_specs, check_vma=False
    )
```

```python
import functools

import jax
import jax.numpy as jnp
from jax import lax
from jax.experimental import pallas as pl
from jax.experimental.pallas import tpu as pltpu
from jax.sharding import PartitionSpec as P

DH = 64
STRETCH = 128
D = 1024
QUADS = 4
QW = D // QUADS
PW = 3 * QW
EPS = 1e-05
VMEM = 60 * 1024 * 1024

f32 = jnp.float32
bf16 = jnp.bfloat16


def nn(a, b):
    return lax.dot_general(a, b, (((1,), (0,)), ((), ())), preferred_element_type=f32)


def nt(a, b):
    return lax.dot_general(a, b, (((1,), (1,)), ((), ())), preferred_element_type=f32)


def tn(a, b):
    return lax.dot_general(a, b, (((0,), (0,)), ((), ())), preferred_element_type=f32)


PAIR = 2 * DH


def side_rows(kind):
    lane = lax.broadcasted_iota(jnp.int32, (1, PAIR), 1) // DH
    return [(lane == h).astype(kind) for h in range(2)]


def spread(block, picks):
    return jnp.concatenate([block * picks[0], block * picks[1]], axis=0)


def pair_product(left, right, picks):
    square = tn(left, right)
    return square[0:DH] * picks[0] + square[DH:PAIR] * picks[1]


def cut(start, width=PAIR):
    return slice(start * width, (start + 1) * width)


def centre(values):
    average = jnp.mean(values, axis=-1, keepdims=True)
    centred = values - average
    spread = jnp.mean(centred * centred, axis=-1, keepdims=True)
    inverse = lax.rsqrt(spread + EPS)
    return centred * inverse, inverse


def norm_back(xhat, inverse, grad, gain):
    w = grad * gain
    return inverse * (
        w
        - jnp.mean(w, axis=-1, keepdims=True)
        - xhat * jnp.mean(w * xhat, axis=-1, keepdims=True)
    )


def fold_rows(values):
    rows, columns = values.shape
    return jnp.sum(values.reshape(rows // 8, 8, columns), axis=0)


def normal_parts(v):
    size = jnp.abs(v) * 0.7071067811865476
    t = 1.0 / (1.0 + 0.3275911 * size)
    bell = jnp.exp(-0.5 * v * v)
    poly = t * (
        0.254829592
        + t * (-0.284496736 + t * (1.421413741 + t * (-1.453152027 + t * 1.061405429)))
    )
    tail = 0.5 * poly * bell
    return jnp.where(v < 0, tail, 1.0 - tail), bell


def qkv_kernel(blocks, fresh, thr, cont, *refs):
    if fresh:
        x, gain, shift, n_out = refs[0], refs[1], refs[2], refs[9]
        wa, ba = refs[3:5], refs[5]
        q_out, k_out, v_out = refs[6:9]
        t_out, st_out, kt_out, state, sums = refs[10:15]
    else:
        n_in = refs[0]
        wa, ba = refs[1:3], refs[3]
        q_out, k_out, v_out = refs[4:7]
        t_out, st_out, kt_out, state, sums = refs[7:12]
    step = pl.program_id(0)
    rows = blocks * STRETCH

    @pl.when(step == 0)
    def _():
        state[...] = jnp.zeros_like(state)
        sums[...] = jnp.zeros_like(sums)

    if fresh:
        xhat, _ = centre(x[...].astype(f32))
        normed = (xhat * gain[...] + shift[...]).astype(bf16)
        n_out[...] = normed
    else:
        normed = n_in[...]
    place = lax.broadcasted_iota(jnp.int32, (STRETCH, 128), 0)
    valid = jnp.concatenate(
        [(place >= thr[step * blocks + b]).astype(f32) for b in range(blocks)], axis=0
    )
    low = lax.broadcasted_iota(jnp.int32, (rows, 128), 1) < DH

    def feature(values):
        return jnp.where(values > 0, values + 1.0, jnp.exp(jnp.minimum(values, 0.0)))

    for g in range(2):
        project = nn(normed, wa[g][...]) + ba[:, g * PW : (g + 1) * PW]
        for pair in range(2):
            c0, c1, c2 = (
                project[:, pair * 384 + j * 128 : pair * 384 + (j + 1) * 128] for j in range(3)
            )
            at = slice(g * QW + pair * 128, g * QW + (pair + 1) * 128)
            q_out[:, at] = feature(jnp.where(low, c0, c1)).astype(bf16)
            key = pltpu.roll(jnp.where(low, c2, c0), DH, 1)
            k_out[:, at] = (valid * feature(key)).astype(bf16)
            v_out[:, at] = jnp.where(low, c1, c2).astype(bf16)
    picks = side_rows(f32)
    for b in range(blocks):
        keep = cont[step * blocks + b].astype(f32)
        here = cut(b, STRETCH)
        state[...] = state[...] * keep
        sums[...] = sums[...] * keep
        st_out[cut(b, DH), :] = state[...]
        kt_out[cut(b, 8), :] = sums[...]
        for p in range(4):
            key = k_out[here, cut(p)]
            state[:, cut(p)] += pair_product(key, v_out[here, cut(p)], picks)
            sums[:, cut(p)] += fold_rows(key.astype(f32))

    @pl.when(step == pl.num_programs(0) - 1)
    def _():
        t_out[0:DH, :] = state[...]
        t_out[DH : DH + 8, :] = sums[...]


def attend_kernel(blocks, first, thr, *refs):
    qkv = refs[0:5], refs[5:10]
    x, s_in, bo, gain, shift = refs[10:15]
    wo = refs[15:19]
    att_out, rec_out, st_out, kt_out, mid_out, n_out = refs[19:25]
    step = pl.program_id(0)
    picks = side_rows(bf16)
    row = lax.broadcasted_iota(jnp.int32, (STRETCH, 2 * STRETCH), 0)
    lane = lax.broadcasted_iota(jnp.int32, (STRETCH, 2 * STRETCH), 1) % STRETCH
    lower = lane <= row
    ones_scores = spread(jnp.ones((STRETCH, PAIR), bf16), picks)
    ones_state = spread(jnp.ones((DH, PAIR), bf16), picks)
    zeros = jnp.zeros((PAIR, PAIR), bf16)
    ones = jnp.concatenate([ones_scores, zeros, ones_state], axis=0)
    came = jnp.sum(s_in[DH : DH + 8], axis=0, keepdims=True)
    for b in range(blocks):
        joins = first[step * blocks + b].astype(f32)
        here = cut(b, STRETCH)
        for p in range(8):
            at, own = cut(p), cut(p % 4)
            q, k, v, st, kt = qkv[p // 4]
            qb, kb, vb = q[here, own], k[here, own], v[here, own]
            state = (st[cut(b, DH), own] + joins * s_in[0:DH, at]).astype(bf16)
            total = jnp.sum(kt[cut(b, 8), own], axis=0, keepdims=True) + joins * came[:, at]
            st_out[cut(b, DH), at] = state
            kt_out[cut(b, 8), at] = jnp.broadcast_to(total, (8, PAIR))
            scores = nt(qb, spread(kb, picks))
            scores = jnp.where(lower, scores, 0.0).astype(bf16)
            weighted = (qb.astype(f32) * total).astype(bf16)
            left = jnp.concatenate([scores, qb, weighted], axis=1)
            right = jnp.concatenate([spread(vb, picks), spread(state, picks), zeros], axis=0)
            both = nn(left, jnp.concatenate([right, ones], axis=1))
            rec = 1.0 / jnp.maximum(both[:, PAIR:], 1.0)
            rec_out[here, at] = rec
            att_out[here, at] = (both[:, :PAIR] * rec).astype(bf16)
    place = lax.broadcasted_iota(jnp.int32, (STRETCH, D), 0)
    for b in range(blocks):
        here = slice(b * STRETCH, (b + 1) * STRETCH)

        @pl.when(thr[step * blocks + b] > 0)
        def _(b=b, here=here):
            valid = (place >= thr[step * blocks + b]).astype(f32)
            rec_out[here, :] = rec_out[here, :] * valid
            att_out[here, :] = (att_out[here, :].astype(f32) * valid).astype(bf16)

    middle = x[...].astype(f32) + bo[...]
    for g in range(QUADS):
        middle = middle + nn(att_out[:, g * QW : (g + 1) * QW], wo[g][...])
    mid_out[...] = middle
    xhat, _ = centre(middle)
    n_out[...] = (xhat * gain[...] + shift[...]).astype(bf16)


def ffn_kernel(blocks, widths, fresh, final, *refs):
    refs = list(refs)

    def take(count):
        taken = refs[:count]
        del refs[:count]
        return taken

    count = len(widths)
    if final:
        (first,) = take(1)
    n2, cot = take(2)
    be = take(count)
    if not fresh:
        part_out, part_grad = take(2)
    we, wr = take(count), take(count)
    if final:
        mid, att, rec, q01, q23, gain, br = take(7)
        wo = take(4)
    grad_out, be_sum = take(count), take(count)
    if final:
        out, gm_out, gb_out, gn_out, t_out, l_out, pr_out, kr_out, sums = take(9)
    else:
        next_out, next_grad = take(2)
    grad_sum = take(count)
    step = pl.program_id(0)

    @pl.when(step == 0)
    def _():
        for total in grad_sum + be_sum:
            total[...] = jnp.zeros_like(total)
        if final:
            l_out[...] = jnp.zeros_like(l_out)
            sums[...] = jnp.zeros_like(sums)

    normed = n2[...]
    cotangent = cot[...]
    reduced = None if fresh else part_out[...]
    grad = None if fresh else part_grad[...]
    for i, width in enumerate(widths):
        hidden = nn(normed, we[i][...]) + be[i][...]
        grad_act = nt(cotangent, wr[i][...])
        phi, bell = normal_parts(hidden)
        active = (hidden * phi).astype(bf16)
        back = (grad_act * (phi + hidden * (0.3989422804014327 * bell))).astype(bf16)
        be_sum[i][...] += fold_rows(back.astype(f32))
        grad_sum[i][0:width, :] += tn(back, normed)
        grad_sum[i][width : 2 * width, :] += tn(active, cotangent)
        more = nn(active, wr[i][...])
        reduced = more if reduced is None else reduced + more
        more = nt(back, we[i][...])
        grad = more if grad is None else grad + more

    @pl.when(step == pl.num_programs(0) - 1)
    def _():
        for out_ref, total in zip(grad_out, grad_sum):
            out_ref[...] = total[...].astype(bf16)

    if not final:
        next_out[...] = reduced
        next_grad[...] = grad
        return
    middle = mid[...]
    out[...] = (middle + reduced + br[...]).astype(bf16)
    xhat, inverse = centre(middle)
    cot_wide = cotangent.astype(f32)
    grad_middle = cot_wide + norm_back(xhat, inverse, grad, gain[...])
    gm_out[...] = grad_middle
    branch = grad_middle.astype(bf16)
    gb_out[...] = branch
    sums[0:8, :] += fold_rows(branch.astype(f32))
    sums[8:16, :] += fold_rows(grad * xhat)
    sums[16:24, :] += fold_rows(grad)
    sums[24:32, :] += fold_rows(cot_wide)
    for g in range(QUADS):
        at = slice(g * QW, (g + 1) * QW)
        grad_att = nt(branch, wo[g][...]).astype(bf16).astype(f32)
        share = rec[:, at]
        numer = grad_att * share
        gn_out[:, at] = numer.astype(bf16)
        t_out[:, at] = jnp.where(
            share < 1.0, -(numer * att[:, at].astype(f32)), 0.0
        ).astype(bf16)
    picks = side_rows(f32)
    ones = spread(jnp.ones((DH, PAIR), bf16), side_rows(bf16))
    for b in range(blocks):
        here = cut(b, STRETCH)
        for p in range(8):
            at = cut(p)
            query = (q01, q23)[p // 4][here, cut(p % 4)]
            pr_out[cut(b, DH), at] = pair_product(query, gn_out[here, at], picks)
            grad_denom = nn(t_out[here, at], ones)
            kr_out[cut(b, 8), at] = fold_rows(grad_denom * query.astype(f32))

        @pl.when(first[step * blocks + b] == 1)
        def _(b=b):
            l_out[0:DH, :] += pr_out[cut(b, DH), :]
            l_out[DH : DH + 8, :] += kr_out[cut(b, 8), :]


def back_kernel(blocks, tiles, quads, cont, q, k, v, gn, t, st, kt, pr, kr, g_in, normed, att, branch, *refs):
    gp_out, da_out, ba_sum = refs[0:quads], refs[quads : 2 * quads], refs[2 * quads]
    state, total = refs[2 * quads + 1 : 2 * quads + 3]
    da_sum = refs[2 * quads + 3 :]
    step = pl.program_id(0)
    tile = tiles - 1 - step

    @pl.when(step == 0)
    def _():
        state[...] = g_in[0:DH]
        total[...] = jnp.broadcast_to(
            jnp.sum(g_in[DH : DH + 8], axis=0, keepdims=True), total.shape
        )
        ba_sum[...] = jnp.zeros_like(ba_sum)
        for da in da_sum:
            da[...] = jnp.zeros_like(da)

    picks = side_rows(bf16)
    row = lax.broadcasted_iota(jnp.int32, (STRETCH, 2 * STRETCH), 0)
    lane = lax.broadcasted_iota(jnp.int32, (STRETCH, 2 * STRETCH), 1) % STRETCH
    lower = lane <= row
    upper = lane >= row
    low_lane = lax.broadcasted_iota(jnp.int32, (STRETCH, PAIR), 1) < DH
    all_ones = jnp.ones((STRETCH, PAIR), bf16)
    ones_scores = spread(all_ones, picks)
    ones_state = spread(jnp.ones((DH, PAIR), bf16), picks)
    for b in reversed(range(blocks)):
        keep = cont[tile * blocks + b + 1].astype(f32)
        here = cut(b, STRETCH)
        for p in range(2 * quads):
            at = cut(p)
            qb, kb, vb, gb, tb = q[here, at], k[here, at], v[here, at], gn[here, at], t[here, at]
            state_here = state[:, at] * keep
            total_here = total[:, at] * keep
            behind = spread(state_here.astype(bf16), picks)
            state[:, at] = state_here + pr[cut(b, DH), at]
            total[:, at] = total_here + jnp.sum(kr[cut(b, 8), at], axis=0, keepdims=True)
            spread_q, spread_g = spread(qb, picks), spread(gb, picks)
            forward = spread(st[cut(b, DH), at], picks)
            scores = nt(
                jnp.concatenate([gb, tb], axis=1),
                jnp.concatenate([spread(vb, picks), ones_scores], axis=1),
            )
            scores = jnp.where(lower, scores, 0.0).astype(bf16)
            turned = nt(
                jnp.concatenate([vb, all_ones], axis=1),
                jnp.concatenate([spread_g, spread(tb, picks)], axis=1),
            )
            turned = jnp.where(upper, turned, 0.0).astype(bf16)
            mixed = jnp.where(upper, nt(kb, spread_q), 0.0).astype(bf16)
            grad_denom = nn(tb, ones_state)
            grad_q = (
                nn(scores, spread(kb, picks))
                + nt(gb, forward)
                + grad_denom * kt[b * 8 : b * 8 + 1, at]
            )
            grad_k = nn(turned, spread_q) + nt(vb, behind) + total_here[0:1]
            grad_v = nn(jnp.concatenate([mixed, kb], axis=1), jnp.concatenate([spread_g, behind]))
            grad_q = grad_q * jnp.minimum(qb.astype(f32), 1.0)
            grad_k = grad_k * jnp.minimum(kb.astype(f32), 1.0)
            swapped = pltpu.roll(grad_k, DH, 1)
            for j, piece in enumerate(
                (
                    jnp.where(low_lane, grad_q, swapped),
                    jnp.where(low_lane, grad_v, grad_q),
                    jnp.where(low_lane, swapped, grad_v),
                )
            ):
                piece = piece.astype(bf16)
                start = (p % 2) * 384 + j * 128
                gp_out[p // 2][here, start : start + 128] = piece
                start += (p // 2) * PW
                ba_sum[:, start : start + 128] += fold_rows(piece.astype(f32))
    for g in range(quads):
        da_sum[g][0:PW, :] += tn(gp_out[g][...], normed[...])
        da_sum[g][PW:, :] += tn(att[:, cut(g, QW)], branch[...])

    @pl.when(step == tiles - 1)
    def _():
        for out, da in zip(da_out, da_sum):
            out[...] = da[...].astype(bf16)


def input_kernel(x, gm, gain, *refs):
    gp, wa = refs[0:4], refs[4:8]
    out, sums = refs[-2:]

    @pl.when(pl.program_id(0) == 0)
    def _():
        sums[...] = jnp.zeros_like(sums)

    grad = nt(gp[0][...], wa[0][...])
    for g in range(1, QUADS):
        grad = grad + nt(gp[g][...], wa[g][...])
    xhat, inverse = centre(x[...].astype(f32))
    out[...] = gm[...] + norm_back(xhat, inverse, grad, gain[...])
    sums[0:8, :] += fold_rows(grad * xhat)
    sums[8:16, :] += fold_rows(grad)


def rows_spec(rows, columns, at=0, start=0):
    return pl.BlockSpec((rows, columns), lambda i, *_: (i + start, at))


def back_spec(rows, columns, tiles, at=0):
    return pl.BlockSpec((rows, columns), lambda i, *_: (tiles - 1 - i, at))


def whole_spec(shape, at=0):
    last = len(shape) - 1
    return pl.BlockSpec(
        shape, lambda i, *_: (0,) * last + (at,), pipeline_mode=pl.Buffered(1)
    )


def part_spec(shape, at):
    return pl.BlockSpec(shape, lambda i, *_: (at, 0), pipeline_mode=pl.Buffered(1))


def sum_spec(shape):
    return pl.BlockSpec(shape, lambda i, *_: (0,) * len(shape))


def call(kernel, name, scalars, tiles, ins, outs, scratch, flops, moved, aliases=None):
    return pl.pallas_call(
        kernel,
        grid_spec=pltpu.PrefetchScalarGridSpec(
            num_scalar_prefetch=len(scalars),
            grid=(tiles,),
            in_specs=[spec for _, spec in ins],
            out_specs=[spec for _, spec in outs],
            scratch_shapes=list(scratch),
        ),
        out_shape=[shape for shape, _ in outs],
        compiler_params=pltpu.CompilerParams(vmem_limit_bytes=VMEM),
        cost_estimate=pl.CostEstimate(flops=flops, bytes_accessed=moved, transcendentals=0),
        input_output_aliases=aliases or {},
        name=name,
    )(*scalars, *[array for array, _ in ins])


def tie(*values):
    return lax.optimization_barrier(list(values))


def swap(value, axis, bit):
    size = lax.axis_size(axis)
    return lax.ppermute(value, axis, [(i, i ^ bit) for i in range(size)])


def bits_of(size):
    bit, bits = 1, []
    while bit < size:
        bits.append(bit)
        bit *= 2
    return bits


def gather_shards(own):
    size = lax.axis_size("head")
    held = {0: own}
    for bit in reversed(bits_of(size)):
        for k in list(held):
            held[k ^ bit] = swap(held[k], "head", bit)
    return [held[k] for k in range(size)]


def half_of(value, which, axis):
    size = value.shape[axis] // 2
    return lax.dynamic_slice_in_dim(value, which * size, size, axis)


def regroup(parts, count, axis):
    if len(parts) == count:
        return list(parts)
    whole = jnp.concatenate(parts, axis=axis)
    width = whole.shape[axis] // count
    return [
        lax.slice_in_dim(whole, k * width, (k + 1) * width, axis=axis) for k in range(count)
    ]


def swap_state(mine, weights):
    size = lax.axis_size("head")
    sent = mine.astype(bf16)
    total = None
    for j in range(1, size):
        got = swap(sent, "head", j)
        slots = jnp.split(got, size, axis=1)
        got = jnp.concatenate([slots[k ^ j] for k in range(size)], axis=1).astype(f32)
        got = got * weights[j]
        total = got if total is None else total + got
    return total


def scatter_head(parts):
    held = dict(enumerate(parts))
    for bit in bits_of(len(parts)):
        for k in [k for k in held if k & bit]:
            got = swap(held.pop(k).astype(bf16), "head", bit)
            held[k ^ bit] = held[k ^ bit].astype(f32) + got.astype(f32)
    return held[0]


class Stages:
    def __init__(self, generator):
        self.generator, self.got = generator, None

    def advance(self):
        sent, self.got = self.generator.send(self.got)
        return sent

    def finish(self):
        while self.advance():
            pass
        return self.got


def sum_stages(terms, apart=False):
    size = lax.axis_size("dp")
    me = lax.axis_index("dp")
    x, z, depth = me % 2, me // 2, size // 2

    def half(which):
        total = None
        for term in terms:
            part = half_of(term, which, 0).astype(f32)
            total = part if total is None else total + part
        return total.astype(bf16)

    sent, kept = tie(half(1 - x), half(x))
    (got,) = yield [sent, kept], [swap(sent, "dp", 1)]
    mine = (kept.astype(f32) + got.astype(f32)).astype(bf16)
    rows = mine.shape[0] // depth
    own = lax.dynamic_slice_in_dim(mine, z * rows, rows, 0)
    sent = [
        lax.dynamic_slice_in_dim(mine, (z ^ j) * rows, rows, 0) for j in range(1, depth)
    ]
    own, *sent = tie(own, *sent)
    got = yield [own] + sent, [swap(part, "dp", 2 * j) for j, part in enumerate(sent, 1)]
    total = own.astype(f32)
    for part in got:
        total = total + part.astype(f32)
    (own,) = tie(total.astype(bf16))
    got = yield [own], [swap(own, "dp", 2 * j) for j in range(1, depth)]
    if apart:
        parts = [own] + list(got)
        got = yield parts, [swap(part, "dp", 1) for part in parts]
        mine, other = jnp.concatenate(parts, axis=0), jnp.concatenate(list(got), axis=0)
    else:
        (mine,) = tie(jnp.concatenate([own] + list(got), axis=0))
        (other,) = yield [mine], [swap(mine, "dp", 1)]

    yield [], [mine, other]


def whole_sum(stages):
    mine, other = stages.finish()
    me = lax.axis_index("dp")
    x, z, depth = me % 2, me // 2, lax.axis_size("dp") // 2
    rows = mine.shape[0] // depth

    def natural(value):
        for bit in bits_of(depth):
            shaped = value.reshape(depth // (2 * bit), 2, bit * rows, value.shape[1])
            turned = jnp.flip(shaped, axis=1)
            value = jnp.where((z & bit) != 0, turned, shaped).reshape(value.shape)
        return value

    mine, other = natural(mine), natural(other)
    pair = [jnp.where(x == 0, mine, other), jnp.where(x == 0, other, mine)]
    return jnp.concatenate(pair, axis=0).astype(f32)


def place_kernel(depth, half, where, *refs):
    sources, out = refs[0:4], refs[4]
    step = pl.program_id(0)
    for unit in range(2):
        for side in range(2):

            @pl.when(jnp.logical_and(step // depth == unit, where[0] == side))
            def _(unit=unit, side=side):
                part = sources[2 * unit + (side ^ half)][...].astype(f32)
                out[...] = part if half else part.T


class Window:
    def __init__(self, *after):
        self.after, self.sent, self.got, self.chains = after, [], [], []

    def swap(self, value, axis, bit):
        value = tie(value, *self.after)[0]
        self.sent.append(value)
        self.got.append(swap(value, axis, bit))
        return Later(self, len(self.got) - 1)

    def step(self, chain):
        self.sent += chain.advance()
        self.chains.append((chain, len(self.got)))
        self.got += chain.got

    def open(self, *values):
        return tie(*values, *self.sent)[: len(values)]

    def close(self, *values):
        tied = tie(*values, *self.got)
        self.got = tied[len(values) :]
        for chain, start in self.chains:
            chain.got = self.got[start : start + len(chain.got)]
        return tied[: len(values)]


class Later:
    def __init__(self, window, place):
        self.window, self.place = window, place

    def get(self):
        return self.window.got[self.place]


def small_stages(shared, split):
    size = len(split)
    held = dict(enumerate(split))
    flat = shared.reshape(-1)
    for bit in bits_of(size):
        gone = [k for k in held if k & bit]
        (sent,) = tie(jnp.concatenate([flat] + [held[k] for k in gone]))
        (got,) = yield [sent], [swap(sent, "head", bit)]
        at = flat.shape[0]
        flat = flat + got[:at]
        for k in gone:
            width = held[k].shape[0]
            held[k ^ bit] = held[k ^ bit] + got[at : at + width]
            del held[k]
            at += width
    both = jnp.concatenate([flat, held[0]])
    for bit in bits_of(lax.axis_size("dp")):
        (both,) = tie(both)
        (got,) = yield [both], [swap(both, "dp", bit)]
        both = both + got
    yield [], [both[: flat.shape[0]].reshape(shared.shape), both[flat.shape[0] :]]


def on_device(
    layer_input,
    cotangent,
    crop_blocks,
    crop_padding,
    first_gain,
    first_shift,
    attend_weight,
    attend_bias,
    output_weight,
    output_bias,
    second_gain,
    second_shift,
    expand_weight,
    expand_bias,
    reduce_weight,
    reduce_bias,
):
    R = layer_input.shape[0]
    n = lax.axis_size("head")
    me = lax.axis_index("head")
    x = lax.axis_index("dp") % 2
    nb = R // STRETCH
    FF = expand_weight.shape[1] * n
    FQ = FF // QUADS
    fast = n == QUADS

    if fast:
        near = swap(attend_weight, "head", 1)
        ba_near = jnp.concatenate([attend_bias, swap(attend_bias, "head", 1)])
        be_near = jnp.concatenate([expand_bias, swap(expand_bias, "head", 1)])
        wa = [attend_weight, near, None, None]
        w = Window()
        wa_far = w.swap(attend_weight, "head", 2)
        bias_far = w.swap(jnp.concatenate([ba_near, be_near]), "head", 2)
        wo_near = w.swap(output_weight, "head", 1)
        we_near = w.swap(expand_weight, "head", 1)
        wr_near = w.swap(reduce_weight, "head", 1)
    else:
        wa = regroup(gather_shards(attend_weight), QUADS, 1)
        ba_near, ba_far = jnp.split(jnp.concatenate(gather_shards(attend_bias)), 2)

    sizes, pads = crop_blocks[0], crop_padding[0]
    crops = sizes.shape[0]
    closing = jnp.sum(jnp.tril(jnp.ones((crops, crops), jnp.int32)) * sizes[None, :], axis=1)

    def crop_of(position):
        return jnp.sum((position[..., None] >= closing).astype(jnp.int32), axis=-1)

    spots = me * nb + jnp.arange(nb, dtype=jnp.int32)
    crop = crop_of(spots)
    belongs = crop[:, None] == jnp.arange(crops, dtype=jnp.int32)[None, :]
    opening = jnp.sum(jnp.where(belongs, (closing - sizes)[None, :], 0), axis=1)
    padding = jnp.sum(jnp.where(belongs, pads[None, :], 0), axis=1)
    thr = jnp.maximum(padding - (spots - opening) * STRETCH, 0).astype(jnp.int32)
    first = (crop == crop[0]).astype(jnp.int32)
    one = jnp.ones((1,), jnp.int32)
    cont = jnp.concatenate([one, (crop[1:] == crop[:-1]).astype(jnp.int32), one])
    others = me ^ jnp.arange(n, dtype=jnp.int32)
    opens = crop_of(others * nb)
    closes = crop_of(others * nb + nb - 1)
    before = jnp.logical_and(others < me, closes == crop[0]).astype(f32)
    after = jnp.logical_and(others > me, opens == crop[nb - 1]).astype(f32)

    blocks = 2 if nb % 2 == 0 else 1
    rows = blocks * STRETCH
    tiles = R // rows
    many = 4 if nb % 4 == 0 else blocks
    gain1, shift1 = first_gain[None, :], first_shift[None, :]
    gain2, shift2 = second_gain[None, :], second_shift[None, :]
    like = jax.ShapeDtypeStruct
    HALF = D // 2
    full, side = rows_spec(rows, D), rows_spec(rows, HALF)
    low, wide = (like((R, D), bf16), full), (like((R, D), f32), full)
    narrow = (like((R, HALF), bf16), side)
    vec = whole_spec((1, D))
    state_rows = DH + 8

    def vector(value):
        return (value, vec)

    def project(source, pick, bias, fresh):
        tall, thin = rows_spec(many * STRETCH, D), rows_spec(many * STRETCH, HALF)
        ins = [(source, tall)]
        if fresh:
            ins += [vector(gain1), vector(shift1)]
        ins += [(wa[k], whole_spec((D, PW))) for k in pick]
        ins += [(bias, whole_spec((1, 2 * PW)))]
        outs = [(narrow[0], thin)] * 3 + ([(low[0], tall)] if fresh else [])
        outs += [
            (like((state_rows, HALF), f32), sum_spec((state_rows, HALF))),
            (like((nb * DH, HALF), f32), rows_spec(many * DH, HALF)),
            (like((nb * 8, HALF), f32), rows_spec(many * 8, HALF)),
        ]
        return call(
            functools.partial(qkv_kernel, many, fresh),
            "qkv",
            (thr, cont),
            nb // many,
            ins,
            outs,
            [pltpu.VMEM((DH, HALF), f32), pltpu.VMEM((8, HALF), f32)],
            3 * R * D * D,
            8 * R * D + 3 * D * D,
        )

    bias = ba_near[None, :]
    source = layer_input
    if fast:
        source, bias = w.open(source, bias)
    q01, k01, v01, normed, trail01, st01, kt01 = project(source, (0, 1), bias, True)
    if fast:
        q01, k01, v01, normed, trail01 = w.close(q01, k01, v01, normed, trail01)
        wa[2] = wa_far.get()
        wa[3] = swap(wa[2], "head", 1)
        ba_far, be_far = bias_far.get()[: ba_near.shape[0]], bias_far.get()[ba_near.shape[0] :]
        be_slots = jnp.split(jnp.concatenate([be_near, be_far]), QUADS)
        wo = [output_weight, wo_near.get(), None, None]
        w = Window(trail01)
        wo_far = w.swap(output_weight, "head", 2)
        normed, wa[3] = w.open(normed, wa[3])
    else:
        wo = regroup(gather_shards(output_weight), QUADS, 0)
        we = regroup(gather_shards(expand_weight), QUADS, 1)
        wr = regroup(gather_shards(reduce_weight), QUADS, 0)
        be_slots = jnp.split(jnp.concatenate(gather_shards(expand_bias)), QUADS)
    q23, k23, v23, trail23, st23, kt23 = project(normed, (2, 3), ba_far[None, :], False)
    if fast:
        q23, k23, v23, trail23 = w.close(q23, k23, v23, trail23)
        wo[2] = wo_far.get()
        wo[3] = swap(wo[2], "head", 1)
    s_in = swap_state(jnp.concatenate([trail01, trail23], axis=1), before)
    if fast:
        w = Window(s_in)
        we_cut, wr_cut = jnp.split(expand_weight, 2, axis=1), jnp.split(reduce_weight, 2)
        wr_far = w.swap(wr_cut[0], "head", 2)
        (s_in,) = w.open(s_in)

    tall, thin = rows_spec(many * STRETCH, D), rows_spec(many * STRETCH, HALF)
    att, rec, st, kt, middle, n2 = call(
        functools.partial(attend_kernel, many),
        "attend",
        (first, thr),
        nb // many,
        [
            (a, spec)
            for part in ((q01, k01, v01, st01, kt01), (q23, k23, v23, st23, kt23))
            for a, spec in zip(
                part,
                [thin] * 3 + [rows_spec(many * DH, HALF), rows_spec(many * 8, HALF)],
            )
        ]
        + [
            (layer_input, tall),
            (s_in, whole_spec((state_rows, D))),
            vector(output_bias[None, :]),
            vector(gain2),
            vector(shift2),
        ]
        + [(w, whole_spec((QW, D))) for w in wo],
        [
            (low[0], tall),
            (wide[0], tall),
            (like((nb * DH, D), bf16), rows_spec(many * DH, D)),
            (like((nb * 8, D), f32), rows_spec(many * 8, D)),
            (wide[0], tall),
            (low[0], tall),
        ],
        [],
        12 * R * D * D,
        20 * R * D,
    )

    if fast:
        att, rec, st, kt, middle, n2 = w.close(att, rec, st, kt, middle, n2)
        we = [expand_weight, we_near.get(), [None, None], [None, None]]
        wr = [reduce_weight, wr_near.get(), [wr_far.get(), None], [None, None]]

    def ffn(picks, part, extra):
        widths = [FQ if half is None else FQ // 2 for _, half in picks]
        spots = [(k, width, half or 0) for (k, half), width in zip(picks, widths)]
        high = rows if extra is not None else many * STRETCH
        row = rows_spec(high, D)
        ins = [(n2, row), (cotangent, row)]
        ins += [(be_slots[k][None, :], whole_spec((1, width), at)) for k, width, at in spots]
        if part is not None:
            ins += [(part[0], row), (part[1], row)]
        for group, spec, dims in ((we, whole_spec, (D, None)), (wr, part_spec, (None, D))):
            for k, width, at in spots:
                shape = tuple(d or width for d in dims)
                halves = isinstance(group[k], list)
                weight = group[k][at] if halves else group[k]
                ins.append((weight, spec(shape, 0 if halves else at)))
        outs = [(like((2 * w, D), bf16), whole_spec((2 * w, D))) for w in widths]
        outs += [(like((8, w), f32), sum_spec((8, w))) for w in widths]
        if extra is None:
            outs += [(wide[0], row)] * 2
        else:
            ins += extra
            outs += [low, wide, low, low, low]
            outs += [
                (like((state_rows, D), f32), sum_spec((state_rows, D))),
                (like((nb * DH, D), f32), rows_spec(blocks * DH, D)),
                (like((nb * 8, D), f32), rows_spec(blocks * 8, D)),
                (like((32, D), f32), sum_spec((32, D))),
            ]
        results = call(
            functools.partial(ffn_kernel, blocks, widths, part is None, extra is not None),
            "ffn",
            (first,) if extra is not None else (),
            R // high,
            ins,
            outs,
            [pltpu.VMEM((2 * w, D), f32) for w in widths],
            12 * R * D * sum(widths),
            20 * R * D,
        )
        for i, (k, half) in enumerate(picks):
            eb[k].append(results[len(picks) + i])
        return list(results[: len(picks)]), list(results[2 * len(picks) :])

    eb = [[], [], [], []]
    extra = [
        (middle, full),
        (att, full),
        (rec, full),
        (q01, side),
        (q23, side),
        vector(gain2),
        vector(reduce_bias[None, :]),
    ] + [(w, whole_spec((QW, D))) for w in wo]
    def total(*terms):
        return sum(term.astype(f32) for term in terms).astype(bf16)

    if fast:
        w = Window(n2)
        we_far = w.swap(we_cut[0], "head", 2)
        wr_far = w.swap(wr_cut[1], "head", 2)
        wr_last = w.swap(wr[2][0], "head", 1)
        (n2,) = w.open(n2)
        (near, own), part = ffn([(1, 0), (0, 0)], None, None)
        n2, near, own, *part = w.close(n2, near, own, *part)
        we[2][0], wr[2][1], wr[3][0] = we_far.get(), wr_far.get(), wr_last.get()
        we[3][0] = swap(we[2][0], "head", 1)
        w = Window(part[0])
        we_far = w.swap(we_cut[1], "head", 2)
        wr_last = w.swap(wr[2][1], "head", 1)
        near = w.swap(near, "head", 1)
        (part[0],) = w.open(part[0])
        (last_far, far), part = ffn([(3, 0), (2, 0)], part, None)
        last_far, far, *part = w.close(last_far, far, *part)
        we[2][1], wr[3][1] = we_far.get(), wr_last.get()
        we[3][1] = swap(we[2][1], "head", 1)
        far = total(far, swap(last_far, "head", 1))
        near_a = near.get()
        w = Window(part[0])
        far = w.swap(far, "head", 2)
        (part[0],) = w.open(part[0])
        (last_far, far_b), part = ffn([(3, 1), (2, 1)], part, None)
        last_far, far_b, *part = w.close(last_far, far_b, *part)
        sum_a = Stages(sum_stages([own, near_a, far.get()]))
        far = total(far_b, swap(last_far, "head", 1))
        w = Window(part[0])
        w.step(sum_a)
        far, part[0] = w.open(far, part[0])
        (near,), part = ffn([(1, 1)], part, None)
        near, *part = w.close(near, *part)
        w = Window(part[0])
        far = w.swap(far, "head", 2)
        near = w.swap(near, "head", 1)
        w.step(sum_a)
        (part[0],) = w.open(part[0])
        (own,), results = ffn([(0, 1)], part, extra)
        own, *results = w.close(own, *results)
        far, near = far.get(), near.get()
    else:
        grads, part = [None] * 4, None
        for k in (3, 2, 1):
            (grads[k],), part = ffn([(k, None)], part, None)
        (grads[0],), results = ffn([(0, None)], part, extra)
    layer_output, grad_middle, branch, gn, t, leading, pr, kr, sums2 = results

    def back(pick, q, k, v, state):
        count = len(pick)
        steps, high = nb // many, many * STRETCH
        at, inner, width = pick[0] // count, (pick[0] % 2) // count, count * QW
        return call(
            functools.partial(back_kernel, many, steps, count),
            "attend_back",
            (cont,),
            steps,
            [(a, back_spec(high, width, steps, inner)) for a in (q, k, v)]
            + [(a, back_spec(high, width, steps, at)) for a in (gn, t)]
            + [
                (st, back_spec(many * DH, width, steps, at)),
                (kt, back_spec(many * 8, width, steps, at)),
                (pr, back_spec(many * DH, width, steps, at)),
                (kr, back_spec(many * 8, width, steps, at)),
                (state, whole_spec((state_rows, width), at)),
                (normed, back_spec(high, D, steps)),
                (att, back_spec(high, width, steps, at)),
                (branch, back_spec(high, D, steps)),
            ],
            [(like((R, PW), bf16), back_spec(high, PW, steps))] * count
            + [(like((PW + QW, D), bf16), whole_spec((PW + QW, D)))] * count
            + [(like((8, count * PW), f32), sum_spec((8, count * PW)))],
            [pltpu.VMEM((DH, width), f32), pltpu.VMEM((8, width), f32)]
            + [pltpu.VMEM((PW + QW, D), f32)] * count,
            6 * count * R * D * D,
            5 * count * R * D,
        )

    def inputs(start, count, out, x_in):
        at = rows_spec(rows, D, 0, start)
        ins = [(x_in, at), (grad_middle, at), vector(gain1)]
        ins += [(g, rows_spec(rows, PW, 0, start)) for g in gp]
        ins += [(w, whole_spec((D, PW))) for w in wa]
        if out is not None:
            ins += [(out, pl.BlockSpec(memory_space=pl.ANY))]
        return call(
            input_kernel,
            "input_grad",
            (),
            count,
            ins,
            [(wide[0], at), (like((16, D), f32), sum_spec((16, D)))],
            [],
            6 * rows * count * D * D,
            16 * rows * count * D,
            None if out is None else {len(ins) - 1: 0},
        )

    gp = [None] * 4
    if fast:
        g_in = swap_state(leading, after)
        sum_b = Stages(sum_stages([own, near, far]))
        w = Window(g_in)
        w.step(sum_b)
        w.step(sum_a)
        (g_in,) = w.open(g_in)
        gp[2], gp[3], da2, da3, ba23 = back((2, 3), q23, k23, v23, g_in)
        gp[2], gp[3], da2, da3, ba23, g_in = w.close(gp[2], gp[3], da2, da3, ba23, g_in)

        far = total(da2, swap(da3, "head", 1))
        w = Window(g_in)
        far = w.swap(far, "head", 2)
        w.step(sum_b)
        w.step(sum_a)
        (g_in,) = w.open(g_in)
        gp[0], gp[1], da0, da1, ba01 = back((0, 1), q01, k01, v01, g_in)
        gp[0], gp[1], da0, da1, ba01 = w.close(gp[0], gp[1], da0, da1, ba01)
        near = swap(da1, "head", 1)
        sum_c = Stages(sum_stages([da0, near, far.get()], True))
        w = Window(gp[0])
        w.step(sum_c)
        w.step(sum_b)
        half = tiles // 2
        (layer_in,) = w.open(layer_input)
        input_grad, sums1 = inputs(0, half, None, layer_in)
        input_grad, sums1 = w.close(input_grad, sums1)
        w = Window(input_grad)
        w.step(sum_c)
        w.step(sum_b)
        (input_grad,) = w.open(input_grad)
        input_grad, more = inputs(half, tiles - half, input_grad, layer_in)
        input_grad, more = w.close(input_grad, more)
        sums1 = sums1 + more
        where = lax.axis_index("dp")
        where = jnp.stack([where % 2, where // 2]).astype(jnp.int32)
        depth = lax.axis_size("dp") // 2
        piece = FQ // 2 // depth

        def source(unit):
            def index(i, where):
                at = jnp.where(i // depth == unit, i % depth, 0 if unit else depth - 1)
                return (at ^ where[1], 0)

            return pl.BlockSpec((piece, D), index)

        ins = [(v, source(0)) for v in sum_a.finish()] + [(v, source(1)) for v in sum_b.finish()]

        def placed(half, shape, block, index):
            w = Window(input_grad)
            w.step(sum_c)
            (at,) = w.open(where)
            out = call(
                functools.partial(place_kernel, depth, half),
                "place",
                (at,),
                2 * depth,
                ins,
                [(like(shape, f32), pl.BlockSpec(block, index))],
                [],
                0,
                6 * FQ * D,
            )
            return w.close(*out)[0]

        expand_weight_grad = placed(0, (D, FQ), (D, piece), lambda i, *_: (0, i))
        sums1 = tie(sums1, expand_weight_grad)[0]
        eb = [list(tie(*parts, sums1)[: len(parts)]) for parts in eb]
        reduce_weight_grad = placed(1, (FQ, D), (piece, D), lambda i, *_: (i, 0))
        sum_c = whole_sum(sum_c)
        attend_weight_grad, output_weight_grad = sum_c[:PW].T, sum_c[PW:]
    else:
        g_in = swap_state(leading, after)
        gp[2], gp[3], *da23, ba23 = back((2, 3), q23, k23, v23, g_in)
        gp[0], gp[1], *da01, ba01 = back((0, 1), q01, k01, v01, g_in)
        da = da01 + da23

        def reduce(parts):
            return whole_sum(Stages(sum_stages([scatter_head(regroup(parts, n, 0))])))

        expand_weight_grad = reduce([g[:FQ] for g in grads]).T
        reduce_weight_grad = reduce([g[FQ:] for g in grads])
        attend_weight_grad = reduce([g[:PW] for g in da]).T
        output_weight_grad = reduce([g[PW:] for g in da])
        input_grad, sums1 = inputs(0, tiles, None, layer_input)

    eb = [jnp.sum(jnp.concatenate(parts, axis=1), axis=0) for parts in eb]
    eb = regroup(eb, n, 0)
    ab = regroup([jnp.sum(jnp.concatenate([ba01, ba23], axis=1), axis=0)], n, 0)
    shared = jnp.concatenate(
        [
            jnp.sum(sums1.reshape(2, 8, D), axis=1),
            jnp.sum(sums2.reshape(4, 8, D), axis=1),
        ]
    )
    split = [jnp.concatenate(both) for both in zip(eb, ab)]
    shared, split = Stages(small_stages(shared, split)).finish()
    shared1, shared2 = shared[:2], shared[2:]
    expand_bias_grad, attend_bias_grad = split[: eb[0].shape[0]], split[eb[0].shape[0] :]
    return (
        layer_output,
        input_grad,
        shared1[0],
        shared1[1],
        attend_weight_grad,
        attend_bias_grad,
        output_weight_grad,
        shared2[0],
        shared2[1],
        shared2[2],
        expand_weight_grad,
        expand_bias_grad,
        reduce_weight_grad,
        shared2[3],
    )


def solution(mesh):
    in_specs = (
        P(("dp", "head"), None),
        P(("dp", "head"), None),
        P("dp", None),
        P("dp", None),
        P(),
        P(),
        P(None, "head"),
        P("head"),
        P("head", None),
        P(),
        P(),
        P(),
        P(None, "head"),
        P("head"),
        P("head", None),
        P(),
    )
    out_specs = (
        P(("dp", "head"), None),
        P(("dp", "head"), None),
        P(),
        P(),
        P(None, "head"),
        P("head"),
        P("head", None),
        P(),
        P(),
        P(),
        P(None, "head"),
        P("head"),
        P("head", None),
        P(),
    )
    return jax.shard_map(
        on_device, mesh=mesh, in_specs=in_specs, out_specs=out_specs, check_vma=False
    )
```

```python
import functools

import jax
import jax.numpy as jnp
from jax import lax
from jax.experimental import pallas as pl
from jax.experimental.pallas import tpu as pltpu
from jax.sharding import PartitionSpec as P

DH = 64
STRETCH = 128
D = 1024
QUADS = 4
QW = D // QUADS
PW = 3 * QW
EPS = 1e-05
VMEM = 60 * 1024 * 1024

f32 = jnp.float32
bf16 = jnp.bfloat16


def nn(a, b):
    return lax.dot_general(a, b, (((1,), (0,)), ((), ())), preferred_element_type=f32)


def nt(a, b):
    return lax.dot_general(a, b, (((1,), (1,)), ((), ())), preferred_element_type=f32)


def tn(a, b):
    return lax.dot_general(a, b, (((0,), (0,)), ((), ())), preferred_element_type=f32)


PAIR = 2 * DH


def side_rows(kind):
    lane = lax.broadcasted_iota(jnp.int32, (1, PAIR), 1) // DH
    return [(lane == h).astype(kind) for h in range(2)]


def spread(block, picks):
    return jnp.concatenate([block * picks[0], block * picks[1]], axis=0)


def pair_product(left, right, picks):
    square = tn(left, right)
    return square[0:DH] * picks[0] + square[DH:PAIR] * picks[1]


def cut(start, width=PAIR):
    return slice(start * width, (start + 1) * width)


def centre(values):
    average = jnp.mean(values, axis=-1, keepdims=True)
    centred = values - average
    spread = jnp.mean(centred * centred, axis=-1, keepdims=True)
    inverse = lax.rsqrt(spread + EPS)
    return centred * inverse, inverse


def norm_back(xhat, inverse, grad, gain):
    w = grad * gain
    return inverse * (
        w
        - jnp.mean(w, axis=-1, keepdims=True)
        - xhat * jnp.mean(w * xhat, axis=-1, keepdims=True)
    )


def fold_rows(values):
    rows, columns = values.shape
    return jnp.sum(values.reshape(rows // 8, 8, columns), axis=0)


def normal_parts(v):
    size = jnp.abs(v) * 0.7071067811865476
    t = 1.0 / (1.0 + 0.3275911 * size)
    bell = jnp.exp(-0.5 * v * v)
    poly = t * (
        0.254829592
        + t * (-0.284496736 + t * (1.421413741 + t * (-1.453152027 + t * 1.061405429)))
    )
    tail = 0.5 * poly * bell
    return jnp.where(v < 0, tail, 1.0 - tail), bell


def qkv_kernel(blocks, fresh, thr, cont, *refs):
    if fresh:
        x, gain, shift, n_out = refs[0], refs[1], refs[2], refs[9]
        wa, ba = refs[3:5], refs[5]
        q_out, k_out, v_out = refs[6:9]
        t_out, st_out, kt_out, state, sums = refs[10:15]
    else:
        n_in = refs[0]
        wa, ba = refs[1:3], refs[3]
        q_out, k_out, v_out = refs[4:7]
        t_out, st_out, kt_out, state, sums = refs[7:12]
    step = pl.program_id(0)
    rows = blocks * STRETCH

    @pl.when(step == 0)
    def _():
        state[...] = jnp.zeros_like(state)
        sums[...] = jnp.zeros_like(sums)

    if fresh:
        xhat, _ = centre(x[...].astype(f32))
        normed = (xhat * gain[...] + shift[...]).astype(bf16)
        n_out[...] = normed
    else:
        normed = n_in[...]
    place = lax.broadcasted_iota(jnp.int32, (STRETCH, 128), 0)
    valid = jnp.concatenate(
        [(place >= thr[step * blocks + b]).astype(f32) for b in range(blocks)], axis=0
    )
    low = lax.broadcasted_iota(jnp.int32, (rows, 128), 1) < DH

    def feature(values):
        return jnp.where(values > 0, values + 1.0, jnp.exp(jnp.minimum(values, 0.0)))

    for g in range(2):
        project = nn(normed, wa[g][...]) + ba[:, g * PW : (g + 1) * PW]
        for pair in range(2):
            c0, c1, c2 = (
                project[:, pair * 384 + j * 128 : pair * 384 + (j + 1) * 128] for j in range(3)
            )
            at = slice(g * QW + pair * 128, g * QW + (pair + 1) * 128)
            q_out[:, at] = feature(jnp.where(low, c0, c1)).astype(bf16)
            key = pltpu.roll(jnp.where(low, c2, c0), DH, 1)
            k_out[:, at] = (valid * feature(key)).astype(bf16)
            v_out[:, at] = jnp.where(low, c1, c2).astype(bf16)
    picks = side_rows(f32)
    for b in range(blocks):
        keep = cont[step * blocks + b].astype(f32)
        here = cut(b, STRETCH)
        state[...] = state[...] * keep
        sums[...] = sums[...] * keep
        st_out[cut(b, DH), :] = state[...]
        kt_out[cut(b, 8), :] = sums[...]
        for p in range(4):
            key = k_out[here, cut(p)]
            state[:, cut(p)] += pair_product(key, v_out[here, cut(p)], picks)
            sums[:, cut(p)] += fold_rows(key.astype(f32))

    @pl.when(step == pl.num_programs(0) - 1)
    def _():
        t_out[0:DH, :] = state[...]
        t_out[DH : DH + 8, :] = sums[...]


def attend_kernel(blocks, first, thr, *refs):
    qkv = refs[0:5], refs[5:10]
    x, s_in, bo, gain, shift = refs[10:15]
    wo = refs[15:19]
    att_out, rec_out, st_out, kt_out, mid_out, n_out = refs[19:25]
    step = pl.program_id(0)
    picks = side_rows(bf16)
    row = lax.broadcasted_iota(jnp.int32, (STRETCH, 2 * STRETCH), 0)
    lane = lax.broadcasted_iota(jnp.int32, (STRETCH, 2 * STRETCH), 1) % STRETCH
    lower = lane <= row
    ones_scores = spread(jnp.ones((STRETCH, PAIR), bf16), picks)
    ones_state = spread(jnp.ones((DH, PAIR), bf16), picks)
    zeros = jnp.zeros((PAIR, PAIR), bf16)
    ones = jnp.concatenate([ones_scores, zeros, ones_state], axis=0)
    came = jnp.sum(s_in[DH : DH + 8], axis=0, keepdims=True)
    for b in range(blocks):
        joins = first[step * blocks + b].astype(f32)
        here = cut(b, STRETCH)
        for p in range(8):
            at, own = cut(p), cut(p % 4)
            q, k, v, st, kt = qkv[p // 4]
            qb, kb, vb = q[here, own], k[here, own], v[here, own]
            state = (st[cut(b, DH), own] + joins * s_in[0:DH, at]).astype(bf16)
            total = jnp.sum(kt[cut(b, 8), own], axis=0, keepdims=True) + joins * came[:, at]
            st_out[cut(b, DH), at] = state
            kt_out[cut(b, 8), at] = jnp.broadcast_to(total, (8, PAIR))
            scores = nt(qb, spread(kb, picks))
            scores = jnp.where(lower, scores, 0.0).astype(bf16)
            weighted = (qb.astype(f32) * total).astype(bf16)
            left = jnp.concatenate([scores, qb, weighted], axis=1)
            right = jnp.concatenate([spread(vb, picks), spread(state, picks), zeros], axis=0)
            both = nn(left, jnp.concatenate([right, ones], axis=1))
            rec = 1.0 / jnp.maximum(both[:, PAIR:], 1.0)
            rec_out[here, at] = rec
            att_out[here, at] = (both[:, :PAIR] * rec).astype(bf16)
    place = lax.broadcasted_iota(jnp.int32, (STRETCH, D), 0)
    for b in range(blocks):
        here = slice(b * STRETCH, (b + 1) * STRETCH)

        @pl.when(thr[step * blocks + b] > 0)
        def _(b=b, here=here):
            valid = (place >= thr[step * blocks + b]).astype(f32)
            rec_out[here, :] = rec_out[here, :] * valid
            att_out[here, :] = (att_out[here, :].astype(f32) * valid).astype(bf16)

    middle = x[...].astype(f32) + bo[...]
    for g in range(QUADS):
        middle = middle + nn(att_out[:, g * QW : (g + 1) * QW], wo[g][...])
    mid_out[...] = middle
    xhat, _ = centre(middle)
    n_out[...] = (xhat * gain[...] + shift[...]).astype(bf16)


def ffn_kernel(blocks, widths, fresh, final, *refs):
    refs = list(refs)

    def take(count):
        taken = refs[:count]
        del refs[:count]
        return taken

    count = len(widths)
    if final:
        (first,) = take(1)
    n2, cot = take(2)
    be = take(count)
    if not fresh:
        part_out, part_grad = take(2)
    we, wr = take(count), take(count)
    if final:
        mid, att, rec, q01, q23, gain, br = take(7)
        wo = take(4)
    grad_out, be_sum = take(count), take(count)
    if final:
        out, gm_out, gb_out, gn_out, t_out, l_out, pr_out, kr_out, sums = take(9)
    else:
        next_out, next_grad = take(2)
    grad_sum = take(count)
    step = pl.program_id(0)

    @pl.when(step == 0)
    def _():
        for total in grad_sum + be_sum:
            total[...] = jnp.zeros_like(total)
        if final:
            l_out[...] = jnp.zeros_like(l_out)
            sums[...] = jnp.zeros_like(sums)

    normed = n2[...]
    cotangent = cot[...]
    reduced = None if fresh else part_out[...]
    grad = None if fresh else part_grad[...]
    for i, width in enumerate(widths):
        hidden = nn(normed, we[i][...]) + be[i][...]
        grad_act = nt(cotangent, wr[i][...])
        phi, bell = normal_parts(hidden)
        active = (hidden * phi).astype(bf16)
        back = (grad_act * (phi + hidden * (0.3989422804014327 * bell))).astype(bf16)
        be_sum[i][...] += fold_rows(back.astype(f32))
        grad_sum[i][0:width, :] += tn(back, normed)
        grad_sum[i][width : 2 * width, :] += tn(active, cotangent)
        more = nn(active, wr[i][...])
        reduced = more if reduced is None else reduced + more
        more = nt(back, we[i][...])
        grad = more if grad is None else grad + more

    @pl.when(step == pl.num_programs(0) - 1)
    def _():
        for out_ref, total in zip(grad_out, grad_sum):
            out_ref[...] = total[...].astype(bf16)

    if not final:
        next_out[...] = reduced
        next_grad[...] = grad
        return
    middle = mid[...]
    out[...] = (middle + reduced + br[...]).astype(bf16)
    xhat, inverse = centre(middle)
    cot_wide = cotangent.astype(f32)
    grad_middle = cot_wide + norm_back(xhat, inverse, grad, gain[...])
    gm_out[...] = grad_middle
    branch = grad_middle.astype(bf16)
    gb_out[...] = branch
    sums[0:8, :] += fold_rows(branch.astype(f32))
    sums[8:16, :] += fold_rows(grad * xhat)
    sums[16:24, :] += fold_rows(grad)
    sums[24:32, :] += fold_rows(cot_wide)
    for g in range(QUADS):
        at = slice(g * QW, (g + 1) * QW)
        grad_att = nt(branch, wo[g][...]).astype(bf16).astype(f32)
        share = rec[:, at]
        numer = grad_att * share
        gn_out[:, at] = numer.astype(bf16)
        t_out[:, at] = jnp.where(
            share < 1.0, -(numer * att[:, at].astype(f32)), 0.0
        ).astype(bf16)
    picks = side_rows(f32)
    ones = spread(jnp.ones((DH, PAIR), bf16), side_rows(bf16))
    for b in range(blocks):
        here = cut(b, STRETCH)
        for p in range(8):
            at = cut(p)
            query = (q01, q23)[p // 4][here, cut(p % 4)]
            pr_out[cut(b, DH), at] = pair_product(query, gn_out[here, at], picks)
            grad_denom = nn(t_out[here, at], ones)
            kr_out[cut(b, 8), at] = fold_rows(grad_denom * query.astype(f32))

        @pl.when(first[step * blocks + b] == 1)
        def _(b=b):
            l_out[0:DH, :] += pr_out[cut(b, DH), :]
            l_out[DH : DH + 8, :] += kr_out[cut(b, 8), :]


def back_kernel(blocks, tiles, quads, cont, q, k, v, gn, t, st, kt, pr, kr, g_in, normed, att, branch, *refs):
    gp_out, da_out, ba_sum = refs[0:quads], refs[quads : 2 * quads], refs[2 * quads]
    state, total = refs[2 * quads + 1 : 2 * quads + 3]
    da_sum = refs[2 * quads + 3 :]
    step = pl.program_id(0)
    tile = tiles - 1 - step

    @pl.when(step == 0)
    def _():
        state[...] = g_in[0:DH]
        total[...] = jnp.broadcast_to(
            jnp.sum(g_in[DH : DH + 8], axis=0, keepdims=True), total.shape
        )
        ba_sum[...] = jnp.zeros_like(ba_sum)
        for da in da_sum:
            da[...] = jnp.zeros_like(da)

    picks = side_rows(bf16)
    row = lax.broadcasted_iota(jnp.int32, (STRETCH, 2 * STRETCH), 0)
    lane = lax.broadcasted_iota(jnp.int32, (STRETCH, 2 * STRETCH), 1) % STRETCH
    lower = lane <= row
    upper = lane >= row
    low_lane = lax.broadcasted_iota(jnp.int32, (STRETCH, PAIR), 1) < DH
    all_ones = jnp.ones((STRETCH, PAIR), bf16)
    ones_scores = spread(all_ones, picks)
    ones_state = spread(jnp.ones((DH, PAIR), bf16), picks)
    for b in reversed(range(blocks)):
        keep = cont[tile * blocks + b + 1].astype(f32)
        here = cut(b, STRETCH)
        for p in range(2 * quads):
            at = cut(p)
            qb, kb, vb, gb, tb = q[here, at], k[here, at], v[here, at], gn[here, at], t[here, at]
            state_here = state[:, at] * keep
            total_here = total[:, at] * keep
            behind = spread(state_here.astype(bf16), picks)
            state[:, at] = state_here + pr[cut(b, DH), at]
            total[:, at] = total_here + jnp.sum(kr[cut(b, 8), at], axis=0, keepdims=True)
            spread_q, spread_g = spread(qb, picks), spread(gb, picks)
            forward = spread(st[cut(b, DH), at], picks)
            scores = nt(
                jnp.concatenate([gb, tb], axis=1),
                jnp.concatenate([spread(vb, picks), ones_scores], axis=1),
            )
            scores = jnp.where(lower, scores, 0.0).astype(bf16)
            turned = nt(
                jnp.concatenate([vb, all_ones], axis=1),
                jnp.concatenate([spread_g, spread(tb, picks)], axis=1),
            )
            turned = jnp.where(upper, turned, 0.0).astype(bf16)
            mixed = jnp.where(upper, nt(kb, spread_q), 0.0).astype(bf16)
            grad_denom = nn(tb, ones_state)
            grad_q = (
                nn(scores, spread(kb, picks))
                + nt(gb, forward)
                + grad_denom * kt[b * 8 : b * 8 + 1, at]
            )
            grad_k = nn(turned, spread_q) + nt(vb, behind) + total_here[0:1]
            grad_v = nn(jnp.concatenate([mixed, kb], axis=1), jnp.concatenate([spread_g, behind]))
            grad_q = grad_q * jnp.minimum(qb.astype(f32), 1.0)
            grad_k = grad_k * jnp.minimum(kb.astype(f32), 1.0)
            swapped = pltpu.roll(grad_k, DH, 1)
            for j, piece in enumerate(
                (
                    jnp.where(low_lane, grad_q, swapped),
                    jnp.where(low_lane, grad_v, grad_q),
                    jnp.where(low_lane, swapped, grad_v),
                )
            ):
                piece = piece.astype(bf16)
                start = (p % 2) * 384 + j * 128
                gp_out[p // 2][here, start : start + 128] = piece
                start += (p // 2) * PW
                ba_sum[:, start : start + 128] += fold_rows(piece.astype(f32))
    for g in range(quads):
        da_sum[g][0:PW, :] += tn(gp_out[g][...], normed[...])
        da_sum[g][PW:, :] += tn(att[:, cut(g, QW)], branch[...])

    @pl.when(step == tiles - 1)
    def _():
        for out, da in zip(da_out, da_sum):
            out[...] = da[...].astype(bf16)


def input_kernel(x, gm, gain, *refs):
    gp, wa = refs[0:4], refs[4:8]
    out, sums = refs[-2:]

    @pl.when(pl.program_id(0) == 0)
    def _():
        sums[...] = jnp.zeros_like(sums)

    grad = nt(gp[0][...], wa[0][...])
    for g in range(1, QUADS):
        grad = grad + nt(gp[g][...], wa[g][...])
    xhat, inverse = centre(x[...].astype(f32))
    out[...] = gm[...] + norm_back(xhat, inverse, grad, gain[...])
    sums[0:8, :] += fold_rows(grad * xhat)
    sums[8:16, :] += fold_rows(grad)


def rows_spec(rows, columns, at=0, start=0):
    return pl.BlockSpec((rows, columns), lambda i, *_: (i + start, at))


def back_spec(rows, columns, tiles, at=0):
    return pl.BlockSpec((rows, columns), lambda i, *_: (tiles - 1 - i, at))


def whole_spec(shape, at=0):
    last = len(shape) - 1
    return pl.BlockSpec(
        shape, lambda i, *_: (0,) * last + (at,), pipeline_mode=pl.Buffered(1)
    )


def part_spec(shape, at):
    return pl.BlockSpec(shape, lambda i, *_: (at, 0), pipeline_mode=pl.Buffered(1))


def sum_spec(shape):
    return pl.BlockSpec(shape, lambda i, *_: (0,) * len(shape))


def call(kernel, name, scalars, tiles, ins, outs, scratch, flops, moved, aliases=None):
    return pl.pallas_call(
        kernel,
        grid_spec=pltpu.PrefetchScalarGridSpec(
            num_scalar_prefetch=len(scalars),
            grid=(tiles,),
            in_specs=[spec for _, spec in ins],
            out_specs=[spec for _, spec in outs],
            scratch_shapes=list(scratch),
        ),
        out_shape=[shape for shape, _ in outs],
        compiler_params=pltpu.CompilerParams(vmem_limit_bytes=VMEM),
        cost_estimate=pl.CostEstimate(flops=flops, bytes_accessed=moved, transcendentals=0),
        input_output_aliases=aliases or {},
        name=name,
    )(*scalars, *[array for array, _ in ins])


def tie(*values):
    return lax.optimization_barrier(list(values))


def swap(value, axis, bit):
    size = lax.axis_size(axis)
    return lax.ppermute(value, axis, [(i, i ^ bit) for i in range(size)])


def bits_of(size):
    bit, bits = 1, []
    while bit < size:
        bits.append(bit)
        bit *= 2
    return bits


def gather_shards(own):
    size = lax.axis_size("head")
    held = {0: own}
    for bit in reversed(bits_of(size)):
        for k in list(held):
            held[k ^ bit] = swap(held[k], "head", bit)
    return [held[k] for k in range(size)]


def half_of(value, which, axis):
    size = value.shape[axis] // 2
    return lax.dynamic_slice_in_dim(value, which * size, size, axis)


def regroup(parts, count, axis):
    if len(parts) == count:
        return list(parts)
    whole = jnp.concatenate(parts, axis=axis)
    width = whole.shape[axis] // count
    return [
        lax.slice_in_dim(whole, k * width, (k + 1) * width, axis=axis) for k in range(count)
    ]


def swap_state(mine, weights):
    size = lax.axis_size("head")
    sent = mine.astype(bf16)
    total = None
    for j in range(1, size):
        got = swap(sent, "head", j)
        slots = jnp.split(got, size, axis=1)
        got = jnp.concatenate([slots[k ^ j] for k in range(size)], axis=1).astype(f32)
        got = got * weights[j]
        total = got if total is None else total + got
    return total


def scatter_head(parts):
    held = dict(enumerate(parts))
    for bit in bits_of(len(parts)):
        for k in [k for k in held if k & bit]:
            got = swap(held.pop(k).astype(bf16), "head", bit)
            held[k ^ bit] = held[k ^ bit].astype(f32) + got.astype(f32)
    return held[0]


class Stages:
    def __init__(self, generator):
        self.generator, self.got = generator, None

    def advance(self):
        sent, self.got = self.generator.send(self.got)
        return sent

    def finish(self):
        while self.advance():
            pass
        return self.got


def sum_stages(terms, apart=False):
    size = lax.axis_size("dp")
    me = lax.axis_index("dp")
    x, z, depth = me % 2, me // 2, size // 2

    def half(which):
        total = None
        for term in terms:
            part = half_of(term, which, 0).astype(f32)
            total = part if total is None else total + part
        return total.astype(bf16)

    sent, kept = tie(half(1 - x), half(x))
    (got,) = yield [sent, kept], [swap(sent, "dp", 1)]
    mine = (kept.astype(f32) + got.astype(f32)).astype(bf16)
    rows = mine.shape[0] // depth
    own = lax.dynamic_slice_in_dim(mine, z * rows, rows, 0)
    sent = [
        lax.dynamic_slice_in_dim(mine, (z ^ j) * rows, rows, 0) for j in range(1, depth)
    ]
    own, *sent = tie(own, *sent)
    got = yield [own] + sent, [swap(part, "dp", 2 * j) for j, part in enumerate(sent, 1)]
    total = own.astype(f32)
    for part in got:
        total = total + part.astype(f32)
    (own,) = tie(total.astype(bf16))
    got = yield [own], [swap(own, "dp", 2 * j) for j in range(1, depth)]
    if apart:
        parts = [own] + list(got)
        got = yield parts, [swap(part, "dp", 1) for part in parts]
        mine, other = jnp.concatenate(parts, axis=0), jnp.concatenate(list(got), axis=0)
    else:
        (mine,) = tie(jnp.concatenate([own] + list(got), axis=0))
        (other,) = yield [mine], [swap(mine, "dp", 1)]

    yield [], [mine, other]


def whole_sum(stages):
    mine, other = stages.finish()
    me = lax.axis_index("dp")
    x, z, depth = me % 2, me // 2, lax.axis_size("dp") // 2
    rows = mine.shape[0] // depth

    def natural(value):
        for bit in bits_of(depth):
            shaped = value.reshape(depth // (2 * bit), 2, bit * rows, value.shape[1])
            turned = jnp.flip(shaped, axis=1)
            value = jnp.where((z & bit) != 0, turned, shaped).reshape(value.shape)
        return value

    mine, other = natural(mine), natural(other)
    pair = [jnp.where(x == 0, mine, other), jnp.where(x == 0, other, mine)]
    return jnp.concatenate(pair, axis=0).astype(f32)


def place_kernel(depth, half, where, *refs):
    sources, out = refs[0:4], refs[4]
    step = pl.program_id(0)
    for unit in range(2):
        for side in range(2):

            @pl.when(jnp.logical_and(step // depth == unit, where[0] == side))
            def _(unit=unit, side=side):
                part = sources[2 * unit + (side ^ half)][...].astype(f32)
                out[...] = part if half else part.T


class Window:
    def __init__(self, *after):
        self.after, self.sent, self.got, self.chains = after, [], [], []

    def swap(self, value, axis, bit):
        value = tie(value, *self.after)[0]
        self.sent.append(value)
        self.got.append(swap(value, axis, bit))
        return Later(self, len(self.got) - 1)

    def step(self, chain):
        self.sent += chain.advance()
        self.chains.append((chain, len(self.got)))
        self.got += chain.got

    def open(self, *values):
        return tie(*values, *self.sent)[: len(values)]

    def close(self, *values):
        tied = tie(*values, *self.got)
        self.got = tied[len(values) :]
        for chain, start in self.chains:
            chain.got = self.got[start : start + len(chain.got)]
        return tied[: len(values)]


class Later:
    def __init__(self, window, place):
        self.window, self.place = window, place

    def get(self):
        return self.window.got[self.place]


def small_stages(shared, split):
    size = len(split)
    held = dict(enumerate(split))
    flat = shared.reshape(-1)
    for bit in bits_of(size):
        gone = [k for k in held if k & bit]
        (sent,) = tie(jnp.concatenate([flat] + [held[k] for k in gone]))
        (got,) = yield [sent], [swap(sent, "head", bit)]
        at = flat.shape[0]
        flat = flat + got[:at]
        for k in gone:
            width = held[k].shape[0]
            held[k ^ bit] = held[k ^ bit] + got[at : at + width]
            del held[k]
            at += width
    both = jnp.concatenate([flat, held[0]])
    for bit in bits_of(lax.axis_size("dp")):
        (both,) = tie(both)
        (got,) = yield [both], [swap(both, "dp", bit)]
        both = both + got
    yield [], [both[: flat.shape[0]].reshape(shared.shape), both[flat.shape[0] :]]


def on_device(
    layer_input,
    cotangent,
    crop_blocks,
    crop_padding,
    first_gain,
    first_shift,
    attend_weight,
    attend_bias,
    output_weight,
    output_bias,
    second_gain,
    second_shift,
    expand_weight,
    expand_bias,
    reduce_weight,
    reduce_bias,
):
    R = layer_input.shape[0]
    n = lax.axis_size("head")
    me = lax.axis_index("head")
    x = lax.axis_index("dp") % 2
    nb = R // STRETCH
    FF = expand_weight.shape[1] * n
    FQ = FF // QUADS
    fast = n == QUADS

    if fast:
        near = swap(attend_weight, "head", 1)
        ba_near = jnp.concatenate([attend_bias, swap(attend_bias, "head", 1)])
        be_near = jnp.concatenate([expand_bias, swap(expand_bias, "head", 1)])
        wa = [attend_weight, near, None, None]
        w = Window()
        wa_far = w.swap(attend_weight, "head", 2)
        bias_far = w.swap(jnp.concatenate([ba_near, be_near]), "head", 2)
        wo_near = w.swap(output_weight, "head", 1)
        we_near = w.swap(expand_weight, "head", 1)
        wr_near = w.swap(reduce_weight, "head", 1)
    else:
        wa = regroup(gather_shards(attend_weight), QUADS, 1)
        ba_near, ba_far = jnp.split(jnp.concatenate(gather_shards(attend_bias)), 2)

    sizes, pads = crop_blocks[0], crop_padding[0]
    crops = sizes.shape[0]
    closing = jnp.sum(jnp.tril(jnp.ones((crops, crops), jnp.int32)) * sizes[None, :], axis=1)

    def crop_of(position):
        return jnp.sum((position[..., None] >= closing).astype(jnp.int32), axis=-1)

    spots = me * nb + jnp.arange(nb, dtype=jnp.int32)
    crop = crop_of(spots)
    belongs = crop[:, None] == jnp.arange(crops, dtype=jnp.int32)[None, :]
    opening = jnp.sum(jnp.where(belongs, (closing - sizes)[None, :], 0), axis=1)
    padding = jnp.sum(jnp.where(belongs, pads[None, :], 0), axis=1)
    thr = jnp.maximum(padding - (spots - opening) * STRETCH, 0).astype(jnp.int32)
    first = (crop == crop[0]).astype(jnp.int32)
    one = jnp.ones((1,), jnp.int32)
    cont = jnp.concatenate([one, (crop[1:] == crop[:-1]).astype(jnp.int32), one])
    others = me ^ jnp.arange(n, dtype=jnp.int32)
    opens = crop_of(others * nb)
    closes = crop_of(others * nb + nb - 1)
    before = jnp.logical_and(others < me, closes == crop[0]).astype(f32)
    after = jnp.logical_and(others > me, opens == crop[nb - 1]).astype(f32)

    blocks = 2 if nb % 2 == 0 else 1
    rows = blocks * STRETCH
    tiles = R // rows
    many = 4 if nb % 4 == 0 else blocks
    gain1, shift1 = first_gain[None, :], first_shift[None, :]
    gain2, shift2 = second_gain[None, :], second_shift[None, :]
    like = jax.ShapeDtypeStruct
    HALF = D // 2
    full, side = rows_spec(rows, D), rows_spec(rows, HALF)
    low, wide = (like((R, D), bf16), full), (like((R, D), f32), full)
    narrow = (like((R, HALF), bf16), side)
    vec = whole_spec((1, D))
    state_rows = DH + 8

    def vector(value):
        return (value, vec)

    def project(source, pick, bias, fresh):
        tall, thin = rows_spec(many * STRETCH, D), rows_spec(many * STRETCH, HALF)
        ins = [(source, tall)]
        if fresh:
            ins += [vector(gain1), vector(shift1)]
        ins += [(wa[k], whole_spec((D, PW))) for k in pick]
        ins += [(bias, whole_spec((1, 2 * PW)))]
        outs = [(narrow[0], thin)] * 3 + ([(low[0], tall)] if fresh else [])
        outs += [
            (like((state_rows, HALF), f32), sum_spec((state_rows, HALF))),
            (like((nb * DH, HALF), f32), rows_spec(many * DH, HALF)),
            (like((nb * 8, HALF), f32), rows_spec(many * 8, HALF)),
        ]
        return call(
            functools.partial(qkv_kernel, many, fresh),
            "qkv",
            (thr, cont),
            nb // many,
            ins,
            outs,
            [pltpu.VMEM((DH, HALF), f32), pltpu.VMEM((8, HALF), f32)],
            3 * R * D * D,
            8 * R * D + 3 * D * D,
        )

    bias = ba_near[None, :]
    source = layer_input
    if fast:
        source, bias = w.open(source, bias)
    q01, k01, v01, normed, trail01, st01, kt01 = project(source, (0, 1), bias, True)
    if fast:
        q01, k01, v01, normed, trail01 = w.close(q01, k01, v01, normed, trail01)
        wa[2] = wa_far.get()
        wa[3] = swap(wa[2], "head", 1)
        ba_far, be_far = bias_far.get()[: ba_near.shape[0]], bias_far.get()[ba_near.shape[0] :]
        be_slots = jnp.split(jnp.concatenate([be_near, be_far]), QUADS)
        wo = [output_weight, wo_near.get(), None, None]
        w = Window(trail01)
        wo_far = w.swap(output_weight, "head", 2)
        normed, wa[3] = w.open(normed, wa[3])
    else:
        wo = regroup(gather_shards(output_weight), QUADS, 0)
        we = regroup(gather_shards(expand_weight), QUADS, 1)
        wr = regroup(gather_shards(reduce_weight), QUADS, 0)
        be_slots = jnp.split(jnp.concatenate(gather_shards(expand_bias)), QUADS)
    q23, k23, v23, trail23, st23, kt23 = project(normed, (2, 3), ba_far[None, :], False)
    if fast:
        q23, k23, v23, trail23 = w.close(q23, k23, v23, trail23)
        wo[2] = wo_far.get()
        wo[3] = swap(wo[2], "head", 1)
    s_in = swap_state(jnp.concatenate([trail01, trail23], axis=1), before)
    if fast:
        w = Window(s_in)
        we_cut, wr_cut = jnp.split(expand_weight, 2, axis=1), jnp.split(reduce_weight, 2)
        wr_far = w.swap(wr_cut[0], "head", 2)
        (s_in,) = w.open(s_in)

    tall, thin = rows_spec(many * STRETCH, D), rows_spec(many * STRETCH, HALF)
    att, rec, st, kt, middle, n2 = call(
        functools.partial(attend_kernel, many),
        "attend",
        (first, thr),
        nb // many,
        [
            (a, spec)
            for part in ((q01, k01, v01, st01, kt01), (q23, k23, v23, st23, kt23))
            for a, spec in zip(
                part,
                [thin] * 3 + [rows_spec(many * DH, HALF), rows_spec(many * 8, HALF)],
            )
        ]
        + [
            (layer_input, tall),
            (s_in, whole_spec((state_rows, D))),
            vector(output_bias[None, :]),
            vector(gain2),
            vector(shift2),
        ]
        + [(w, whole_spec((QW, D))) for w in wo],
        [
            (low[0], tall),
            (wide[0], tall),
            (like((nb * DH, D), bf16), rows_spec(many * DH, D)),
            (like((nb * 8, D), f32), rows_spec(many * 8, D)),
            (wide[0], tall),
            (low[0], tall),
        ],
        [],
        12 * R * D * D,
        20 * R * D,
    )

    if fast:
        att, rec, st, kt, middle, n2 = w.close(att, rec, st, kt, middle, n2)
        we = [expand_weight, we_near.get(), [None, None], [None, None]]
        wr = [reduce_weight, wr_near.get(), [wr_far.get(), None], [None, None]]

    def ffn(picks, part, extra):
        widths = [FQ if half is None else FQ // 2 for _, half in picks]
        spots = [(k, width, half or 0) for (k, half), width in zip(picks, widths)]
        high = many * STRETCH
        row = rows_spec(high, D)
        ins = [(n2, row), (cotangent, row)]
        ins += [(be_slots[k][None, :], whole_spec((1, width), at)) for k, width, at in spots]
        if part is not None:
            ins += [(part[0], row), (part[1], row)]
        for group, spec, dims in ((we, whole_spec, (D, None)), (wr, part_spec, (None, D))):
            for k, width, at in spots:
                shape = tuple(d or width for d in dims)
                halves = isinstance(group[k], list)
                weight = group[k][at] if halves else group[k]
                ins.append((weight, spec(shape, 0 if halves else at)))
        outs = [(like((2 * w, D), bf16), whole_spec((2 * w, D))) for w in widths]
        outs += [(like((8, w), f32), sum_spec((8, w))) for w in widths]
        if extra is None:
            outs += [(wide[0], row)] * 2
        else:
            ins += extra
            outs += [(kind[0], row) for kind in (low, wide, low, low, low)]
            outs += [
                (like((state_rows, D), f32), sum_spec((state_rows, D))),
                (like((nb * DH, D), f32), rows_spec(many * DH, D)),
                (like((nb * 8, D), f32), rows_spec(many * 8, D)),
                (like((32, D), f32), sum_spec((32, D))),
            ]
        results = call(
            functools.partial(ffn_kernel, many, widths, part is None, extra is not None),
            "ffn",
            (first,) if extra is not None else (),
            R // high,
            ins,
            outs,
            [pltpu.VMEM((2 * w, D), f32) for w in widths],
            12 * R * D * sum(widths),
            20 * R * D,
        )
        for i, (k, half) in enumerate(picks):
            eb[k].append(results[len(picks) + i])
        return list(results[: len(picks)]), list(results[2 * len(picks) :])

    eb = [[], [], [], []]
    extra = [
        (middle, tall),
        (att, tall),
        (rec, tall),
        (q01, thin),
        (q23, thin),
        vector(gain2),
        vector(reduce_bias[None, :]),
    ] + [(w, whole_spec((QW, D))) for w in wo]
    def total(*terms):
        return sum(term.astype(f32) for term in terms).astype(bf16)

    if fast:
        w = Window(n2)
        we_far = w.swap(we_cut[0], "head", 2)
        wr_far = w.swap(wr_cut[1], "head", 2)
        wr_last = w.swap(wr[2][0], "head", 1)
        (n2,) = w.open(n2)
        (near, own), part = ffn([(1, 0), (0, 0)], None, None)
        n2, near, own, *part = w.close(n2, near, own, *part)
        we[2][0], wr[2][1], wr[3][0] = we_far.get(), wr_far.get(), wr_last.get()
        we[3][0] = swap(we[2][0], "head", 1)
        w = Window(part[0])
        we_far = w.swap(we_cut[1], "head", 2)
        wr_last = w.swap(wr[2][1], "head", 1)
        near = w.swap(near, "head", 1)
        (part[0],) = w.open(part[0])
        (last_far, far), part = ffn([(3, 0), (2, 0)], part, None)
        last_far, far, *part = w.close(last_far, far, *part)
        we[2][1], wr[3][1] = we_far.get(), wr_last.get()
        we[3][1] = swap(we[2][1], "head", 1)
        far = total(far, swap(last_far, "head", 1))
        near_a = near.get()
        w = Window(part[0])
        far = w.swap(far, "head", 2)
        (part[0],) = w.open(part[0])
        (last_far, far_b), part = ffn([(3, 1), (2, 1)], part, None)
        last_far, far_b, *part = w.close(last_far, far_b, *part)
        sum_a = Stages(sum_stages([own, near_a, far.get()]))
        far = total(far_b, swap(last_far, "head", 1))
        w = Window(part[0])
        w.step(sum_a)
        far, part[0] = w.open(far, part[0])
        (near,), part = ffn([(1, 1)], part, None)
        near, *part = w.close(near, *part)
        w = Window(part[0])
        far = w.swap(far, "head", 2)
        near = w.swap(near, "head", 1)
        w.step(sum_a)
        (part[0],) = w.open(part[0])
        (own,), results = ffn([(0, 1)], part, extra)
        own, *results = w.close(own, *results)
        far, near = far.get(), near.get()
    else:
        grads, part = [None] * 4, None
        for k in (3, 2, 1):
            (grads[k],), part = ffn([(k, None)], part, None)
        (grads[0],), results = ffn([(0, None)], part, extra)
    layer_output, grad_middle, branch, gn, t, leading, pr, kr, sums2 = results

    def back(pick, q, k, v, state):
        count = len(pick)
        steps, high = nb // many, many * STRETCH
        at, inner, width = pick[0] // count, (pick[0] % 2) // count, count * QW
        return call(
            functools.partial(back_kernel, many, steps, count),
            "attend_back",
            (cont,),
            steps,
            [(a, back_spec(high, width, steps, inner)) for a in (q, k, v)]
            + [(a, back_spec(high, width, steps, at)) for a in (gn, t)]
            + [
                (st, back_spec(many * DH, width, steps, at)),
                (kt, back_spec(many * 8, width, steps, at)),
                (pr, back_spec(many * DH, width, steps, at)),
                (kr, back_spec(many * 8, width, steps, at)),
                (state, whole_spec((state_rows, width), at)),
                (normed, back_spec(high, D, steps)),
                (att, back_spec(high, width, steps, at)),
                (branch, back_spec(high, D, steps)),
            ],
            [(like((R, PW), bf16), back_spec(high, PW, steps))] * count
            + [(like((PW + QW, D), bf16), whole_spec((PW + QW, D)))] * count
            + [(like((8, count * PW), f32), sum_spec((8, count * PW)))],
            [pltpu.VMEM((DH, width), f32), pltpu.VMEM((8, width), f32)]
            + [pltpu.VMEM((PW + QW, D), f32)] * count,
            6 * count * R * D * D,
            5 * count * R * D,
        )

    def inputs(start, count, out, x_in):
        at = rows_spec(rows, D, 0, start)
        ins = [(x_in, at), (grad_middle, at), vector(gain1)]
        ins += [(g, rows_spec(rows, PW, 0, start)) for g in gp]
        ins += [(w, whole_spec((D, PW))) for w in wa]
        if out is not None:
            ins += [(out, pl.BlockSpec(memory_space=pl.ANY))]
        return call(
            input_kernel,
            "input_grad",
            (),
            count,
            ins,
            [(wide[0], at), (like((16, D), f32), sum_spec((16, D)))],
            [],
            6 * rows * count * D * D,
            16 * rows * count * D,
            None if out is None else {len(ins) - 1: 0},
        )

    gp = [None] * 4
    if fast:
        g_in = swap_state(leading, after)
        sum_b = Stages(sum_stages([own, near, far]))
        w = Window(g_in)
        w.step(sum_b)
        w.step(sum_a)
        (g_in,) = w.open(g_in)
        gp[2], gp[3], da2, da3, ba23 = back((2, 3), q23, k23, v23, g_in)
        gp[2], gp[3], da2, da3, ba23, g_in = w.close(gp[2], gp[3], da2, da3, ba23, g_in)

        far = total(da2, swap(da3, "head", 1))
        w = Window(g_in)
        far = w.swap(far, "head", 2)
        w.step(sum_b)
        w.step(sum_a)
        (g_in,) = w.open(g_in)
        gp[0], gp[1], da0, da1, ba01 = back((0, 1), q01, k01, v01, g_in)
        gp[0], gp[1], da0, da1, ba01 = w.close(gp[0], gp[1], da0, da1, ba01)
        near = swap(da1, "head", 1)
        sum_c = Stages(sum_stages([da0, near, far.get()], True))
        w = Window(gp[0])
        w.step(sum_c)
        w.step(sum_b)
        half = tiles // 2
        (layer_in,) = w.open(layer_input)
        input_grad, sums1 = inputs(0, half, None, layer_in)
        input_grad, sums1 = w.close(input_grad, sums1)
        w = Window(input_grad)
        w.step(sum_c)
        w.step(sum_b)
        (input_grad,) = w.open(input_grad)
        input_grad, more = inputs(half, tiles - half, input_grad, layer_in)
        input_grad, more = w.close(input_grad, more)
        sums1 = sums1 + more
        where = lax.axis_index("dp")
        where = jnp.stack([where % 2, where // 2]).astype(jnp.int32)
        depth = lax.axis_size("dp") // 2
        piece = FQ // 2 // depth

        def source(unit):
            def index(i, where):
                at = jnp.where(i // depth == unit, i % depth, 0 if unit else depth - 1)
                return (at ^ where[1], 0)

            return pl.BlockSpec((piece, D), index)

        ins = [(v, source(0)) for v in sum_a.finish()] + [(v, source(1)) for v in sum_b.finish()]

        def placed(half, shape, block, index):
            w = Window(input_grad)
            w.step(sum_c)
            (at,) = w.open(where)
            out = call(
                functools.partial(place_kernel, depth, half),
                "place",
                (at,),
                2 * depth,
                ins,
                [(like(shape, f32), pl.BlockSpec(block, index))],
                [],
                0,
                6 * FQ * D,
            )
            return w.close(*out)[0]

        expand_weight_grad = placed(0, (D, FQ), (D, piece), lambda i, *_: (0, i))
        sums1 = tie(sums1, expand_weight_grad)[0]
        eb = [list(tie(*parts, sums1)[: len(parts)]) for parts in eb]
        reduce_weight_grad = placed(1, (FQ, D), (piece, D), lambda i, *_: (i, 0))
        sum_c = whole_sum(sum_c)
        attend_weight_grad, output_weight_grad = sum_c[:PW].T, sum_c[PW:]
    else:
        g_in = swap_state(leading, after)
        gp[2], gp[3], *da23, ba23 = back((2, 3), q23, k23, v23, g_in)
        gp[0], gp[1], *da01, ba01 = back((0, 1), q01, k01, v01, g_in)
        da = da01 + da23

        def reduce(parts):
            return whole_sum(Stages(sum_stages([scatter_head(regroup(parts, n, 0))])))

        expand_weight_grad = reduce([g[:FQ] for g in grads]).T
        reduce_weight_grad = reduce([g[FQ:] for g in grads])
        attend_weight_grad = reduce([g[:PW] for g in da]).T
        output_weight_grad = reduce([g[PW:] for g in da])
        input_grad, sums1 = inputs(0, tiles, None, layer_input)

    eb = [jnp.sum(jnp.concatenate(parts, axis=1), axis=0) for parts in eb]
    eb = regroup(eb, n, 0)
    ab = regroup([jnp.sum(jnp.concatenate([ba01, ba23], axis=1), axis=0)], n, 0)
    shared = jnp.concatenate(
        [
            jnp.sum(sums1.reshape(2, 8, D), axis=1),
            jnp.sum(sums2.reshape(4, 8, D), axis=1),
        ]
    )
    split = [jnp.concatenate(both) for both in zip(eb, ab)]
    shared, split = Stages(small_stages(shared, split)).finish()
    shared1, shared2 = shared[:2], shared[2:]
    expand_bias_grad, attend_bias_grad = split[: eb[0].shape[0]], split[eb[0].shape[0] :]
    return (
        layer_output,
        input_grad,
        shared1[0],
        shared1[1],
        attend_weight_grad,
        attend_bias_grad,
        output_weight_grad,
        shared2[0],
        shared2[1],
        shared2[2],
        expand_weight_grad,
        expand_bias_grad,
        reduce_weight_grad,
        shared2[3],
    )


def solution(mesh):
    in_specs = (
        P(("dp", "head"), None),
        P(("dp", "head"), None),
        P("dp", None),
        P("dp", None),
        P(),
        P(),
        P(None, "head"),
        P("head"),
        P("head", None),
        P(),
        P(),
        P(),
        P(None, "head"),
        P("head"),
        P("head", None),
        P(),
    )
    out_specs = (
        P(("dp", "head"), None),
        P(("dp", "head"), None),
        P(),
        P(),
        P(None, "head"),
        P("head"),
        P("head", None),
        P(),
        P(),
        P(),
        P(None, "head"),
        P("head"),
        P("head", None),
        P(),
    )
    return jax.shard_map(
        on_device, mesh=mesh, in_specs=in_specs, out_specs=out_specs, check_vma=False
    )
```
